32 devices in a mesh: groups: 2 (over x), tm: 16 (over z, y, core).
Axes of the slice: x: 2, y: 2, z: 4, core: 2. Of those that a mesh axis runs over, the one named last changes fastest.
Arguments:
- space_time: bfloat16 [32, 512, 1024], P(('groups', 'tm')), parts along dimension 0, may hold values from -16 to 16
- w_lin: bfloat16 [1024, 3072], replicated, may hold values from -0.1875 to 0.1875
- gain_lin: bfloat16 [1024], replicated, may hold values from 0.099609375 to 1.8984375
- w_query: bfloat16 [1024, 1024], replicated, may hold values from -4 to 4
- w_kv: bfloat16 [1024, 512], replicated, may hold values from -4 to 4
- frame_attention_gain: bfloat16 [1024], replicated, may hold values from 0.099609375 to 1.8984375
Outputs:
- attended: bfloat16 [32, 512, 1024], P(('groups', 'tm')), parts along dimension 0
The draws below stay inside these ranges and needn't reach their ends.
There are 2 independent parts, one for each index of `groups`. The reference program is written for one: setup_inputs(seed, part) draws one part's arguments, and reference() takes and returns one part's arrays. A program takes and returns all parts, laid end to end along the dimension named above; an argument that names none is the same for every part. Nothing has to cross between parts.
All inputs are finite; a program needn't handle non-finite values.
Results may differ from the reference program's by a relative error of at most 0.028.
The reference program's roundings to bfloat16 on the way count: a program that leaves them out, or rounds other values in their place, can miss the bound.
Values may be sent and summed in bfloat16 or wider, within the bound.
No kernel may reach another device: no remote copies, remote signals or barrier semaphores. Data moves between devices by JAX's collectives and lax.ppermute only.
A program may use at most 64 MiB of HBM per device.

```python
import math
import jax
import jax.numpy as jnp
from jax import lax

D = 1024
HEADS = 8
HD = 128
KVH = 2
P_SIZE = 512
SB = 16
SPAN = 128
ROWS_DEV = 512
FRAMES = 16
N_TM = 16


def draw_space_time(key, part):
    subkeys = jax.random.split(jax.random.fold_in(key, 11), 1)
    standard = jax.random.normal(subkeys[0], (N_TM, ROWS_DEV, D), jnp.float32)
    return jnp.clip(standard, -6.0, 6.0).astype(jnp.bfloat16)


def paired_weights(base_key):
    subkeys = jax.random.split(jax.random.fold_in(base_key, 23), 3)
    query_scale = 2.5 / math.sqrt(D)
    query_weight = jax.random.normal(subkeys[0], (D, HEADS * HD), jnp.float32) * query_scale
    key_weight = jax.random.normal(subkeys[1], (D, KVH * HD), jnp.float32) / math.sqrt(D)
    value_weight = jax.random.normal(subkeys[2], (D, KVH * HD), jnp.float32) / math.sqrt(D)
    joined = jnp.concatenate([key_weight, value_weight], axis=1)
    return (jnp.clip(query_weight, -4.0, 4.0), jnp.clip(joined, -4.0, 4.0))


def draw_w_query(key, part):
    return paired_weights(key)[0].astype(jnp.bfloat16)


def draw_w_kv(key, part):
    return paired_weights(key)[1].astype(jnp.bfloat16)


def centred(own_key, shape, deviation, reach, kind=jnp.bfloat16):
    values = jax.random.normal(own_key, shape, jnp.float32) * deviation
    return jnp.minimum(jnp.maximum(values, -reach), reach).astype(kind)


def setup_inputs(seed: int = 0, part: int = 0) -> dict:
    key_of = jax.random.split(jax.random.key(seed), 7)
    part_keys = jax.random.split(jax.random.fold_in(key_of[6], part), 7)
    space_time = draw_space_time(jax.random.fold_in(jax.random.fold_in(key_of[6], part), 71), part)
    w_lin = centred(key_of[1], (D, 3 * D), D ** -0.5, 0.1875)
    gain_lin = jnp.clip(1.0 + 0.18 * jax.random.normal(key_of[2], (D,), jnp.float32), 0.099609375, 1.8984375).astype(jnp.bfloat16)
    w_query = draw_w_query(jax.random.fold_in(key_of[6], 71), part)
    w_kv = draw_w_kv(jax.random.fold_in(key_of[6], 71), part)
    frame_attention_gain = jnp.clip(1.0 + 0.18 * jax.random.normal(key_of[5], (D,), jnp.float32), 0.099609375, 1.8984375).astype(jnp.bfloat16)
    return dict(space_time=space_time, w_lin=w_lin, gain_lin=gain_lin, w_query=w_query, w_kv=w_kv, frame_attention_gain=frame_attention_gain)


epsilon = 1e-06

def reference(space_time, w_lin, gain_lin, w_query, w_kv, frame_attention_gain):
    time_ranges = N_TM // SB
    causal_mask = jnp.tril(jnp.ones((SPAN, SPAN), jnp.float32)) > 0
    line_gain = gain_lin.astype(jnp.float32).reshape(HEADS, HD)
    sequences = space_time.reshape(time_ranges, SB, ROWS_DEV, D).transpose(1, 0, 2, 3).reshape(SB, time_ranges * ROWS_DEV, D)

    def block_mixer(sequence):
        packed = jnp.dot(sequence, w_lin, preferred_element_type=jnp.float32).astype(jnp.bfloat16)
        span_count = sequence.shape[0] // SPAN
        query_rows = packed[:, :D].reshape(span_count, SPAN, HEADS, HD)
        key_rows = packed[:, D:2 * D].reshape(span_count, SPAN, HEADS, HD)
        value_rows = packed[:, 2 * D:].reshape(span_count, SPAN, HEADS, HD)

        def advance(carried, pieces):
            expanded_query_heads = pieces[0].astype(jnp.float32)
            expanded_key_heads = pieces[1].astype(jnp.float32)
            value_wide = pieces[2].astype(jnp.float32)
            rounded = lax.optimization_barrier(carried.astype(jnp.bfloat16)).astype(jnp.float32)
            readout = jnp.einsum('nhd,hde->nhe', expanded_query_heads, rounded)
            attention_logits = jnp.einsum('lzx,uzx->zlu', expanded_query_heads, expanded_key_heads)
            weights = lax.optimization_barrier(jnp.where(causal_mask, attention_logits, 0.0).astype(jnp.bfloat16)).astype(jnp.float32)
            local_sum = jnp.einsum('hnm,mhe->nhe', weights, value_wide)
            updated = carried + jnp.einsum('nhd,nhe->hde', expanded_key_heads, value_wide)
            return (updated, readout + local_sum)
        _, outputs = lax.scan(advance, jnp.zeros((HEADS, HD, HD), jnp.float32), (query_rows, key_rows, value_rows))
        outputs = outputs.reshape(-1, HEADS, HD)
        mean_square = lax.optimization_barrier(jnp.mean(outputs * outputs, axis=-1, keepdims=True))
        normed = outputs * lax.rsqrt(mean_square + epsilon) * line_gain
        return (sequence.astype(jnp.float32) + normed.reshape(-1, D)).astype(jnp.bfloat16)
    hidden = lax.map(block_mixer, sequences)
    frames_all = hidden.reshape(SB, FRAMES, P_SIZE // SB, D).transpose(1, 0, 2, 3).reshape(FRAMES * P_SIZE, D)
    widened = frames_all.astype(jnp.float32)
    mean_square = lax.optimization_barrier(jnp.mean(widened * widened, axis=-1, keepdims=True))
    normed = (widened * lax.rsqrt(mean_square + epsilon) * frame_attention_gain.astype(jnp.float32)).astype(jnp.bfloat16)
    group_size = HEADS // KVH
    queries = jnp.dot(normed, w_query, preferred_element_type=jnp.float32).astype(jnp.bfloat16)
    queries = queries.reshape(FRAMES, P_SIZE, KVH, group_size, HD)
    key_value_product = jnp.dot(normed, w_kv, preferred_element_type=jnp.float32).astype(jnp.bfloat16)
    key_value_product = key_value_product.reshape(FRAMES, P_SIZE, 2 * KVH * HD)
    positions = jnp.arange(2 * P_SIZE)
    scale_factor = 1.0 / math.sqrt(HD)

    def frame_attend(frame_index):
        current = lax.dynamic_index_in_dim(key_value_product, frame_index, 0, keepdims=False)
        earlier = lax.dynamic_index_in_dim(key_value_product, jnp.maximum(frame_index - 1, 0), 0, keepdims=False)
        window = jnp.concatenate([earlier, current], axis=0)
        key_rows = window[:, :KVH * HD].reshape(2 * P_SIZE, KVH, HD).astype(jnp.float32)
        value_rows = window[:, KVH * HD:].reshape(2 * P_SIZE, KVH, HD).astype(jnp.float32)
        query_rows = lax.dynamic_index_in_dim(queries, frame_index, 0, keepdims=False).astype(jnp.float32)
        attention_logits = jnp.einsum('pkgd,mkd->kgpm', query_rows, key_rows) * scale_factor
        usable_key = (positions >= P_SIZE) | (frame_index > 0)
        attention_logits = jnp.where(usable_key, attention_logits, -jnp.inf)
        largest = lax.optimization_barrier(jnp.max(attention_logits, axis=-1, keepdims=True))
        raised = jnp.exp(attention_logits - largest)
        weights = raised / lax.optimization_barrier(jnp.sum(raised, axis=-1, keepdims=True))
        weights = lax.optimization_barrier(weights.astype(jnp.bfloat16)).astype(jnp.float32)
        result = jnp.einsum('kgpm,mkd->pkgd', weights, value_rows)
        return result.astype(jnp.bfloat16).reshape(P_SIZE, D)
    return lax.map(frame_attend, jnp.arange(FRAMES, dtype=jnp.int32))
```

```python
import functools
import math

import jax
import jax.numpy as jnp
from jax import lax
from jax.experimental import pallas as pl
from jax.experimental.pallas import tpu as pltpu
from jax.sharding import PartitionSpec as P

HEADS = 8
HD = 128
KVH = 2
SB = 16
SPAN = 128
PAIR = 2

epsilon = 1e-06
MIB = 1 << 20


def shifted(block, axis, distance):
    devices = range(lax.axis_size(axis))
    route = [(i - distance, i) for i in devices if i - distance in devices]
    return lax.ppermute(block, axis, route)


def dot(a, b):
    return jnp.dot(a, b, preferred_element_type=jnp.float32)


def dot_nt(a, b):
    return lax.dot_general(a, b, (((1,), (1,)), ((), ())), preferred_element_type=jnp.float32)


def dot_tn(a, b):
    return lax.dot_general(a, b, (((0,), (0,)), ((), ())), preferred_element_type=jnp.float32)


def mixer_kernel(has_state, *refs):
    if has_state:
        tokens_ref, residual_ref, wq_ref, wk_ref, wv_ref, gain_ref, state_ref, out_ref = refs
    else:
        tokens_ref, residual_ref, wq_ref, wk_ref, wv_ref, gain_ref, out_ref = refs
    tokens = tokens_ref[...]
    rows = tokens.shape[0]
    query = dot(tokens, wq_ref[...]).astype(jnp.bfloat16)
    key = dot(tokens, wk_ref[...]).astype(jnp.bfloat16)
    value = dot(tokens, wv_ref[...]).astype(jnp.bfloat16)
    causal = lax.broadcasted_iota(jnp.int32, (SPAN, SPAN), 0) >= lax.broadcasted_iota(
        jnp.int32, (SPAN, SPAN), 1
    )
    for head in range(PAIR):
        lanes = slice(head * HD, (head + 1) * HD)
        gain = gain_ref[:, lanes].astype(jnp.float32)
        state = state_ref[head] if has_state else None
        for span in range(rows // SPAN):
            here = slice(span * SPAN, (span + 1) * SPAN)
            q, k, v = query[here, lanes], key[here, lanes], value[here, lanes]
            local = jnp.where(causal, dot_nt(q, k), 0.0).astype(jnp.bfloat16)
            if state is None:
                mixed = dot(local, v)
            else:
                mixed = dot(
                    jnp.concatenate([q, local], axis=1),
                    jnp.concatenate([state.astype(jnp.bfloat16), v], axis=0),
                )
            if (span + 1) * SPAN < rows:
                update = dot_tn(k, v)
                state = update if state is None else state + update
            mean_square = jnp.mean(mixed * mixed, axis=-1, keepdims=True)
            normed = mixed * lax.rsqrt(mean_square + epsilon) * gain
            out_ref[here, lanes] = (
                residual_ref[here, lanes].astype(jnp.float32) + normed
            ).astype(jnp.bfloat16)


def mixer(tokens, w_lin, gain_lin, state):
    rows, width = tokens.shape
    steps = HEADS // PAIR
    columns = PAIR * HD
    in_specs = [
        pl.BlockSpec((rows, width), lambda c: (0, 0)),
        pl.BlockSpec((rows, columns), lambda c: (0, c)),
        pl.BlockSpec((width, columns), lambda c: (0, c)),
        pl.BlockSpec((width, columns), lambda c: (0, steps + c)),
        pl.BlockSpec((width, columns), lambda c: (0, 2 * steps + c)),
        pl.BlockSpec((1, columns), lambda c: (0, c)),
    ]
    operands = [tokens, tokens, w_lin, w_lin, w_lin, gain_lin.reshape(1, width)]
    if state is not None:
        in_specs.append(pl.BlockSpec((PAIR, HD, HD), lambda c: (c, 0, 0)))
        operands.append(state)
    return pl.pallas_call(
        functools.partial(mixer_kernel, state is not None),
        grid=(steps,),
        in_specs=in_specs,
        out_specs=pl.BlockSpec((rows, columns), lambda c: (0, c)),
        out_shape=jax.ShapeDtypeStruct((rows, width), jnp.bfloat16),
        compiler_params=pltpu.CompilerParams(vmem_limit_bytes=24 * MIB),
        cost_estimate=pl.CostEstimate(
            flops=2 * rows * width * 3 * width + 8 * rows * SPAN * width,
            bytes_accessed=2 * (3 * width * width + 2 * rows * width),
            transcendentals=rows * HEADS,
        ),
        name="mixer",
    )(*operands)


def incoming_state(tokens, w_lin, time_ranges):
    rows, width = tokens.shape
    packed = dot(tokens, w_lin[:, width:]).astype(jnp.bfloat16).reshape(rows, 2, HEADS, HD)
    block_total = jnp.einsum(
        "nhd,nhe->hde", packed[:, 0], packed[:, 1], preferred_element_type=jnp.float32
    )
    within = lax.axis_index("tm") // SB

    def advance_hop(turn_index, running_total):
        moved = shifted(running_total + block_total, "tm", SB)
        return jnp.where(within > 0, moved, 0.0)

    return lax.fori_loop(0, time_ranges - 1, advance_hop, jnp.zeros_like(block_total))


def pairs_kernel(hidden_ref, gain_ref, w_ref, normed_ref, pairs_ref):
    widened = hidden_ref[...].astype(jnp.float32)
    mean_square = jnp.mean(widened * widened, axis=-1, keepdims=True)
    normed = (
        widened * lax.rsqrt(mean_square + epsilon) * gain_ref[...].astype(jnp.float32)
    ).astype(jnp.bfloat16)
    normed_ref[...] = normed
    pairs_ref[...] = dot(normed, w_ref[...]).astype(jnp.bfloat16)


def make_pairs(hidden, gain, w_kv):
    rows, width = hidden.shape
    wide = w_kv.shape[1]
    block = rows // 2
    return pl.pallas_call(
        pairs_kernel,
        grid=(rows // block,),
        in_specs=[
            pl.BlockSpec((block, width), lambda i: (i, 0)),
            pl.BlockSpec((1, width), lambda i: (0, 0)),
            pl.BlockSpec((width, wide), lambda i: (0, 0)),
        ],
        out_specs=[
            pl.BlockSpec((block, width), lambda i: (i, 0)),
            pl.BlockSpec((block, wide), lambda i: (i, 0)),
        ],
        out_shape=[
            jax.ShapeDtypeStruct((rows, width), jnp.bfloat16),
            jax.ShapeDtypeStruct((rows, wide), jnp.bfloat16),
        ],
        compiler_params=pltpu.CompilerParams(vmem_limit_bytes=16 * MIB),
        cost_estimate=pl.CostEstimate(
            flops=2 * rows * width * wide,
            bytes_accessed=2 * (2 * rows * width + width * wide + rows * wide),
            transcendentals=rows,
        ),
        name="pairs",
    )(hidden, gain.reshape(1, width), w_kv)


SCORE_SCALE = math.log2(math.e) / math.sqrt(HD)


def with_ones(value):
    return jnp.concatenate([value, jnp.ones_like(value)], axis=1)


def own_kernel(normed_ref, w_ref, key_ref, value_ref, query_ref, partial_ref, log_ref):
    query = dot(normed_ref[...], w_ref[...]).astype(jnp.bfloat16)
    query_ref[...] = query
    key = key_ref[...]
    value = with_ones(value_ref[...])
    for head in range(PAIR):
        lanes = slice(head * HD, (head + 1) * HD)
        scores = dot_nt(query[:, lanes], key)
        largest = jnp.max(scores, axis=-1, keepdims=True)
        raised = jnp.exp2((scores - largest) * SCORE_SCALE).astype(jnp.bfloat16)
        summed = dot(raised, value)
        total = summed[:, HD:]
        partial_ref[:, lanes] = summed[:, :HD] / total
        log_ref[0, :, head : head + 1] = largest * SCORE_SCALE + jnp.log2(total[:, :1])


def own_frame(normed, w_query, pairs):
    rows, width = normed.shape
    steps = HEADS // PAIR
    columns = PAIR * HD
    per_kv = HEADS // KVH // PAIR
    return pl.pallas_call(
        own_kernel,
        grid=(steps,),
        in_specs=[
            pl.BlockSpec((rows, width), lambda c: (0, 0)),
            pl.BlockSpec((width, columns), lambda c: (0, c)),
            pl.BlockSpec((rows, HD), lambda c: (0, c // per_kv)),
            pl.BlockSpec((rows, HD), lambda c: (0, KVH + c // per_kv)),
        ],
        out_specs=[
            pl.BlockSpec((rows, columns), lambda c: (0, c)),
            pl.BlockSpec((rows, columns), lambda c: (0, c)),
            pl.BlockSpec((1, rows, PAIR), lambda c: (c, 0, 0)),
        ],
        out_shape=[
            jax.ShapeDtypeStruct((rows, width), jnp.bfloat16),
            jax.ShapeDtypeStruct((rows, width), jnp.float32),
            jax.ShapeDtypeStruct((steps, rows, PAIR), jnp.float32),
        ],
        compiler_params=pltpu.CompilerParams(vmem_limit_bytes=32 * MIB),
        cost_estimate=pl.CostEstimate(
            flops=2 * rows * width * width + 4 * rows * rows * width,
            bytes_accessed=2 * width * width + 8 * rows * width,
            transcendentals=rows * rows * HEADS,
        ),
        name="own_frame",
    )(normed, w_query, pairs, pairs)


def earlier_kernel(query_ref, key_ref, value_ref, partial_ref, log_ref, usable_ref, out_ref):
    query = query_ref[...]
    key = key_ref[...]
    value = with_ones(value_ref[...])
    barred = jnp.where(usable_ref[0] > 0, 0.0, -jnp.inf)
    for head in range(PAIR):
        lanes = slice(head * HD, (head + 1) * HD)
        own = log_ref[0, :, head : head + 1]
        scores = dot_nt(query[:, lanes], key)
        here = jnp.max(scores, axis=-1, keepdims=True) * SCORE_SCALE + barred
        largest = jnp.maximum(here, own)
        raised = jnp.exp2(scores * SCORE_SCALE - (largest - barred)).astype(jnp.bfloat16)
        summed = dot(raised, value)
        share = jnp.exp2(own - largest)
        out_ref[:, lanes] = (
            (partial_ref[:, lanes] * share + summed[:, :HD]) / (share + summed[:, HD:])
        ).astype(jnp.bfloat16)


def earlier_frame(query, earlier_pairs, partial, log_total, usable):
    rows, width = query.shape
    steps = HEADS // PAIR
    columns = PAIR * HD
    per_kv = HEADS // KVH // PAIR
    return pl.pallas_call(
        earlier_kernel,
        grid=(steps,),
        in_specs=[
            pl.BlockSpec((rows, columns), lambda c: (0, c)),
            pl.BlockSpec((rows, HD), lambda c: (0, c // per_kv)),
            pl.BlockSpec((rows, HD), lambda c: (0, KVH + c // per_kv)),
            pl.BlockSpec((rows, columns), lambda c: (0, c)),
            pl.BlockSpec((1, rows, PAIR), lambda c: (c, 0, 0)),
            pl.BlockSpec(memory_space=pltpu.SMEM),
        ],
        out_specs=pl.BlockSpec((rows, columns), lambda c: (0, c)),
        out_shape=jax.ShapeDtypeStruct((rows, width), jnp.bfloat16),
        compiler_params=pltpu.CompilerParams(vmem_limit_bytes=32 * MIB),
        cost_estimate=pl.CostEstimate(
            flops=4 * rows * rows * width,
            bytes_accessed=10 * rows * width,
            transcendentals=rows * rows * HEADS,
        ),
        name="earlier_frame",
    )(query, earlier_pairs, earlier_pairs, partial, log_total, usable)


def body(space_time, w_lin, gain_lin, w_query, w_kv, frame_attention_gain):
    tokens = space_time[0]
    rows, width = tokens.shape
    devices = lax.axis_size("tm")
    time_ranges = devices // SB
    state = incoming_state(tokens, w_lin, time_ranges) if time_ranges > 1 else None
    hidden = mixer(tokens, w_lin, gain_lin, state)
    teams = [[t * SB + s for s in range(SB)] for t in range(time_ranges)]
    frame_rows = lax.all_to_all(
        hidden.reshape(SB, rows // SB, width),
        "tm",
        0,
        0,
        axis_index_groups=teams,
        tiled=True,
    ).reshape(rows, width)
    normed, pairs = make_pairs(frame_rows, frame_attention_gain, w_kv)
    earlier_pairs = shifted(pairs, "tm", 1)
    query, partial, log_total = own_frame(normed, w_query, pairs)
    usable = (lax.axis_index("tm") > 0).astype(jnp.int32).reshape(1)
    attended = earlier_frame(query, earlier_pairs, partial, log_total, usable)
    return attended[None]


def solution(mesh):
    placed = (P(("groups", "tm"), None, None), P(), P(), P(), P(), P())
    return jax.shard_map(
        body, mesh=mesh, in_specs=placed, out_specs=P(("groups", "tm"), None, None), check_vma=False
    )
```

```python
import functools
import math

import jax
import jax.numpy as jnp
from jax import lax
from jax.experimental import pallas as pl
from jax.experimental.pallas import tpu as pltpu
from jax.sharding import PartitionSpec as P

HEADS = 8
HD = 128
KVH = 2
SB = 16
SPAN = 128
PAIR = 2

APART = (0, 15, 14, 4, 10, 3, 9, 2, 8, 1, 7, 13, 6, 12, 5, 11)

epsilon = 1e-06
MIB = 1 << 20


def shifted(block, axis, distance):
    devices = range(lax.axis_size(axis))
    route = [(i - distance, i) for i in devices if i - distance in devices]
    return lax.ppermute(block, axis, route)


def dot(a, b):
    return jnp.dot(a, b, preferred_element_type=jnp.float32)


def dot_nt(a, b):
    return lax.dot_general(a, b, (((1,), (1,)), ((), ())), preferred_element_type=jnp.float32)


def dot_tn(a, b):
    return lax.dot_general(a, b, (((0,), (0,)), ((), ())), preferred_element_type=jnp.float32)


def mixer_kernel(has_state, place_ref, *refs):
    if has_state:
        state_ref, *refs = refs
    tokens_ref, residual_ref, wq_ref, wk_ref, wv_ref, gain_ref, *tiles, hidden_ref = refs
    tokens = tokens_ref[...]
    rows = tokens.shape[0]
    query = dot(tokens, wq_ref[...]).astype(jnp.bfloat16)
    key = dot(tokens, wk_ref[...]).astype(jnp.bfloat16)
    value = dot(tokens, wv_ref[...]).astype(jnp.bfloat16)
    causal = lax.broadcasted_iota(jnp.int32, (SPAN, SPAN), 0) >= lax.broadcasted_iota(
        jnp.int32, (SPAN, SPAN), 1
    )
    spans = rows // SPAN
    units = []
    for head in range(PAIR):
        for span in range(spans):
            here = slice(span * SPAN, (span + 1) * SPAN)
            lanes = slice(head * HD, (head + 1) * HD)
            units.append((head, span, here, lanes))
    local, before = {}, {}
    for head, span, here, lanes in units:
        scores = dot_nt(query[here, lanes], key[here, lanes])
        local[head, span] = jnp.where(causal, scores, 0.0).astype(jnp.bfloat16)
    for head in range(PAIR):
        state = state_ref[head] if has_state else None
        for span in range(spans):
            before[head, span] = state
            if span + 1 < spans:
                here = slice(span * SPAN, (span + 1) * SPAN)
                lanes = slice(head * HD, (head + 1) * HD)
                update = dot_tn(key[here, lanes], value[here, lanes])
                state = update if state is None else state + update
    mixed = {}
    for head, span, here, lanes in units:
        state = before[head, span]
        if state is None:
            mixed[head, span] = dot(local[head, span], value[here, lanes])
        else:
            mixed[head, span] = dot(
                jnp.concatenate([query[here, lanes], local[head, span]], axis=1),
                jnp.concatenate([state.astype(jnp.bfloat16), value[here, lanes]], axis=0),
            )
    for head, span, here, lanes in units:
        out = mixed[head, span]
        mean_square = jnp.mean(out * out, axis=-1, keepdims=True)
        normed = out * lax.rsqrt(mean_square + epsilon) * gain_ref[:, lanes].astype(jnp.float32)
        hidden_ref[here, lanes] = (
            residual_ref[here, lanes].astype(jnp.float32) + normed
        ).astype(jnp.bfloat16)
    size = rows // SB
    for apart, tile in zip(APART, tiles):
        start = pl.multiple_of((place_ref[0] ^ apart) * size, size)
        tile[...] = hidden_ref[pl.ds(start, size), :]


def mixer(place, tokens, w_lin, gain_lin, state):
    rows, width = tokens.shape
    steps = HEADS // PAIR
    columns = PAIR * HD
    in_specs = [pl.BlockSpec(memory_space=pltpu.SMEM)]
    operands = [place]
    if state is not None:
        in_specs.append(pl.BlockSpec((PAIR, HD, HD), lambda c: (c, 0, 0)))
        operands.append(state)
    in_specs += [
        pl.BlockSpec((rows, width), lambda c: (0, 0)),
        pl.BlockSpec((rows, columns), lambda c: (0, c)),
        pl.BlockSpec((width, columns), lambda c: (0, c)),
        pl.BlockSpec((width, columns), lambda c: (0, steps + c)),
        pl.BlockSpec((width, columns), lambda c: (0, 2 * steps + c)),
        pl.BlockSpec((1, columns), lambda c: (0, c)),
    ]
    operands += [tokens, tokens, w_lin, w_lin, w_lin, gain_lin.reshape(1, width)]
    return pl.pallas_call(
        functools.partial(mixer_kernel, state is not None),
        grid=(steps,),
        in_specs=in_specs,
        out_specs=[pl.BlockSpec((rows // SB, columns), lambda c: (0, c))] * SB,
        out_shape=[jax.ShapeDtypeStruct((rows // SB, width), jnp.bfloat16)] * SB,
        scratch_shapes=[pltpu.VMEM((rows, columns), jnp.bfloat16)],
        compiler_params=pltpu.CompilerParams(vmem_limit_bytes=56 * MIB),
        cost_estimate=pl.CostEstimate(
            flops=2 * rows * width * 3 * width + 8 * rows * SPAN * width,
            bytes_accessed=2 * (3 * width * width + 2 * rows * width),
            transcendentals=rows * HEADS,
        ),
        name="mixer",
    )(*operands)


def incoming_state(tokens, w_lin, time_ranges):
    rows, width = tokens.shape
    packed = dot(tokens, w_lin[:, width:]).astype(jnp.bfloat16).reshape(rows, 2, HEADS, HD)
    block_total = jnp.einsum(
        "nhd,nhe->hde", packed[:, 0], packed[:, 1], preferred_element_type=jnp.float32
    )
    within = lax.axis_index("tm") // SB

    def advance_hop(turn_index, running_total):
        moved = shifted(running_total + block_total, "tm", SB)
        return jnp.where(within > 0, moved, 0.0)

    return lax.fori_loop(0, time_ranges - 1, advance_hop, jnp.zeros_like(block_total))


def pairs_kernel(gain_ref, w_ref, *refs):
    tiles, normed_ref, pairs_ref = refs[:-2], refs[-2], refs[-1]
    widened = jnp.concatenate([tile[...] for tile in tiles], axis=0).astype(jnp.float32)
    mean_square = jnp.mean(widened * widened, axis=-1, keepdims=True)
    normed = (
        widened * lax.rsqrt(mean_square + epsilon) * gain_ref[...].astype(jnp.float32)
    ).astype(jnp.bfloat16)
    normed_ref[...] = normed
    pairs_ref[...] = dot(normed, w_ref[...]).astype(jnp.bfloat16)


def make_pairs(tiles, gain, w_kv):
    size, width = tiles[0].shape
    rows = size * len(tiles)
    wide = w_kv.shape[1]
    return pl.pallas_call(
        pairs_kernel,
        out_shape=[
            jax.ShapeDtypeStruct((rows, width), jnp.bfloat16),
            jax.ShapeDtypeStruct((rows, wide), jnp.bfloat16),
        ],
        compiler_params=pltpu.CompilerParams(vmem_limit_bytes=16 * MIB),
        cost_estimate=pl.CostEstimate(
            flops=2 * rows * width * wide,
            bytes_accessed=2 * (2 * rows * width + width * wide + rows * wide),
            transcendentals=rows,
        ),
        name="pairs",
    )(gain.reshape(1, width), w_kv, *tiles)


SCORE_SCALE = math.log2(math.e) / math.sqrt(HD)


def with_ones(value):
    return jnp.concatenate([value, jnp.ones_like(value)], axis=1)


def head_lanes(head):
    return slice(head * HD, (head + 1) * HD)


def own_kernel(normed_ref, w_ref, key_ref, value_ref, query_ref, partial_ref, log_ref):
    query = dot(normed_ref[...], w_ref[...]).astype(jnp.bfloat16)
    query_ref[...] = query
    key = key_ref[...]
    value = with_ones(value_ref[...])
    heads = query.shape[1] // HD
    scores = dot_nt(query[:, head_lanes(0)], key)
    for head in range(heads):
        upcoming = dot_nt(query[:, head_lanes(head + 1)], key) if head + 1 < heads else None
        largest = jnp.max(scores, axis=-1, keepdims=True)
        raised = jnp.exp2((scores - largest) * SCORE_SCALE).astype(jnp.bfloat16)
        summed = dot(raised, value)
        total = summed[:, HD:]
        partial_ref[:, head_lanes(head)] = summed[:, :HD] / total
        log_ref[0, :, head : head + 1] = largest * SCORE_SCALE + jnp.log2(total[:, :1])
        scores = upcoming


def own_frame(normed, w_query, pairs):
    rows, width = normed.shape
    group = HEADS // KVH
    columns = group * HD
    return pl.pallas_call(
        own_kernel,
        grid=(KVH,),
        in_specs=[
            pl.BlockSpec((rows, width), lambda c: (0, 0)),
            pl.BlockSpec((width, columns), lambda c: (0, c)),
            pl.BlockSpec((rows, HD), lambda c: (0, c)),
            pl.BlockSpec((rows, HD), lambda c: (0, KVH + c)),
        ],
        out_specs=[
            pl.BlockSpec((rows, columns), lambda c: (0, c)),
            pl.BlockSpec((rows, columns), lambda c: (0, c)),
            pl.BlockSpec((1, rows, group), lambda c: (c, 0, 0)),
        ],
        out_shape=[
            jax.ShapeDtypeStruct((rows, width), jnp.bfloat16),
            jax.ShapeDtypeStruct((rows, width), jnp.float32),
            jax.ShapeDtypeStruct((KVH, rows, group), jnp.float32),
        ],
        compiler_params=pltpu.CompilerParams(vmem_limit_bytes=32 * MIB),
        cost_estimate=pl.CostEstimate(
            flops=2 * rows * width * width + 4 * rows * rows * width,
            bytes_accessed=2 * width * width + 8 * rows * width,
            transcendentals=rows * rows * HEADS,
        ),
        name="own_frame",
    )(normed, w_query, pairs, pairs)


def earlier_kernel(place_ref, query_ref, key_ref, value_ref, partial_ref, log_ref, out_ref):
    rows = query_ref.shape[0]
    heads = query_ref.shape[1] // HD
    key = key_ref[...]
    value = with_ones(value_ref[...])
    barred = jnp.where(place_ref[1] > 0, 0.0, -jnp.inf)
    size = rows // SB
    scores = dot_nt(query_ref[:, head_lanes(0)], key)
    for head in range(heads):
        lanes = head_lanes(head)
        upcoming = dot_nt(query_ref[:, head_lanes(head + 1)], key) if head + 1 < heads else None
        own = log_ref[0, :, head : head + 1]
        here = jnp.max(scores, axis=-1, keepdims=True) * SCORE_SCALE + barred
        largest = jnp.maximum(here, own)
        raised = jnp.exp2(scores * SCORE_SCALE - (largest - barred)).astype(jnp.bfloat16)
        summed = dot(raised, value)
        share = jnp.exp2(own - largest)
        mixed = (
            (partial_ref[:, lanes] * share + summed[:, :HD]) / (share + summed[:, HD:])
        ).astype(jnp.bfloat16)
        for slot, apart in enumerate(APART):
            start = pl.multiple_of((place_ref[0] ^ apart) * size, size)
            out_ref[pl.ds(start, size), lanes] = mixed[slot * size : (slot + 1) * size]
        scores = upcoming


def earlier_frame(place, query, earlier_pairs, partial, log_total):
    rows, width = query.shape
    group = HEADS // KVH
    columns = group * HD
    return pl.pallas_call(
        earlier_kernel,
        grid=(KVH,),
        in_specs=[
            pl.BlockSpec(memory_space=pltpu.SMEM),
            pl.BlockSpec((rows, columns), lambda c: (0, c)),
            pl.BlockSpec((rows, HD), lambda c: (0, c)),
            pl.BlockSpec((rows, HD), lambda c: (0, KVH + c)),
            pl.BlockSpec((rows, columns), lambda c: (0, c)),
            pl.BlockSpec((1, rows, group), lambda c: (c, 0, 0)),
        ],
        out_specs=pl.BlockSpec((rows, columns), lambda c: (0, c)),
        out_shape=jax.ShapeDtypeStruct((rows, width), jnp.bfloat16),
        compiler_params=pltpu.CompilerParams(vmem_limit_bytes=32 * MIB),
        cost_estimate=pl.CostEstimate(
            flops=4 * rows * rows * width,
            bytes_accessed=10 * rows * width,
            transcendentals=rows * rows * HEADS,
        ),
        name="earlier_frame",
    )(place, query, earlier_pairs, earlier_pairs, partial, log_total)


def exchange(tiles):
    devices = lax.axis_size("tm")
    arrived = []
    for apart, tile in zip(APART, tiles):
        route = [(i, i - i % SB + (i % SB ^ apart)) for i in range(devices)]
        arrived.append(lax.ppermute(tile, "tm", route) if apart else tile)
    return arrived


def body(space_time, w_lin, gain_lin, w_query, w_kv, frame_attention_gain):
    tokens = space_time[0]
    time_ranges = lax.axis_size("tm") // SB
    index = lax.axis_index("tm")
    place = jnp.stack([index % SB, (index > 0).astype(jnp.int32)])
    state = incoming_state(tokens, w_lin, time_ranges) if time_ranges > 1 else None
    tiles = exchange(mixer(place, tokens, w_lin, gain_lin, state))
    normed, pairs = make_pairs(tiles, frame_attention_gain, w_kv)
    earlier_pairs = shifted(pairs, "tm", 1)
    query, partial, log_total = own_frame(normed, w_query, pairs)
    attended = earlier_frame(place, query, earlier_pairs, partial, log_total)
    return attended[None]


def solution(mesh):
    placed = (P(("groups", "tm"), None, None), P(), P(), P(), P(), P())
    return jax.shard_map(
        body, mesh=mesh, in_specs=placed, out_specs=P(("groups", "tm"), None, None), check_vma=False
    )
```

```python
import functools
import math

import jax
import jax.numpy as jnp
from jax import lax
from jax.experimental import pallas as pl
from jax.experimental.pallas import tpu as pltpu
from jax.sharding import PartitionSpec as P

HEADS = 8
HD = 128
KVH = 2
SB = 16
SPAN = 128
PAIR = 2

epsilon = 1e-06
MIB = 1 << 20


def shifted(block, axis, distance):
    devices = range(lax.axis_size(axis))
    route = [(i - distance, i) for i in devices if i - distance in devices]
    return lax.ppermute(block, axis, route)


def dot(a, b):
    return jnp.dot(a, b, preferred_element_type=jnp.float32)


def dot_nt(a, b):
    return lax.dot_general(a, b, (((1,), (1,)), ((), ())), preferred_element_type=jnp.float32)


def dot_tn(a, b):
    return lax.dot_general(a, b, (((0,), (0,)), ((), ())), preferred_element_type=jnp.float32)


def head_lanes(head):
    return slice(head * HD, (head + 1) * HD)


def mixer_kernel(first, heads, has_state, *refs):
    if has_state:
        state_ref, *refs = refs
    tokens_ref, w_ref, gain_ref, out_ref, weights, arrived = refs
    rows, width = tokens_ref.shape
    spans = rows // SPAN
    columns = PAIR * HD
    pairs = heads // PAIR
    copies = []
    for pair in range(pairs):
        for part in range(3):
            start = part * width + first * HD + pair * columns
            copies.append(
                pltpu.make_async_copy(
                    w_ref.at[:, start : start + columns],
                    weights.at[pair, part],
                    arrived.at[pair, part],
                )
            )
    for copy in copies:
        copy.start()
    tokens = tokens_ref[...]
    gains = gain_ref[...].astype(jnp.float32).reshape(1, width)
    causal = lax.broadcasted_iota(jnp.int32, (SPAN, SPAN), 0) >= lax.broadcasted_iota(
        jnp.int32, (SPAN, SPAN), 1
    )

    def project(pair):
        packed = []
        for part in range(3):
            copies[3 * pair + part].wait()
            packed.append(dot(tokens, weights[pair, part]).astype(jnp.bfloat16))
        return packed

    def attend(pair, query, key, value):
        units = []
        for head in range(PAIR):
            for span in range(spans):
                here = slice(span * SPAN, (span + 1) * SPAN)
                units.append((head, span, here, head_lanes(head)))
        local, before, mixed = {}, {}, {}
        for head, span, here, lanes in units:
            scores = dot_nt(query[here, lanes], key[here, lanes])
            local[head, span] = jnp.where(causal, scores, 0.0).astype(jnp.bfloat16)
        for head, span, here, lanes in units:
            if span == 0:
                state = state_ref[pair * PAIR + head] if has_state else None
            before[head, span] = state
            if span + 1 < spans:
                update = dot_tn(key[here, lanes], value[here, lanes])
                state = update if state is None else state + update
        for head, span, here, lanes in units:
            if before[head, span] is None:
                mixed[head, span] = dot(local[head, span], value[here, lanes])
            else:
                mixed[head, span] = dot(
                    jnp.concatenate([query[here, lanes], local[head, span]], axis=1),
                    jnp.concatenate(
                        [before[head, span].astype(jnp.bfloat16), value[here, lanes]], axis=0
                    ),
                )
        for head, span, here, lanes in units:
            out = mixed[head, span]
            own = pair * PAIR + head
            mean_square = jnp.mean(out * out, axis=-1, keepdims=True)
            gain = gains[:, head_lanes(first + own)]
            normed = out * lax.rsqrt(mean_square + epsilon) * gain
            residual = tokens_ref[here, head_lanes(first + own)].astype(jnp.float32)
            out_ref[here, head_lanes(own)] = (residual + normed).astype(jnp.bfloat16)

    packed = project(0)
    for pair in range(pairs):
        upcoming = project(pair + 1) if pair + 1 < pairs else None
        attend(pair, *packed)
        packed = upcoming


def mixer(first, heads, tokens, w_lin, gain_lin, state):
    rows, width = tokens.shape
    columns = heads * HD
    operands = [tokens, w_lin, gain_lin]
    in_specs = [
        pl.BlockSpec(memory_space=pltpu.VMEM),
        pl.BlockSpec(memory_space=pl.ANY),
        pl.BlockSpec(memory_space=pltpu.VMEM),
    ]
    if state is not None:
        operands.insert(0, state[first : first + heads])
        in_specs.insert(0, pl.BlockSpec(memory_space=pltpu.VMEM))
    return pl.pallas_call(
        functools.partial(mixer_kernel, first, heads, state is not None),
        in_specs=in_specs,
        out_shape=jax.ShapeDtypeStruct((rows, columns), jnp.bfloat16),
        scratch_shapes=[
            pltpu.VMEM((heads // PAIR, 3, width, PAIR * HD), jnp.bfloat16),
            pltpu.SemaphoreType.DMA((heads // PAIR, 3)),
        ],
        compiler_params=pltpu.CompilerParams(vmem_limit_bytes=56 * MIB),
        cost_estimate=pl.CostEstimate(
            flops=2 * rows * width * 3 * columns + 8 * rows * SPAN * columns,
            bytes_accessed=2 * (3 * width * columns + rows * width + rows * columns),
            transcendentals=rows * heads,
        ),
        name="mixer",
    )(*operands)


def incoming_state(tokens, w_lin, time_ranges):
    rows, width = tokens.shape
    packed = dot(tokens, w_lin[:, width:]).astype(jnp.bfloat16).reshape(rows, 2, HEADS, HD)
    block_total = jnp.einsum(
        "nhd,nhe->hde", packed[:, 0], packed[:, 1], preferred_element_type=jnp.float32
    )
    within = lax.axis_index("tm") // SB

    def advance_hop(turn_index, running_total):
        moved = shifted(running_total + block_total, "tm", SB)
        return jnp.where(within > 0, moved, 0.0)

    return lax.fori_loop(0, time_ranges - 1, advance_hop, jnp.zeros_like(block_total))


def pairs_kernel(left_ref, right_ref, gain_ref, w_ref, normed_ref, pairs_ref):
    widened = jnp.concatenate([left_ref[...], right_ref[...]], axis=1).astype(jnp.float32)
    mean_square = jnp.mean(widened * widened, axis=-1, keepdims=True)
    normed = (
        widened * lax.rsqrt(mean_square + epsilon) * gain_ref[...].astype(jnp.float32).reshape(1, -1)
    ).astype(jnp.bfloat16)
    normed_ref[...] = normed
    pairs_ref[...] = dot(normed, w_ref[...]).astype(jnp.bfloat16)


def make_pairs(left, right, gain, w_kv):
    rows = left.shape[0]
    width, wide = w_kv.shape
    return pl.pallas_call(
        pairs_kernel,
        out_shape=[
            jax.ShapeDtypeStruct((rows, width), jnp.bfloat16),
            jax.ShapeDtypeStruct((rows, wide), jnp.bfloat16),
        ],
        compiler_params=pltpu.CompilerParams(vmem_limit_bytes=16 * MIB),
        cost_estimate=pl.CostEstimate(
            flops=2 * rows * width * wide,
            bytes_accessed=2 * (2 * rows * width + width * wide + rows * wide),
            transcendentals=rows,
        ),
        name="pairs",
    )(left, right, gain, w_kv)


SCORE_SCALE = math.log2(math.e) / math.sqrt(HD)


def with_ones(value):
    return jnp.concatenate([value, jnp.ones_like(value)], axis=1)


def own_kernel(normed_ref, w_ref, key_ref, value_ref, query_ref, partial_ref, log_ref):
    query = dot(normed_ref[...], w_ref[...]).astype(jnp.bfloat16)
    query_ref[...] = query
    key = key_ref[...]
    value = with_ones(value_ref[...])
    heads = query.shape[1] // HD
    scores = dot_nt(query[:, head_lanes(0)], key)
    for head in range(heads):
        upcoming = dot_nt(query[:, head_lanes(head + 1)], key) if head + 1 < heads else None
        largest = jnp.max(scores, axis=-1, keepdims=True)
        raised = jnp.exp2((scores - largest) * SCORE_SCALE).astype(jnp.bfloat16)
        summed = dot(raised, value)
        total = summed[:, HD:]
        partial_ref[:, head_lanes(head)] = summed[:, :HD] / total
        log_ref[:, head_lanes(head)] = largest * SCORE_SCALE + jnp.log2(total)
        scores = upcoming


def own_frame(normed, w_query, pairs):
    rows, width = normed.shape
    group = HEADS // KVH
    columns = group * HD
    return pl.pallas_call(
        own_kernel,
        grid=(KVH,),
        in_specs=[
            pl.BlockSpec((rows, width), lambda c: (0, 0)),
            pl.BlockSpec((width, columns), lambda c: (0, c)),
            pl.BlockSpec((rows, HD), lambda c: (0, c)),
            pl.BlockSpec((rows, HD), lambda c: (0, KVH + c)),
        ],
        out_specs=[
            pl.BlockSpec((rows, columns), lambda c: (0, c)),
            pl.BlockSpec((rows, columns), lambda c: (0, c)),
            pl.BlockSpec((rows, columns), lambda c: (0, c)),
        ],
        out_shape=[
            jax.ShapeDtypeStruct((rows, width), jnp.bfloat16),
            jax.ShapeDtypeStruct((rows, width), jnp.float32),
            jax.ShapeDtypeStruct((rows, width), jnp.float32),
        ],
        compiler_params=pltpu.CompilerParams(vmem_limit_bytes=32 * MIB),
        cost_estimate=pl.CostEstimate(
            flops=2 * rows * width * width + 4 * rows * rows * width,
            bytes_accessed=2 * width * width + 8 * rows * width,
            transcendentals=rows * rows * HEADS,
        ),
        name="own_frame",
    )(normed, w_query, pairs, pairs)


def earlier_kernel(query_ref, key_ref, value_ref, partial_ref, log_ref, out_ref):
    rows = query_ref.shape[0]
    heads = query_ref.shape[1] // HD
    key = key_ref[...]
    value = with_ones(value_ref[...])
    barred = jnp.where(lax.axis_index("tm") > 0, 0.0, -jnp.inf)
    scores = dot_nt(query_ref[:, head_lanes(0)], key)
    for head in range(heads):
        lanes = head_lanes(head)
        upcoming = dot_nt(query_ref[:, head_lanes(head + 1)], key) if head + 1 < heads else None
        own = log_ref[:, lanes]
        here = jnp.max(scores, axis=-1, keepdims=True) * SCORE_SCALE + barred
        largest = jnp.maximum(jnp.broadcast_to(here, own.shape), own)
        below = jnp.concatenate([largest - barred] * (rows // HD), axis=1)
        raised = jnp.exp2(scores * SCORE_SCALE - below).astype(jnp.bfloat16)
        summed = dot(raised, value)
        share = jnp.exp2(own - largest)
        out_ref[:, lanes] = (
            (partial_ref[:, lanes] * share + summed[:, :HD]) / (share + summed[:, HD:])
        ).astype(jnp.bfloat16)
        scores = upcoming


def earlier_frame(query, earlier_pairs, partial, log_total):
    rows, width = query.shape
    group = HEADS // KVH
    columns = group * HD
    return pl.pallas_call(
        earlier_kernel,
        grid=(KVH,),
        in_specs=[
            pl.BlockSpec((rows, columns), lambda c: (0, c)),
            pl.BlockSpec((rows, HD), lambda c: (0, c)),
            pl.BlockSpec((rows, HD), lambda c: (0, KVH + c)),
            pl.BlockSpec((rows, columns), lambda c: (0, c)),
            pl.BlockSpec((rows, columns), lambda c: (0, c)),
        ],
        out_specs=pl.BlockSpec((rows, columns), lambda c: (0, c)),
        out_shape=jax.ShapeDtypeStruct((rows, width), jnp.bfloat16),
        compiler_params=pltpu.CompilerParams(vmem_limit_bytes=32 * MIB),
        cost_estimate=pl.CostEstimate(
            flops=4 * rows * rows * width,
            bytes_accessed=10 * rows * width,
            transcendentals=rows * rows * HEADS,
        ),
        name="earlier_frame",
    )(query, earlier_pairs, earlier_pairs, partial, log_total)


def to_frames(part):
    rows, columns = part.shape
    teams = [[t * SB + s for s in range(SB)] for t in range(lax.axis_size("tm") // SB)]
    moved = lax.all_to_all(
        part.reshape(SB, rows // SB, columns), "tm", 0, 0, axis_index_groups=teams, tiled=True
    )
    return moved.reshape(rows, columns)


def body(space_time, w_lin, gain_lin, w_query, w_kv, frame_attention_gain):
    tokens = space_time[0]
    time_ranges = lax.axis_size("tm") // SB
    state = incoming_state(tokens, w_lin, time_ranges) if time_ranges > 1 else None
    half = HEADS // 2
    left = to_frames(mixer(0, half, tokens, w_lin, gain_lin, state))
    right = to_frames(mixer(half, half, tokens, w_lin, gain_lin, state))
    normed, pairs = make_pairs(left, right, frame_attention_gain, w_kv)
    earlier_pairs = shifted(pairs, "tm", 1)
    query, partial, log_total = own_frame(normed, w_query, pairs)
    attended = earlier_frame(query, earlier_pairs, partial, log_total)
    return attended[None]


def solution(mesh):
    placed = (P(("groups", "tm"), None, None), P(), P(), P(), P(), P())
    return jax.shard_map(
        body, mesh=mesh, in_specs=placed, out_specs=P(("groups", "tm"), None, None), check_vma=False
    )
```

```python
import functools
import math

import jax
import jax.numpy as jnp
from jax import lax
from jax.experimental import pallas as pl
from jax.experimental.pallas import tpu as pltpu
from jax.sharding import PartitionSpec as P

HEADS = 8
HD = 128
KVH = 2
SB = 16
SPAN = 128
PAIR = 2

APART = (0, 12, 8, 13, 9, 14, 15, 7, 10, 6, 11, 5, 4, 3, 2, 1)
AHEAD = (12, 8, 13, 9, 14)

epsilon = 1e-06
MIB = 1 << 20


def shifted(block, axis, distance):
    devices = range(lax.axis_size(axis))
    route = [(i - distance, i) for i in devices if i - distance in devices]
    return lax.ppermute(block, axis, route)


def dot(a, b):
    return jnp.dot(a, b, preferred_element_type=jnp.float32)


def dot_nt(a, b):
    return lax.dot_general(a, b, (((1,), (1,)), ((), ())), preferred_element_type=jnp.float32)


def dot_tn(a, b):
    return lax.dot_general(a, b, (((0,), (0,)), ((), ())), preferred_element_type=jnp.float32)


def head_lanes(head):
    return slice(head * HD, (head + 1) * HD)


def mixer_kernel(has_state, *refs):
    if has_state:
        state_ref, *refs = refs
    tokens_ref, residual_ref, wq_ref, wk_ref, wv_ref, gain_ref, out_ref = refs
    tokens = tokens_ref[...]
    rows = tokens.shape[0]
    block = 2 * SPAN
    query = dot(tokens, wq_ref[...]).astype(jnp.bfloat16)
    key = dot(tokens, wk_ref[...]).astype(jnp.bfloat16)
    value = dot(tokens, wv_ref[...]).astype(jnp.bfloat16)
    units = [(head, start) for head in range(PAIR) for start in range(0, rows, block)]

    def scores_of(unit):
        head, start = unit
        lanes = head_lanes(head)
        return dot_nt(query[start : start + block, lanes], key[: start + block, lanes])

    scores = scores_of(units[0])
    for index, (head, start) in enumerate(units):
        upcoming = scores_of(units[index + 1]) if index + 1 < len(units) else None
        lanes = head_lanes(head)
        here = slice(start, start + block)
        causal = lax.broadcasted_iota(jnp.int32, scores.shape, 1) <= start + (
            lax.broadcasted_iota(jnp.int32, scores.shape, 0)
        )
        local = jnp.where(causal, scores, 0.0).astype(jnp.bfloat16)
        out = dot(local, value[: start + block, lanes])
        if has_state:
            out += dot(query[here, lanes], state_ref[head].astype(jnp.bfloat16))
        mean_square = jnp.mean(out * out, axis=-1, keepdims=True)
        gain = gain_ref[:, lanes].astype(jnp.float32)
        normed = out * lax.rsqrt(mean_square + epsilon) * gain
        residual = residual_ref[here, lanes].astype(jnp.float32)
        out_ref[here, lanes] = (residual + normed).astype(jnp.bfloat16)
        scores = upcoming


def lead_kernel(has_state, *refs):
    *refs, hidden_ref = refs
    tiles = refs[-len(AHEAD) :]
    mixer_kernel(has_state, *refs[: -len(AHEAD)], hidden_ref)
    size = hidden_ref.shape[0] // SB
    place = lax.rem(lax.axis_index("tm"), SB)
    for apart, tile in zip(AHEAD, tiles):
        start = pl.multiple_of((place ^ apart) * size, size)
        tile[...] = hidden_ref[pl.ds(start, size), :]


def rest_kernel(has_state, lead_ref, *refs):
    *refs, scratch = refs
    tiles = refs[-len(APART) :]
    step = pl.program_id(0)
    mixer_kernel(has_state, *refs[: -len(APART)], scratch.at[step])
    size = scratch.shape[1] // SB
    place = lax.rem(lax.axis_index("tm"), SB)

    @pl.when(step == pl.num_programs(0) - 1)
    def _():
        for apart, tile in zip(APART, tiles):
            rows = pl.ds(pl.multiple_of((place ^ apart) * size, size), size)
            parts = [scratch[j, rows, :] for j in range(scratch.shape[0])]
            if apart not in AHEAD:
                parts.insert(0, lead_ref[rows, :])
            tile[...] = jnp.concatenate(parts, axis=1)


def mixer(first, tokens, w_lin, gain_lin, state, lead=None):
    rows, width = tokens.shape
    columns = PAIR * HD
    steps = HEADS // PAIR
    skip = first // PAIR
    half = width // 2
    size = rows // SB
    in_specs = [
        pl.BlockSpec((rows, width), lambda c: (0, 0)),
        pl.BlockSpec((rows, columns), lambda c: (0, skip + c)),
        pl.BlockSpec((width, columns), lambda c: (0, skip + c)),
        pl.BlockSpec((width, columns), lambda c: (0, steps + skip + c)),
        pl.BlockSpec((width, columns), lambda c: (0, 2 * steps + skip + c)),
        pl.BlockSpec((1, columns), lambda c: (0, skip + c)),
    ]
    operands = [tokens, tokens, w_lin, w_lin, w_lin, gain_lin]
    if state is not None:
        operands.insert(0, state)
        in_specs.insert(0, pl.BlockSpec((PAIR, HD, HD), lambda c: (skip + c, 0, 0)))
    if lead is None:
        kernel = lead_kernel
        out_specs = [pl.BlockSpec((size, columns), lambda c: (0, c)) for _ in AHEAD]
        out_specs.append(pl.BlockSpec((rows, columns), lambda c: (0, c)))
        out_shape = [jax.ShapeDtypeStruct((size, half), jnp.bfloat16) for _ in AHEAD]
        out_shape.append(jax.ShapeDtypeStruct((rows, half), jnp.bfloat16))
        scratch = []
    else:
        kernel = rest_kernel
        operands.insert(0, lead)
        in_specs.insert(0, pl.BlockSpec((rows, half), lambda c: (0, 0)))
        widths = [half if apart in AHEAD else width for apart in APART]
        out_specs = [pl.BlockSpec((size, wide), lambda c: (0, 0)) for wide in widths]
        out_shape = [jax.ShapeDtypeStruct((size, wide), jnp.bfloat16) for wide in widths]
        scratch = [pltpu.VMEM((steps // 2, rows, columns), jnp.bfloat16)]
    return pl.pallas_call(
        functools.partial(kernel, state is not None),
        grid=(steps // 2,),
        in_specs=in_specs,
        out_specs=out_specs,
        out_shape=out_shape,
        scratch_shapes=scratch,
        compiler_params=pltpu.CompilerParams(vmem_limit_bytes=56 * MIB),
        cost_estimate=pl.CostEstimate(
            flops=2 * rows * width * 3 * half + 8 * rows * SPAN * half,
            bytes_accessed=2 * (3 * width * half + 2 * rows * width),
            transcendentals=rows * HEADS // 2,
        ),
        name="mixer",
    )(*operands)


def incoming_state(tokens, w_lin, time_ranges):
    rows, width = tokens.shape
    packed = dot(tokens, w_lin[:, width:]).astype(jnp.bfloat16).reshape(rows, 2, HEADS, HD)
    block_total = jnp.einsum(
        "nhd,nhe->hde", packed[:, 0], packed[:, 1], preferred_element_type=jnp.float32
    )
    within = lax.axis_index("tm") // SB

    def advance_hop(turn_index, running_total):
        moved = shifted(running_total + block_total, "tm", SB)
        return jnp.where(within > 0, moved, 0.0)

    return lax.fori_loop(0, time_ranges - 1, advance_hop, jnp.zeros_like(block_total))


def pairs_kernel(gain_ref, w_ref, *refs):
    *parts, normed_ref, pairs_ref = refs
    parts = iter(parts)
    rows = []
    for apart in APART:
        tile = next(parts)[...]
        if apart in AHEAD:
            tile = jnp.concatenate([tile, next(parts)[...]], axis=1)
        rows.append(tile)
    widened = jnp.concatenate(rows, axis=0).astype(jnp.float32)
    mean_square = jnp.mean(widened * widened, axis=-1, keepdims=True)
    normed = (
        widened * lax.rsqrt(mean_square + epsilon) * gain_ref[...].astype(jnp.float32).reshape(1, -1)
    ).astype(jnp.bfloat16)
    normed_ref[...] = normed
    pairs_ref[...] = dot(normed, w_ref[...]).astype(jnp.bfloat16)


def make_pairs(parts, gain, w_kv):
    width, wide = w_kv.shape
    rows = sum(part.shape[0] * part.shape[1] for part in parts) // width
    return pl.pallas_call(
        pairs_kernel,
        out_shape=[
            jax.ShapeDtypeStruct((rows, width), jnp.bfloat16),
            jax.ShapeDtypeStruct((rows, wide), jnp.bfloat16),
        ],
        compiler_params=pltpu.CompilerParams(vmem_limit_bytes=16 * MIB),
        cost_estimate=pl.CostEstimate(
            flops=2 * rows * width * wide,
            bytes_accessed=2 * (2 * rows * width + width * wide + rows * wide),
            transcendentals=rows,
        ),
        name="pairs",
    )(gain, w_kv, *parts)


SCORE_SCALE = math.log2(math.e) / math.sqrt(HD)


def with_ones(value):
    return jnp.concatenate([value, jnp.ones_like(value)], axis=1)


def own_kernel(normed_ref, w_ref, key_ref, value_ref, query_ref, partial_ref, log_ref):
    query = dot(normed_ref[...], w_ref[...]).astype(jnp.bfloat16)
    query_ref[...] = query
    key = key_ref[...]
    value = with_ones(value_ref[...])
    heads = query.shape[1] // HD
    scores = dot_nt(query[:, head_lanes(0)], key)
    for head in range(heads):
        upcoming = dot_nt(query[:, head_lanes(head + 1)], key) if head + 1 < heads else None
        largest = jnp.max(scores, axis=-1, keepdims=True)
        raised = jnp.exp2((scores - largest) * SCORE_SCALE).astype(jnp.bfloat16)
        summed = dot(raised, value)
        total = summed[:, HD:]
        partial_ref[:, head_lanes(head)] = summed[:, :HD] / total
        log_ref[:, head_lanes(head)] = largest * SCORE_SCALE + jnp.log2(total)
        scores = upcoming


def own_frame(normed, w_query, pairs):
    rows, width = normed.shape
    group = HEADS // KVH
    columns = group * HD
    return pl.pallas_call(
        own_kernel,
        grid=(KVH,),
        in_specs=[
            pl.BlockSpec((rows, width), lambda c: (0, 0)),
            pl.BlockSpec((width, columns), lambda c: (0, c)),
            pl.BlockSpec((rows, HD), lambda c: (0, c)),
            pl.BlockSpec((rows, HD), lambda c: (0, KVH + c)),
        ],
        out_specs=[
            pl.BlockSpec((rows, columns), lambda c: (0, c)),
            pl.BlockSpec((rows, columns), lambda c: (0, c)),
            pl.BlockSpec((rows, columns), lambda c: (0, c)),
        ],
        out_shape=[
            jax.ShapeDtypeStruct((rows, width), jnp.bfloat16),
            jax.ShapeDtypeStruct((rows, width), jnp.float32),
            jax.ShapeDtypeStruct((rows, width), jnp.float32),
        ],
        compiler_params=pltpu.CompilerParams(vmem_limit_bytes=32 * MIB),
        cost_estimate=pl.CostEstimate(
            flops=2 * rows * width * width + 4 * rows * rows * width,
            bytes_accessed=2 * width * width + 8 * rows * width,
            transcendentals=rows * rows * HEADS,
        ),
        name="own_frame",
    )(normed, w_query, pairs, pairs)


def earlier_kernel(query_ref, key_ref, value_ref, partial_ref, log_ref, out_ref):
    rows = query_ref.shape[0]
    heads = query_ref.shape[1] // HD
    key = key_ref[...]
    value = with_ones(value_ref[...])
    index = lax.axis_index("tm")
    barred = jnp.where(index > 0, 0.0, -jnp.inf)
    place = lax.rem(index, SB)
    size = rows // SB
    scores = dot_nt(query_ref[:, head_lanes(0)], key)
    for head in range(heads):
        lanes = head_lanes(head)
        upcoming = dot_nt(query_ref[:, head_lanes(head + 1)], key) if head + 1 < heads else None
        own = log_ref[:, lanes]
        here = jnp.max(scores, axis=-1, keepdims=True) * SCORE_SCALE + barred
        largest = jnp.maximum(jnp.broadcast_to(here, own.shape), own)
        below = jnp.concatenate([largest - barred] * (rows // HD), axis=1)
        raised = jnp.exp2(scores * SCORE_SCALE - below).astype(jnp.bfloat16)
        summed = dot(raised, value)
        share = jnp.exp2(own - largest)
        mixed = (
            (partial_ref[:, lanes] * share + summed[:, :HD]) / (share + summed[:, HD:])
        ).astype(jnp.bfloat16)
        for slot, apart in enumerate(APART):
            start = pl.multiple_of((place ^ apart) * size, size)
            out_ref[pl.ds(start, size), lanes] = mixed[slot * size : (slot + 1) * size]
        scores = upcoming


def earlier_frame(query, earlier_pairs, partial, log_total):
    rows, width = query.shape
    group = HEADS // KVH
    columns = group * HD
    return pl.pallas_call(
        earlier_kernel,
        grid=(KVH,),
        in_specs=[
            pl.BlockSpec((rows, columns), lambda c: (0, c)),
            pl.BlockSpec((rows, HD), lambda c: (0, c)),
            pl.BlockSpec((rows, HD), lambda c: (0, KVH + c)),
            pl.BlockSpec((rows, columns), lambda c: (0, c)),
            pl.BlockSpec((rows, columns), lambda c: (0, c)),
        ],
        out_specs=pl.BlockSpec((rows, columns), lambda c: (0, c)),
        out_shape=jax.ShapeDtypeStruct((rows, width), jnp.bfloat16),
        compiler_params=pltpu.CompilerParams(vmem_limit_bytes=32 * MIB),
        cost_estimate=pl.CostEstimate(
            flops=4 * rows * rows * width,
            bytes_accessed=10 * rows * width,
            transcendentals=rows * rows * HEADS,
        ),
        name="earlier_frame",
    )(query, earlier_pairs, earlier_pairs, partial, log_total)


def swap(tile, apart):
    devices = lax.axis_size("tm")
    route = [(i, i - i % SB + (i % SB ^ apart)) for i in range(devices)]
    return lax.ppermute(tile, "tm", route)


def body(space_time, w_lin, gain_lin, w_query, w_kv, frame_attention_gain):
    tokens = space_time[0]
    time_ranges = lax.axis_size("tm") // SB
    state = incoming_state(tokens, w_lin, time_ranges) if time_ranges > 1 else None
    gain_lin = gain_lin.reshape(1, -1)
    *ahead, lead = mixer(0, tokens, w_lin, gain_lin, state)
    ahead = {apart: swap(tile, apart) for apart, tile in zip(AHEAD, ahead)}
    tiles = mixer(HEADS // 2, tokens, w_lin, gain_lin, state, lead)
    parts = []
    for apart, tile in zip(APART, tiles):
        if apart in ahead:
            parts.append(ahead[apart])
        parts.append(swap(tile, apart) if apart else tile)
    normed, pairs = make_pairs(parts, frame_attention_gain, w_kv)
    earlier_pairs = shifted(pairs, "tm", 1)
    query, partial, log_total = own_frame(normed, w_query, pairs)
    attended = earlier_frame(query, earlier_pairs, partial, log_total)
    return attended[None]


def solution(mesh):
    placed = (P(("groups", "tm"), None, None), P(), P(), P(), P(), P())
    return jax.shard_map(
        body, mesh=mesh, in_specs=placed, out_specs=P(("groups", "tm"), None, None), check_vma=False
    )
```

```python
import functools
import math

import jax
import jax.numpy as jnp
from jax import lax
from jax.experimental import pallas as pl
from jax.experimental.pallas import tpu as pltpu
from jax.sharding import PartitionSpec as P

HEADS = 8
HD = 128
KVH = 2
SB = 16
SPAN = 128
PAIR = 2

APART = (0, 15, 14, 13, 6, 12, 5, 11, 4, 10, 3, 9, 2, 8, 1, 7)

epsilon = 1e-06
MIB = 1 << 20


def shifted(block, axis, distance):
    devices = range(lax.axis_size(axis))
    route = [(i - distance, i) for i in devices if i - distance in devices]
    return lax.ppermute(block, axis, route)


def dot(a, b):
    return jnp.dot(a, b, preferred_element_type=jnp.float32)


def dot_nt(a, b):
    return lax.dot_general(a, b, (((1,), (1,)), ((), ())), preferred_element_type=jnp.float32)


def dot_tn(a, b):
    return lax.dot_general(a, b, (((0,), (0,)), ((), ())), preferred_element_type=jnp.float32)


def head_lanes(head):
    return slice(head * HD, (head + 1) * HD)


def causal_mask():
    shape = (SPAN, SPAN)
    return lax.broadcasted_iota(jnp.int32, shape, 0) >= lax.broadcasted_iota(jnp.int32, shape, 1)


def mix_heads(query, key, value, states, turned):
    rows = query.shape[0]
    causal = causal_mask()
    spans = [slice(start, start + SPAN) for start in range(0, rows, SPAN)]
    heads = range(query.shape[1] // HD)
    local, before, mixed = {}, {}, {}
    turns = {}
    for head in heads:
        lanes = head_lanes(head)
        if turned:
            turns[head] = key[:, lanes].T
        for span, here in enumerate(spans):
            if turned:
                scores = dot(query[here, lanes], turns[head][:, here])
            else:
                scores = dot_nt(query[here, lanes], key[here, lanes])
            local[head, span] = jnp.where(causal, scores, 0.0).astype(jnp.bfloat16)
    for head in heads:
        lanes = head_lanes(head)
        state = states[head]
        for span, here in enumerate(spans):
            before[head, span] = state
            if span + 1 < len(spans):
                if turned:
                    update = dot(turns[head][:, here], value[here, lanes])
                else:
                    update = dot_tn(key[here, lanes], value[here, lanes])
                state = update if state is None else state + update
    for head in heads:
        lanes = head_lanes(head)
        for span, here in enumerate(spans):
            if before[head, span] is None:
                mixed[head, span] = dot(local[head, span], value[here, lanes])
            else:
                mixed[head, span] = dot(
                    jnp.concatenate([query[here, lanes], local[head, span]], axis=1),
                    jnp.concatenate(
                        [before[head, span].astype(jnp.bfloat16), value[here, lanes]], axis=0
                    ),
                )
    return [(head, here, mixed[head, span]) for head in heads for span, here in enumerate(spans)]


def mixer_kernel(first, has_state, turned, *refs):
    if has_state:
        state_ref, *refs = refs
    tokens_ref, residual_ref, wq_ref, wk_ref, wv_ref, gain_ref, out_ref = refs
    tokens = tokens_ref[...]
    query = dot(tokens, wq_ref[...]).astype(jnp.bfloat16)
    key = dot(tokens, wk_ref[...]).astype(jnp.bfloat16)
    value = dot(tokens, wv_ref[...]).astype(jnp.bfloat16)
    states = [state_ref[head] if has_state else None for head in range(PAIR)]
    start = pl.multiple_of(first * HD + pl.program_id(0) * PAIR * HD, PAIR * HD)
    gains = gain_ref[pl.ds(start, PAIR * HD)].astype(jnp.float32).reshape(1, PAIR * HD)
    for head, here, out in mix_heads(query, key, value, states, turned):
        lanes = head_lanes(head)
        mean_square = jnp.mean(out * out, axis=-1, keepdims=True)
        normed = out * lax.rsqrt(mean_square + epsilon) * gains[:, lanes]
        residual = residual_ref[here, lanes].astype(jnp.float32)
        out_ref[here, lanes] = (residual + normed).astype(jnp.bfloat16)


def last_kernel(first, has_state, turned, lead_ref, *refs):
    *refs, scratch = refs
    tiles = refs[-len(APART) :]
    step = pl.program_id(0)
    mixer_kernel(first, has_state, turned, *refs[: -len(APART)], scratch.at[step])
    size = scratch.shape[1] // SB
    place = lax.rem(lax.axis_index("tm"), SB)

    @pl.when(step == pl.num_programs(0) - 1)
    def _():
        for apart, tile in zip(APART, tiles):
            rows = pl.ds(pl.multiple_of((place ^ apart) * size, size), size)
            parts = [lead_ref[rows, :]] + [scratch[j, rows, :] for j in range(scratch.shape[0])]
            tile[...] = jnp.concatenate(parts, axis=1)


def mixer(first, tokens, w_lin, gain_lin, state, lead=None):
    rows, width = tokens.shape
    columns = PAIR * HD
    steps = HEADS // PAIR
    skip = first // PAIR
    half = width // 2
    size = rows // SB
    in_specs = [
        pl.BlockSpec((rows, width), lambda c: (0, 0)),
        pl.BlockSpec((rows, columns), lambda c: (0, skip + c)),
        pl.BlockSpec((width, columns), lambda c: (0, skip + c)),
        pl.BlockSpec((width, columns), lambda c: (0, steps + skip + c)),
        pl.BlockSpec((width, columns), lambda c: (0, 2 * steps + skip + c)),
        pl.BlockSpec(memory_space=pltpu.VMEM),
    ]
    operands = [tokens, tokens, w_lin, w_lin, w_lin, gain_lin]
    if state is not None:
        operands.insert(0, state)
        in_specs.insert(0, pl.BlockSpec((PAIR, HD, HD), lambda c: (skip + c, 0, 0)))
    if lead is None:
        kernel = functools.partial(mixer_kernel, first, state is not None, True)
        out_specs = pl.BlockSpec((rows, columns), lambda c: (0, c))
        out_shape = jax.ShapeDtypeStruct((rows, half), jnp.bfloat16)
        scratch = []
    else:
        kernel = functools.partial(last_kernel, first, state is not None, False)
        operands.insert(0, lead)
        in_specs.insert(0, pl.BlockSpec((rows, half), lambda c: (0, 0)))
        out_specs = [pl.BlockSpec((size, width), lambda c: (0, 0)) for _ in APART]
        out_shape = [jax.ShapeDtypeStruct((size, width), jnp.bfloat16) for _ in APART]
        scratch = [pltpu.VMEM((steps // 2, rows, columns), jnp.bfloat16)]
    return pl.pallas_call(
        kernel,
        grid=(steps // 2,),
        in_specs=in_specs,
        out_specs=out_specs,
        out_shape=out_shape,
        scratch_shapes=scratch,
        compiler_params=pltpu.CompilerParams(vmem_limit_bytes=56 * MIB),
        cost_estimate=pl.CostEstimate(
            flops=2 * rows * width * 3 * half + 8 * rows * SPAN * half,
            bytes_accessed=2 * (3 * width * half + 2 * rows * width),
            transcendentals=rows * HEADS // 2,
        ),
        name="mixer",
    )(*operands)


def incoming_state(tokens, w_lin, time_ranges):
    rows, width = tokens.shape
    packed = dot(tokens, w_lin[:, width:]).astype(jnp.bfloat16).reshape(rows, 2, HEADS, HD)
    block_total = jnp.einsum(
        "nhd,nhe->hde", packed[:, 0], packed[:, 1], preferred_element_type=jnp.float32
    )
    within = lax.axis_index("tm") // SB

    def advance_hop(turn_index, running_total):
        moved = shifted(running_total + block_total, "tm", SB)
        return jnp.where(within > 0, moved, 0.0)

    return lax.fori_loop(0, time_ranges - 1, advance_hop, jnp.zeros_like(block_total))


def pairs_kernel(gain_ref, w_ref, kept_ref, *refs):
    *tiles, normed_ref, first_ref, second_ref, kept, arrived = refs
    copy = pltpu.make_async_copy(kept_ref, kept, arrived)
    copy.start()
    gain = gain_ref[...].astype(jnp.float32).reshape(1, -1)
    w_kv = w_ref[...]

    def norm(rows):
        widened = rows.astype(jnp.float32)
        mean_square = jnp.mean(widened * widened, axis=-1, keepdims=True)
        return (widened * lax.rsqrt(mean_square + epsilon) * gain).astype(jnp.bfloat16)

    def give(normed, start, out_ref):
        rows = normed.shape[0]
        pairs = dot(normed, w_kv).astype(jnp.bfloat16)
        normed_ref[start : start + rows] = normed
        out_ref[: KVH * HD] = pairs[:, : KVH * HD].T
        out_ref[KVH * HD :] = pairs[:, KVH * HD :]

    half = len(APART) // 2
    normed = norm(jnp.concatenate([tile[...] for tile in tiles[half - 1 :]], axis=0))
    give(normed, normed.shape[0], second_ref)
    copy.wait()
    normed = norm(jnp.concatenate([kept[...]] + [tile[...] for tile in tiles[: half - 1]], axis=0))
    give(normed, 0, first_ref)


def make_pairs(tiles, gain, w_kv):
    size, width = tiles[0].shape
    wide = w_kv.shape[1]
    rows = size * len(tiles)
    vmem = pl.BlockSpec(memory_space=pltpu.VMEM)
    return pl.pallas_call(
        pairs_kernel,
        in_specs=[vmem, vmem, pl.BlockSpec(memory_space=pltpu.HBM)] + [vmem] * (len(tiles) - 1),
        out_shape=[jax.ShapeDtypeStruct((rows, width), jnp.bfloat16)]
        + [jax.ShapeDtypeStruct((wide, rows // 2), jnp.bfloat16)] * 2,
        scratch_shapes=[pltpu.VMEM((size, width), jnp.bfloat16), pltpu.SemaphoreType.DMA],
        compiler_params=pltpu.CompilerParams(vmem_limit_bytes=40 * MIB),
        cost_estimate=pl.CostEstimate(
            flops=2 * rows * width * wide,
            bytes_accessed=2 * (2 * rows * width + width * wide + rows * wide),
            transcendentals=rows,
        ),
        name="pairs",
    )(gain, w_kv, *tiles)


SCORE_SCALE = math.log2(math.e) / math.sqrt(HD)
GROUP = HEADS // KVH


def keys_and_values(refs):
    both = []
    for head in range(KVH):
        keys = [ref[head_lanes(head)] for ref in refs]
        values = [ref[KVH * HD :, head_lanes(head)] for ref in refs]
        key = keys[0] if len(keys) == 1 else jnp.concatenate(keys, axis=1)
        value = values[0] if len(values) == 1 else jnp.concatenate(values, axis=0)
        both.append((key, jnp.concatenate([value, jnp.ones_like(value)], axis=1)))
    return both


def own_kernel(normed_ref, w_ref, first_ref, second_ref, query_ref, partial_ref, log_ref):
    both = keys_and_values([first_ref, second_ref])
    columns = GROUP * HD

    def project(group):
        lanes = slice(group * columns, (group + 1) * columns)
        query = dot(normed_ref[...], w_ref[:, lanes]).astype(jnp.bfloat16)
        query_ref[:, lanes] = query
        return query

    queries = {0: project(0)}

    def scores_of(head):
        group = head // GROUP
        return dot(queries[group][:, head_lanes(head % GROUP)], both[group][0])

    scores = scores_of(0)
    for head in range(HEADS):
        if head % GROUP == 0 and head + GROUP < HEADS:
            queries[head // GROUP + 1] = project(head // GROUP + 1)
        upcoming = scores_of(head + 1) if head + 1 < HEADS else None
        largest = jnp.max(scores, axis=-1, keepdims=True)
        raised = jnp.exp2((scores - largest) * SCORE_SCALE).astype(jnp.bfloat16)
        summed = dot(raised, both[head // GROUP][1])
        total = summed[:, HD:]
        partial_ref[:, head_lanes(head)] = summed[:, :HD] / total
        log_ref[:, head_lanes(head)] = largest * SCORE_SCALE + jnp.log2(total)
        scores = upcoming


def own_frame(normed, w_query, first, second):
    rows, width = normed.shape
    return pl.pallas_call(
        own_kernel,
        out_shape=[
            jax.ShapeDtypeStruct((rows, width), jnp.bfloat16),
            jax.ShapeDtypeStruct((rows, width), jnp.float32),
            jax.ShapeDtypeStruct((rows, width), jnp.float32),
        ],
        compiler_params=pltpu.CompilerParams(vmem_limit_bytes=32 * MIB),
        cost_estimate=pl.CostEstimate(
            flops=2 * rows * width * width + 4 * rows * rows * width,
            bytes_accessed=2 * width * width + 8 * rows * width,
            transcendentals=rows * rows * HEADS,
        ),
        name="own_frame",
    )(normed, w_query, first, second)


def earlier_kernel(last, query_ref, pairs_ref, partial_ref, log_ref, *outs):
    rows = query_ref.shape[0]
    both = keys_and_values([pairs_ref])
    index = lax.axis_index("tm")
    barred = jnp.where(index > 0, 0.0, -jnp.inf)
    place = lax.rem(index, SB)
    size = rows // SB

    def scores_of(head):
        return dot(query_ref[:, head_lanes(head)], both[head // GROUP][0])

    scores = scores_of(0)
    for head in range(HEADS):
        lanes = head_lanes(head)
        upcoming = scores_of(head + 1) if head + 1 < HEADS else None
        before = log_ref[:, lanes]
        here = jnp.max(scores, axis=-1, keepdims=True) * SCORE_SCALE + barred
        largest = jnp.maximum(jnp.broadcast_to(here, before.shape), before)
        below = jnp.concatenate([largest - barred] * (scores.shape[1] // HD), axis=1)
        raised = jnp.exp2(scores * SCORE_SCALE - below).astype(jnp.bfloat16)
        summed = dot(raised, both[head // GROUP][1])
        share = jnp.exp2(before - largest)
        total = share + summed[:, HD:]
        mixed = (partial_ref[:, lanes] * share + summed[:, :HD]) / total
        if last:
            mixed = mixed.astype(jnp.bfloat16)
            for slot, apart in enumerate(APART):
                start = pl.multiple_of((place ^ apart) * size, size)
                outs[0][pl.ds(start, size), lanes] = mixed[slot * size : (slot + 1) * size]
        else:
            outs[0][:, lanes] = mixed
            outs[1][:, lanes] = largest + jnp.log2(total)
        scores = upcoming


def earlier_frame(last, query, pairs, partial, log_total):
    rows, width = query.shape
    if last:
        out_shape = jax.ShapeDtypeStruct((rows, width), jnp.bfloat16)
    else:
        out_shape = [jax.ShapeDtypeStruct((rows, width), jnp.float32)] * 2
    return pl.pallas_call(
        functools.partial(earlier_kernel, last),
        out_shape=out_shape,
        compiler_params=pltpu.CompilerParams(vmem_limit_bytes=32 * MIB),
        cost_estimate=pl.CostEstimate(
            flops=4 * rows * pairs.shape[1] * width,
            bytes_accessed=10 * rows * width,
            transcendentals=rows * pairs.shape[1] * HEADS,
        ),
        name="earlier_frame",
    )(query, pairs, partial, log_total)


def swap(tile, apart):
    devices = lax.axis_size("tm")
    route = [(i, i - i % SB + (i % SB ^ apart)) for i in range(devices)]
    return lax.ppermute(tile, "tm", route)


def body(space_time, w_lin, gain_lin, w_query, w_kv, frame_attention_gain):
    tokens = space_time[0]
    time_ranges = lax.axis_size("tm") // SB
    state = incoming_state(tokens, w_lin, time_ranges) if time_ranges > 1 else None
    lead = mixer(0, tokens, w_lin, gain_lin, state)
    tiles = mixer(HEADS // 2, tokens, w_lin, gain_lin, state, lead)
    tiles = [swap(tile, apart) if apart else tile for apart, tile in zip(APART, tiles)]
    normed, first, second = make_pairs(tiles, frame_attention_gain, w_kv)
    earlier_first = shifted(first, "tm", 1)
    earlier_second = shifted(second, "tm", 1)
    query, partial, log_total = own_frame(normed, w_query, first, second)
    partial, log_total = earlier_frame(False, query, earlier_first, partial, log_total)
    attended = earlier_frame(True, query, earlier_second, partial, log_total)
    return attended[None]


def solution(mesh):
    placed = (P(("groups", "tm"), None, None), P(), P(), P(), P(), P())
    return jax.shard_map(
        body, mesh=mesh, in_specs=placed, out_specs=P(("groups", "tm"), None, None), check_vma=False
    )
```

```python
import functools
import math

import jax
import jax.numpy as jnp
from jax import lax
from jax.experimental import pallas as pl
from jax.experimental.pallas import tpu as pltpu
from jax.sharding import PartitionSpec as P

HEADS = 8
HD = 128
KVH = 2
SB = 16
SPAN = 128
PAIR = 2

APART = (0, 12, 8, 13, 9, 14, 15, 7, 10, 6, 11, 5, 4, 3, 2, 1)
AHEAD = (12, 8, 13, 9, 14)

epsilon = 1e-06
MIB = 1 << 20


def shifted(block, axis, distance):
    devices = range(lax.axis_size(axis))
    route = [(i - distance, i) for i in devices if i - distance in devices]
    return lax.ppermute(block, axis, route)


def dot(a, b):
    return jnp.dot(a, b, preferred_element_type=jnp.float32)


def dot_nt(a, b):
    return lax.dot_general(a, b, (((1,), (1,)), ((), ())), preferred_element_type=jnp.float32)


def dot_tn(a, b):
    return lax.dot_general(a, b, (((0,), (0,)), ((), ())), preferred_element_type=jnp.float32)


def head_lanes(head):
    return slice(head * HD, (head + 1) * HD)


def causal_mask():
    shape = (SPAN, SPAN)
    return lax.broadcasted_iota(jnp.int32, shape, 0) >= lax.broadcasted_iota(jnp.int32, shape, 1)


def mix_heads(query, key, value, states):
    rows = query.shape[0]
    causal = causal_mask()
    spans = [slice(start, start + SPAN) for start in range(0, rows, SPAN)]
    heads = range(query.shape[1] // HD)
    units = [(head, span) for head in heads for span in range(len(spans))]
    local, before, after, mixed = {}, {}, [], []
    for head, span in units:
        lanes, here = head_lanes(head), spans[span]
        scores = dot_nt(query[here, lanes], key[here, lanes])
        local[head, span] = jnp.where(causal, scores, 0.0).astype(jnp.bfloat16)
    for head in heads:
        lanes = head_lanes(head)
        state = states[head]
        for span, here in enumerate(spans):
            before[head, span] = state
            update = dot_tn(key[here, lanes], value[here, lanes])
            state = update if state is None else state + update
        after.append(state)
    for head, span in units:
        lanes, here = head_lanes(head), spans[span]
        if before[head, span] is None:
            out = dot(local[head, span], value[here, lanes])
        else:
            out = dot(
                jnp.concatenate([query[here, lanes], local[head, span]], axis=1),
                jnp.concatenate(
                    [before[head, span].astype(jnp.bfloat16), value[here, lanes]], axis=0
                ),
            )
        mixed.append((head, here, out))
    return mixed, after


def mixer_kernel(first, has_state, *refs):
    if has_state:
        state_ref, *refs = refs
    tokens_ref, residual_ref, wq_ref, wk_ref, wv_ref, gain_ref, out_ref = refs
    rows = tokens_ref.shape[0]
    columns = PAIR * HD
    states = [state_ref[head] if has_state else None for head in range(PAIR)]
    step = pl.program_id(0) * columns
    start = pl.multiple_of(first * HD + step, columns)
    gains = gain_ref[pl.ds(start, columns)].astype(jnp.float32).reshape(1, columns)

    def store(offset, mixed):
        for head, here, out in mixed:
            lanes = head_lanes(head)
            here = slice(offset + here.start, offset + here.stop)
            mean_square = jnp.mean(out * out, axis=-1, keepdims=True)
            normed = out * lax.rsqrt(mean_square + epsilon) * gains[:, lanes]
            residual = residual_ref[here, lanes].astype(jnp.float32)
            out_ref[here, pl.ds(pl.multiple_of(step + head * HD, HD), HD)] = (
                residual + normed
            ).astype(jnp.bfloat16)

    if first == 0:
        weights = jnp.concatenate([wq_ref[...], wk_ref[...], wv_ref[...]], axis=1)
        packed = dot(tokens_ref[...], weights).astype(jnp.bfloat16)
        parts = [packed[:, part * columns : (part + 1) * columns] for part in range(3)]
        store(0, mix_heads(*parts, states)[0])
    else:
        block = rows // 2

        def project(offset):
            tokens = tokens_ref[offset : offset + block]
            return [dot(tokens, w[...]).astype(jnp.bfloat16) for w in (wq_ref, wk_ref, wv_ref)]

        parts = project(0)
        upcoming = project(block)
        mixed, states = mix_heads(*parts, states)
        store(0, mixed)
        mixed, states = mix_heads(*upcoming, states)
        store(block, mixed)


def ahead_kernel(first, has_state, *refs):
    *refs, out_ref = refs
    tiles = refs[-len(AHEAD) :]
    mixer_kernel(first, has_state, *refs[: -len(AHEAD)], out_ref)
    size = out_ref.shape[0] // SB
    place = lax.rem(lax.axis_index("tm"), SB)
    step = pl.multiple_of(pl.program_id(0) * PAIR * HD, PAIR * HD)
    for apart, tile in zip(AHEAD, tiles):
        rows = pl.ds(pl.multiple_of((place ^ apart) * size, size), size)
        tile[...] = out_ref[rows, pl.ds(step, tile.shape[1])]


def mixer(first, tokens, w_lin, gain_lin, state):
    rows, width = tokens.shape
    columns = PAIR * HD
    steps = HEADS // PAIR
    skip = first // PAIR
    half = width // 2
    size = rows // SB
    in_specs = [
        pl.BlockSpec((rows, width), lambda c: (0, 0)),
        pl.BlockSpec((rows, columns), lambda c: (0, skip + c)),
        pl.BlockSpec((width, columns), lambda c: (0, skip + c)),
        pl.BlockSpec((width, columns), lambda c: (0, steps + skip + c)),
        pl.BlockSpec((width, columns), lambda c: (0, 2 * steps + skip + c)),
        pl.BlockSpec(memory_space=pltpu.VMEM),
    ]
    operands = [tokens, tokens, w_lin, w_lin, w_lin, gain_lin]
    if state is not None:
        operands.insert(0, state)
        in_specs.insert(0, pl.BlockSpec((PAIR, HD, HD), lambda c: (skip + c, 0, 0)))
    tiles = len(AHEAD) if first == 0 else 0
    out_specs = [pl.BlockSpec((size, columns), lambda c: (0, c))] * tiles
    out_specs.append(pl.BlockSpec(memory_space=pltpu.VMEM))
    out_shape = [jax.ShapeDtypeStruct((size, half), jnp.bfloat16)] * tiles
    out_shape.append(jax.ShapeDtypeStruct((rows, half), jnp.bfloat16))
    return pl.pallas_call(
        functools.partial(ahead_kernel if tiles else mixer_kernel, first, state is not None),
        grid=(steps // 2,),
        in_specs=in_specs,
        out_specs=out_specs,
        out_shape=out_shape,
        compiler_params=pltpu.CompilerParams(vmem_limit_bytes=(56 if tiles else 24) * MIB),
        cost_estimate=pl.CostEstimate(
            flops=2 * rows * width * 3 * half + 8 * rows * SPAN * half,
            bytes_accessed=2 * (3 * width * half + 2 * rows * width),
            transcendentals=rows * HEADS // 2,
        ),
        name="mixer",
    )(*operands)


def cut_kernel(left_ref, right_ref, *refs):
    tiles = refs[len(AHEAD) :]
    size = left_ref.shape[0] // SB
    place = lax.rem(lax.axis_index("tm"), SB)
    for apart, tile in zip(APART, tiles):
        rows = pl.ds(pl.multiple_of((place ^ apart) * size, size), size)
        if apart in AHEAD:
            tile[...] = right_ref[rows, :]
        else:
            tile[...] = jnp.concatenate([left_ref[rows, :], right_ref[rows, :]], axis=1)


def cut_tiles(left, right, arrived):
    rows, half = left.shape
    size = rows // SB
    vmem = pl.BlockSpec(memory_space=pltpu.VMEM)
    widths = [half if apart in AHEAD else 2 * half for apart in APART]
    return pl.pallas_call(
        cut_kernel,
        in_specs=[vmem, vmem] + [pl.BlockSpec(memory_space=pl.ANY)] * len(arrived),
        out_shape=[jax.ShapeDtypeStruct((size, wide), jnp.bfloat16) for wide in widths],
        compiler_params=pltpu.CompilerParams(vmem_limit_bytes=16 * MIB),
        cost_estimate=pl.CostEstimate(flops=0, bytes_accessed=8 * rows * half, transcendentals=0),
        name="cut",
    )(left, right, *arrived)


def incoming_state(tokens, w_lin, time_ranges):
    rows, width = tokens.shape
    packed = dot(tokens, w_lin[:, width:]).astype(jnp.bfloat16).reshape(rows, 2, HEADS, HD)
    block_total = jnp.einsum(
        "nhd,nhe->hde", packed[:, 0], packed[:, 1], preferred_element_type=jnp.float32
    )
    within = lax.axis_index("tm") // SB

    def advance_hop(turn_index, running_total):
        moved = shifted(running_total + block_total, "tm", SB)
        return jnp.where(within > 0, moved, 0.0)

    return lax.fori_loop(0, time_ranges - 1, advance_hop, jnp.zeros_like(block_total))


def pairs_kernel(gain_ref, w_ref, *refs):
    *parts, normed_ref, first_ref, second_ref = refs
    gain = gain_ref[...].astype(jnp.float32).reshape(1, -1)
    w_kv = w_ref[...]
    parts = iter(parts)
    tiles = []
    for apart in APART:
        tile = next(parts)[...]
        if apart in AHEAD:
            tile = jnp.concatenate([tile, next(parts)[...]], axis=1)
        tiles.append(tile)
    half = len(APART) // 2
    for index, out_ref in enumerate((first_ref, second_ref)):
        widened = jnp.concatenate(tiles[index * half : (index + 1) * half], axis=0)
        widened = widened.astype(jnp.float32)
        mean_square = jnp.mean(widened * widened, axis=-1, keepdims=True)
        normed = (widened * lax.rsqrt(mean_square + epsilon) * gain).astype(jnp.bfloat16)
        rows = normed.shape[0]
        normed_ref[index * rows : (index + 1) * rows] = normed
        pairs = dot(normed, w_kv).astype(jnp.bfloat16)
        out_ref[: KVH * HD] = pairs[:, : KVH * HD].T
        out_ref[KVH * HD :] = pairs[:, KVH * HD :]


def make_pairs(parts, gain, w_kv):
    width, wide = w_kv.shape
    rows = sum(part.size for part in parts) // width
    return pl.pallas_call(
        pairs_kernel,
        out_shape=[jax.ShapeDtypeStruct((rows, width), jnp.bfloat16)]
        + [jax.ShapeDtypeStruct((wide, rows // 2), jnp.bfloat16)] * 2,
        compiler_params=pltpu.CompilerParams(vmem_limit_bytes=16 * MIB),
        cost_estimate=pl.CostEstimate(
            flops=2 * rows * width * wide,
            bytes_accessed=2 * (2 * rows * width + width * wide + rows * wide),
            transcendentals=rows,
        ),
        name="pairs",
    )(gain, w_kv, *parts)


SCORE_SCALE = math.log2(math.e) / math.sqrt(HD)
GROUP = HEADS // KVH


def keys_and_values(refs):
    both = []
    for head in range(KVH):
        keys = [ref[head_lanes(head)] for ref in refs]
        values = [ref[KVH * HD :, head_lanes(head)] for ref in refs]
        key = keys[0] if len(keys) == 1 else jnp.concatenate(keys, axis=1)
        value = values[0] if len(values) == 1 else jnp.concatenate(values, axis=0)
        both.append((key, jnp.concatenate([value, jnp.ones_like(value)], axis=1)))
    return both


def own_kernel(normed_ref, w_ref, first_ref, second_ref, query_ref, partial_ref, log_ref):
    both = keys_and_values([first_ref, second_ref])
    columns = GROUP * HD

    def project(group):
        lanes = slice(group * columns, (group + 1) * columns)
        query = dot(normed_ref[...], w_ref[:, lanes]).astype(jnp.bfloat16)
        query_ref[:, lanes] = query
        return query

    queries = {0: project(0)}

    def scores_of(head):
        group = head // GROUP
        return dot(queries[group][:, head_lanes(head % GROUP)], both[group][0])

    scores = scores_of(0)
    for head in range(HEADS):
        if head % GROUP == 0 and head + GROUP < HEADS:
            queries[head // GROUP + 1] = project(head // GROUP + 1)
        upcoming = scores_of(head + 1) if head + 1 < HEADS else None
        largest = jnp.max(scores, axis=-1, keepdims=True)
        raised = jnp.exp2((scores - largest) * SCORE_SCALE).astype(jnp.bfloat16)
        summed = dot(raised, both[head // GROUP][1])
        total = summed[:, HD:]
        partial_ref[:, head_lanes(head)] = summed[:, :HD] / total
        log_ref[:, head_lanes(head)] = largest * SCORE_SCALE + jnp.log2(total)
        scores = upcoming


def own_frame(normed, w_query, first, second):
    rows, width = normed.shape
    return pl.pallas_call(
        own_kernel,
        out_shape=[
            jax.ShapeDtypeStruct((rows, width), jnp.bfloat16),
            jax.ShapeDtypeStruct((rows, width), jnp.float32),
            jax.ShapeDtypeStruct((rows, width), jnp.float32),
        ],
        compiler_params=pltpu.CompilerParams(vmem_limit_bytes=32 * MIB),
        cost_estimate=pl.CostEstimate(
            flops=2 * rows * width * width + 4 * rows * rows * width,
            bytes_accessed=2 * width * width + 8 * rows * width,
            transcendentals=rows * rows * HEADS,
        ),
        name="own_frame",
    )(normed, w_query, first, second)


def earlier_kernel(last, query_ref, pairs_ref, partial_ref, log_ref, *outs):
    rows = query_ref.shape[0]
    both = keys_and_values([pairs_ref])
    index = lax.axis_index("tm")
    barred = jnp.where(index > 0, 0.0, -jnp.inf)
    place = lax.rem(index, SB)
    size = rows // SB

    def scores_of(head):
        return dot(query_ref[:, head_lanes(head)], both[head // GROUP][0])

    scores = scores_of(0)
    for head in range(HEADS):
        lanes = head_lanes(head)
        upcoming = scores_of(head + 1) if head + 1 < HEADS else None
        before = log_ref[:, lanes]
        here = jnp.max(scores, axis=-1, keepdims=True) * SCORE_SCALE + barred
        largest = jnp.maximum(jnp.broadcast_to(here, before.shape), before)
        below = jnp.concatenate([largest - barred] * (scores.shape[1] // HD), axis=1)
        raised = jnp.exp2(scores * SCORE_SCALE - below).astype(jnp.bfloat16)
        summed = dot(raised, both[head // GROUP][1])
        share = jnp.exp2(before - largest)
        total = share + summed[:, HD:]
        mixed = (partial_ref[:, lanes] * share + summed[:, :HD]) / total
        if last:
            mixed = mixed.astype(jnp.bfloat16)
            for slot, apart in enumerate(APART):
                start = pl.multiple_of((place ^ apart) * size, size)
                outs[0][pl.ds(start, size), lanes] = mixed[slot * size : (slot + 1) * size]
        else:
            outs[0][:, lanes] = mixed
            outs[1][:, lanes] = largest + jnp.log2(total)
        scores = upcoming


def earlier_frame(last, query, pairs, partial, log_total):
    rows, width = query.shape
    if last:
        out_shape = jax.ShapeDtypeStruct((rows, width), jnp.bfloat16)
    else:
        out_shape = [jax.ShapeDtypeStruct((rows, width), jnp.float32)] * 2
    return pl.pallas_call(
        functools.partial(earlier_kernel, last),
        out_shape=out_shape,
        compiler_params=pltpu.CompilerParams(vmem_limit_bytes=32 * MIB),
        cost_estimate=pl.CostEstimate(
            flops=4 * rows * pairs.shape[1] * width,
            bytes_accessed=10 * rows * width,
            transcendentals=rows * pairs.shape[1] * HEADS,
        ),
        name="earlier_frame",
    )(query, pairs, partial, log_total)


def swap(tile, apart):
    devices = lax.axis_size("tm")
    route = [(i, i - i % SB + (i % SB ^ apart)) for i in range(devices)]
    return lax.ppermute(tile, "tm", route)


def body(space_time, w_lin, gain_lin, w_query, w_kv, frame_attention_gain):
    tokens = space_time[0]
    time_ranges = lax.axis_size("tm") // SB
    state = incoming_state(tokens, w_lin, time_ranges) if time_ranges > 1 else None
    *ahead, left = mixer(0, tokens, w_lin, gain_lin, state)
    ahead = {apart: swap(tile, apart) for apart, tile in zip(AHEAD, ahead)}
    (right,) = mixer(HEADS // 2, tokens, w_lin, gain_lin, state)
    parts = []
    for apart, tile in zip(APART, cut_tiles(left, right, list(ahead.values()))):
        if apart in ahead:
            parts.append(ahead[apart])
        parts.append(swap(tile, apart) if apart else tile)
    normed, first, second = make_pairs(parts, frame_attention_gain, w_kv)
    earlier_first = shifted(first, "tm", 1)
    earlier_second = shifted(second, "tm", 1)
    query, partial, log_total = own_frame(normed, w_query, first, second)
    partial, log_total = earlier_frame(False, query, earlier_first, partial, log_total)
    attended = earlier_frame(True, query, earlier_second, partial, log_total)
    return attended[None]


def solution(mesh):
    placed = (P(("groups", "tm"), None, None), P(), P(), P(), P(), P())
    return jax.shard_map(
        body, mesh=mesh, in_specs=placed, out_specs=P(("groups", "tm"), None, None), check_vma=False
    )
```

```python
import functools
import math

import jax
import jax.numpy as jnp
from jax import lax
from jax.experimental import pallas as pl
from jax.experimental.pallas import tpu as pltpu
from jax.sharding import PartitionSpec as P

HEADS = 8
HD = 128
KVH = 2
SB = 16
SPAN = 128
PAIR = 2

epsilon = 1e-06
MIB = 1 << 20


def shifted(block, axis, distance):
    devices = range(lax.axis_size(axis))
    route = [(i - distance, i) for i in devices if i - distance in devices]
    return lax.ppermute(block, axis, route)


def dot(a, b):
    return jnp.dot(a, b, preferred_element_type=jnp.float32)


def dot_nt(a, b):
    return lax.dot_general(a, b, (((1,), (1,)), ((), ())), preferred_element_type=jnp.float32)


def dot_tn(a, b):
    return lax.dot_general(a, b, (((0,), (0,)), ((), ())), preferred_element_type=jnp.float32)


def head_lanes(head):
    return slice(head * HD, (head + 1) * HD)


def causal_mask():
    shape = (SPAN, SPAN)
    return lax.broadcasted_iota(jnp.int32, shape, 0) >= lax.broadcasted_iota(jnp.int32, shape, 1)


def mix_heads(query, key, value, states):
    rows = query.shape[0]
    causal = causal_mask()
    spans = [slice(start, start + SPAN) for start in range(0, rows, SPAN)]
    heads = range(query.shape[1] // HD)
    units = [(head, span) for head in heads for span in range(len(spans))]
    local, before, after, mixed = {}, {}, [], []
    for head, span in units:
        lanes, here = head_lanes(head), spans[span]
        scores = dot_nt(query[here, lanes], key[here, lanes])
        local[head, span] = jnp.where(causal, scores, 0.0).astype(jnp.bfloat16)
    for head in heads:
        lanes = head_lanes(head)
        state = states[head]
        for span, here in enumerate(spans):
            before[head, span] = state
            update = dot_tn(key[here, lanes], value[here, lanes])
            state = update if state is None else state + update
        after.append(state)
    for head, span in units:
        lanes, here = head_lanes(head), spans[span]
        if before[head, span] is None:
            out = dot(local[head, span], value[here, lanes])
        else:
            out = dot(
                jnp.concatenate([query[here, lanes], local[head, span]], axis=1),
                jnp.concatenate(
                    [before[head, span].astype(jnp.bfloat16), value[here, lanes]], axis=0
                ),
            )
        mixed.append((head, here, out))
    return mixed, after


def mixer_kernel(has_state, *refs):
    if has_state:
        state_ref, *refs = refs
    tokens_hbm, w_hbm, gain_ref, out_ref, tokens_ref, weights, tokens_in, weights_in = refs
    rows, width = tokens_ref.shape
    block = rows // 2
    columns = PAIR * HD
    step = pl.program_id(0)
    slot = lax.rem(step, 2)

    def token_copy(index):
        here = slice(index * block, (index + 1) * block)
        return pltpu.make_async_copy(
            tokens_hbm.at[here], tokens_ref.at[here], tokens_in.at[index]
        )

    def weight_copy(pair, to, part):
        start = pl.multiple_of(part * width + pair * columns, columns)
        return pltpu.make_async_copy(
            w_hbm.at[:, pl.ds(start, columns)], weights.at[to, part], weights_in.at[to, part]
        )

    @pl.when(step == 0)
    def _():
        token_copy(0).start()
        weight_copy(0, 0, 0).start()
        weight_copy(0, 0, 1).start()
        token_copy(1).start()
        weight_copy(0, 0, 2).start()

    @pl.when(step + 1 < pl.num_programs(0))
    def _():
        for part in range(3):
            weight_copy(step + 1, 1 - slot, part).start()

    @pl.when(step == 0)
    def _():
        token_copy(0).wait()
        token_copy(1).wait()

    for part in range(3):
        weight_copy(step, slot, part).wait()

    states = [state_ref[head] if has_state else None for head in range(PAIR)]
    start = pl.multiple_of(step * columns, columns)
    gains = gain_ref[pl.ds(start, columns)].astype(jnp.float32).reshape(1, columns)

    def project(offset):
        tokens = tokens_ref[offset : offset + block]
        return [dot(tokens, weights[slot, part]).astype(jnp.bfloat16) for part in range(3)]

    def store(offset, mixed):
        for head, here, out in mixed:
            lanes = head_lanes(head)
            here = slice(offset + here.start, offset + here.stop)
            mean_square = jnp.mean(out * out, axis=-1, keepdims=True)
            normed = out * lax.rsqrt(mean_square + epsilon) * gains[:, lanes]
            there = pl.ds(pl.multiple_of(start + head * HD, HD), HD)
            residual = tokens_ref[here, there].astype(jnp.float32)
            out_ref[here, lanes] = (residual + normed).astype(jnp.bfloat16)

    parts = project(0)
    upcoming = project(block)
    mixed, states = mix_heads(*parts, states)
    store(0, mixed)
    mixed, states = mix_heads(*upcoming, states)
    store(block, mixed)


def mixer(tokens, w_lin, gain_lin, state):
    rows, width = tokens.shape
    columns = PAIR * HD
    in_specs = [
        pl.BlockSpec(memory_space=pl.ANY),
        pl.BlockSpec(memory_space=pl.ANY),
        pl.BlockSpec(memory_space=pltpu.VMEM),
    ]
    operands = [tokens, w_lin, gain_lin]
    if state is not None:
        operands.insert(0, state)
        in_specs.insert(0, pl.BlockSpec((PAIR, HD, HD), lambda c: (c, 0, 0)))
    return pl.pallas_call(
        functools.partial(mixer_kernel, state is not None),
        grid=(HEADS // PAIR,),
        in_specs=in_specs,
        out_specs=pl.BlockSpec((rows, columns), lambda c: (0, c)),
        out_shape=jax.ShapeDtypeStruct((rows, width), jnp.bfloat16),
        scratch_shapes=[
            pltpu.VMEM((rows, width), jnp.bfloat16),
            pltpu.VMEM((2, 3, width, columns), jnp.bfloat16),
            pltpu.SemaphoreType.DMA((2,)),
            pltpu.SemaphoreType.DMA((2, 3)),
        ],
        compiler_params=pltpu.CompilerParams(vmem_limit_bytes=56 * MIB),
        cost_estimate=pl.CostEstimate(
            flops=2 * rows * width * 3 * width + 8 * rows * SPAN * width,
            bytes_accessed=2 * (3 * width * width + 2 * rows * width),
            transcendentals=rows * HEADS,
        ),
        name="mixer",
    )(*operands)


def incoming_state(tokens, w_lin, time_ranges):
    rows, width = tokens.shape
    packed = dot(tokens, w_lin[:, width:]).astype(jnp.bfloat16).reshape(rows, 2, HEADS, HD)
    block_total = jnp.einsum(
        "nhd,nhe->hde", packed[:, 0], packed[:, 1], preferred_element_type=jnp.float32
    )
    within = lax.axis_index("tm") // SB

    def advance_hop(turn_index, running_total):
        moved = shifted(running_total + block_total, "tm", SB)
        return jnp.where(within > 0, moved, 0.0)

    return lax.fori_loop(0, time_ranges - 1, advance_hop, jnp.zeros_like(block_total))


def pairs_kernel(hidden_ref, gain_ref, w_ref, normed_ref, *outs):
    gain = gain_ref[...].astype(jnp.float32).reshape(1, -1)
    widened = hidden_ref[...].astype(jnp.float32)
    mean_square = jnp.mean(widened * widened, axis=-1, keepdims=True)
    normed = (widened * lax.rsqrt(mean_square + epsilon) * gain).astype(jnp.bfloat16)
    normed_ref[...] = normed
    pairs = dot(normed, w_ref[...]).astype(jnp.bfloat16)
    offset = 0
    for out_ref in outs:
        for start in range(0, out_ref.shape[0], HD):
            here = slice(offset + start, offset + start + HD)
            for head in range(KVH):
                out_ref[start : start + HD, head_lanes(head)] = pairs[here, head_lanes(head)].T
        rows = out_ref.shape[0]
        out_ref[:, KVH * HD :] = pairs[offset : offset + rows, KVH * HD :]
        offset += rows


def make_pairs(hidden, gain, w_kv):
    rows, width = hidden.shape
    wide = w_kv.shape[1]
    return pl.pallas_call(
        pairs_kernel,
        out_shape=[
            jax.ShapeDtypeStruct((rows, width), jnp.bfloat16),
            jax.ShapeDtypeStruct((rows - LATE, wide), jnp.bfloat16),
            jax.ShapeDtypeStruct((LATE, wide), jnp.bfloat16),
        ],
        compiler_params=pltpu.CompilerParams(vmem_limit_bytes=16 * MIB),
        cost_estimate=pl.CostEstimate(
            flops=2 * rows * width * wide,
            bytes_accessed=2 * (2 * rows * width + width * wide + rows * wide),
            transcendentals=rows,
        ),
        name="pairs",
    )(hidden, gain, w_kv)


SCORE_SCALE = math.log2(math.e) / math.sqrt(HD)
GROUP = HEADS // KVH
LATE = 128


def keys_and_values(refs):
    both = []
    for head in range(KVH):
        keys, values = [], []
        for ref in refs:
            for start in range(0, ref.shape[0], HD):
                keys.append(ref[start : start + HD, head_lanes(head)])
            values.append(ref[:, head_lanes(KVH + head)])
        key = jnp.concatenate(keys, axis=1)
        value = jnp.concatenate(values, axis=0)
        both.append((key, jnp.concatenate([value, jnp.ones_like(value)], axis=1)))
    return both


def own_kernel(normed_ref, w_ref, first_ref, second_ref, query_ref, partial_ref, log_ref):
    both = keys_and_values([first_ref, second_ref])
    columns = GROUP * HD

    def project(group):
        lanes = slice(group * columns, (group + 1) * columns)
        query = dot(normed_ref[...], w_ref[:, lanes]).astype(jnp.bfloat16)
        query_ref[:, lanes] = query
        return query

    queries = {0: project(0)}

    def scores_of(head):
        group = head // GROUP
        return dot(queries[group][:, head_lanes(head % GROUP)], both[group][0])

    scores = scores_of(0)
    for head in range(HEADS):
        if head % GROUP == 0 and head + GROUP < HEADS:
            queries[head // GROUP + 1] = project(head // GROUP + 1)
        upcoming = scores_of(head + 1) if head + 1 < HEADS else None
        largest = jnp.max(scores, axis=-1, keepdims=True)
        raised = jnp.exp2((scores - largest) * SCORE_SCALE).astype(jnp.bfloat16)
        summed = dot(raised, both[head // GROUP][1])
        total = summed[:, HD:]
        partial_ref[:, head_lanes(head)] = summed[:, :HD] / total
        log_ref[:, head_lanes(head)] = largest * SCORE_SCALE + jnp.log2(total)
        scores = upcoming


def own_frame(normed, w_query, first, second):
    rows, width = normed.shape
    return pl.pallas_call(
        own_kernel,
        out_shape=[
            jax.ShapeDtypeStruct((rows, width), jnp.bfloat16),
            jax.ShapeDtypeStruct((rows, width), jnp.float32),
            jax.ShapeDtypeStruct((rows, width), jnp.float32),
        ],
        compiler_params=pltpu.CompilerParams(vmem_limit_bytes=32 * MIB),
        cost_estimate=pl.CostEstimate(
            flops=2 * rows * width * width + 4 * rows * rows * width,
            bytes_accessed=2 * width * width + 8 * rows * width,
            transcendentals=rows * rows * HEADS,
        ),
        name="own_frame",
    )(normed, w_query, first, second)


def earlier_kernel(last, query_ref, pairs_ref, partial_ref, log_ref, *outs):
    both = keys_and_values([pairs_ref])
    barred = jnp.where(lax.axis_index("tm") > 0, 0.0, -jnp.inf)

    def scores_of(head):
        return dot(query_ref[:, head_lanes(head)], both[head // GROUP][0])

    scores = scores_of(0)
    for head in range(HEADS):
        lanes = head_lanes(head)
        upcoming = scores_of(head + 1) if head + 1 < HEADS else None
        before = log_ref[:, lanes]
        here = jnp.max(scores, axis=-1, keepdims=True) * SCORE_SCALE + barred
        largest = jnp.maximum(jnp.broadcast_to(here, before.shape), before)
        below = jnp.concatenate([largest - barred] * (scores.shape[1] // HD), axis=1)
        raised = jnp.exp2(scores * SCORE_SCALE - below).astype(jnp.bfloat16)
        summed = dot(raised, both[head // GROUP][1])
        share = jnp.exp2(before - largest)
        total = share + summed[:, HD:]
        mixed = (partial_ref[:, lanes] * share + summed[:, :HD]) / total
        if last:
            outs[0][:, lanes] = mixed.astype(jnp.bfloat16)
        else:
            outs[0][:, lanes] = mixed
            outs[1][:, lanes] = largest + jnp.log2(total)
        scores = upcoming


def earlier_frame(last, query, pairs, partial, log_total):
    rows, width = query.shape
    if last:
        out_shape = jax.ShapeDtypeStruct((rows, width), jnp.bfloat16)
    else:
        out_shape = [jax.ShapeDtypeStruct((rows, width), jnp.float32)] * 2
    return pl.pallas_call(
        functools.partial(earlier_kernel, last),
        out_shape=out_shape,
        compiler_params=pltpu.CompilerParams(vmem_limit_bytes=32 * MIB),
        cost_estimate=pl.CostEstimate(
            flops=4 * rows * pairs.shape[0] * width,
            bytes_accessed=10 * rows * width,
            transcendentals=rows * pairs.shape[0] * HEADS,
        ),
        name="earlier_frame",
    )(query, pairs, partial, log_total)


def to_frames(hidden):
    rows, columns = hidden.shape
    teams = [[t * SB + s for s in range(SB)] for t in range(lax.axis_size("tm") // SB)]
    moved = lax.all_to_all(
        hidden.reshape(SB, rows // SB, columns), "tm", 0, 0, axis_index_groups=teams, tiled=True
    )
    return moved.reshape(rows, columns)


def body(space_time, w_lin, gain_lin, w_query, w_kv, frame_attention_gain):
    tokens = space_time[0]
    time_ranges = lax.axis_size("tm") // SB
    state = incoming_state(tokens, w_lin, time_ranges) if time_ranges > 1 else None
    frame_rows = to_frames(mixer(tokens, w_lin, gain_lin, state))
    normed, first, second = make_pairs(frame_rows, frame_attention_gain, w_kv)
    earlier_first = shifted(first, "tm", 1)
    earlier_second = shifted(second, "tm", 1)
    query, partial, log_total = own_frame(normed, w_query, first, second)
    partial, log_total = earlier_frame(False, query, earlier_first, partial, log_total)
    attended = earlier_frame(True, query, earlier_second, partial, log_total)
    return attended[None]


def solution(mesh):
    placed = (P(("groups", "tm"), None, None), P(), P(), P(), P(), P())
    return jax.shard_map(
        body, mesh=mesh, in_specs=placed, out_specs=P(("groups", "tm"), None, None), check_vma=False
    )
```

```python
import functools
import math

import jax
import jax.numpy as jnp
from jax import lax
from jax.experimental import pallas as pl
from jax.experimental.pallas import tpu as pltpu
from jax.sharding import PartitionSpec as P

HEADS = 8
HD = 128
KVH = 2
SB = 16
SPAN = 128
PAIR = 4

epsilon = 1e-06
MIB = 1 << 20


def shifted(block, axis, distance):
    devices = range(lax.axis_size(axis))
    route = [(i - distance, i) for i in devices if i - distance in devices]
    return lax.ppermute(block, axis, route)


def dot(a, b):
    return jnp.dot(a, b, preferred_element_type=jnp.float32)


def dot_nt(a, b):
    return lax.dot_general(a, b, (((1,), (1,)), ((), ())), preferred_element_type=jnp.float32)


def dot_tn(a, b):
    return lax.dot_general(a, b, (((0,), (0,)), ((), ())), preferred_element_type=jnp.float32)


def head_lanes(head):
    return slice(head * HD, (head + 1) * HD)


def causal_mask():
    shape = (SPAN, SPAN)
    return lax.broadcasted_iota(jnp.int32, shape, 0) >= lax.broadcasted_iota(jnp.int32, shape, 1)


def mix_heads(query, key, value, states):
    rows = query.shape[0]
    causal = causal_mask()
    spans = [slice(start, start + SPAN) for start in range(0, rows, SPAN)]
    heads = range(query.shape[1] // HD)
    units = [(head, span) for head in heads for span in range(len(spans))]
    local, before, after, mixed = {}, {}, [], []
    for head, span in units:
        lanes, here = head_lanes(head), spans[span]
        scores = dot_nt(query[here, lanes], key[here, lanes])
        local[head, span] = jnp.where(causal, scores, 0.0).astype(jnp.bfloat16)
    for head in heads:
        lanes = head_lanes(head)
        state = states[head]
        for span, here in enumerate(spans):
            before[head, span] = state
            update = dot_tn(key[here, lanes], value[here, lanes])
            state = update if state is None else state + update
        after.append(state)
    for head, span in units:
        lanes, here = head_lanes(head), spans[span]
        if before[head, span] is None:
            out = dot(local[head, span], value[here, lanes])
        else:
            out = dot(
                jnp.concatenate([query[here, lanes], local[head, span]], axis=1),
                jnp.concatenate(
                    [before[head, span].astype(jnp.bfloat16), value[here, lanes]], axis=0
                ),
            )
        mixed.append((head, here, out))
    return mixed, after


def mixer_kernel(has_state, *refs):
    if has_state:
        state_ref, *refs = refs
    tokens_hbm, w_hbm, gain_ref, out_ref, tokens_ref, weights, tokens_in, weights_in = refs
    rows, width = tokens_ref.shape
    block = rows // 2
    columns = PAIR * HD
    step = pl.program_id(0)
    slot = lax.rem(step, 2)

    def token_copy(index):
        here = slice(index * block, (index + 1) * block)
        return pltpu.make_async_copy(
            tokens_hbm.at[here], tokens_ref.at[here], tokens_in.at[index]
        )

    def weight_copy(pair, to, part):
        start = pl.multiple_of(part * width + pair * columns, columns)
        return pltpu.make_async_copy(
            w_hbm.at[:, pl.ds(start, columns)], weights.at[to, part], weights_in.at[to, part]
        )

    @pl.when(step == 0)
    def _():
        token_copy(0).start()
        weight_copy(0, 0, 0).start()
        weight_copy(0, 0, 1).start()
        token_copy(1).start()
        weight_copy(0, 0, 2).start()

    @pl.when(step + 1 < pl.num_programs(0))
    def _():
        for part in range(3):
            weight_copy(step + 1, 1 - slot, part).start()

    @pl.when(step == 0)
    def _():
        token_copy(0).wait()
        token_copy(1).wait()

    for part in range(3):
        weight_copy(step, slot, part).wait()

    states = [state_ref[head] if has_state else None for head in range(PAIR)]
    start = pl.multiple_of(step * columns, columns)
    gains = gain_ref[pl.ds(start, columns)].astype(jnp.float32).reshape(1, columns)

    def project(offset):
        tokens = tokens_ref[offset : offset + block]
        return [dot(tokens, weights[slot, part]).astype(jnp.bfloat16) for part in range(3)]

    def store(offset, mixed):
        for head, here, out in mixed:
            lanes = head_lanes(head)
            here = slice(offset + here.start, offset + here.stop)
            mean_square = jnp.mean(out * out, axis=-1, keepdims=True)
            normed = out * lax.rsqrt(mean_square + epsilon) * gains[:, lanes]
            there = pl.ds(pl.multiple_of(start + head * HD, HD), HD)
            residual = tokens_ref[here, there].astype(jnp.float32)
            out_ref[here, lanes] = (residual + normed).astype(jnp.bfloat16)

    parts = project(0)
    upcoming = project(block)
    mixed, states = mix_heads(*parts, states)
    store(0, mixed)
    mixed, states = mix_heads(*upcoming, states)
    store(block, mixed)


def mixer(tokens, w_lin, gain_lin, state):
    rows, width = tokens.shape
    columns = PAIR * HD
    in_specs = [
        pl.BlockSpec(memory_space=pl.ANY),
        pl.BlockSpec(memory_space=pl.ANY),
        pl.BlockSpec(memory_space=pltpu.VMEM),
    ]
    operands = [tokens, w_lin, gain_lin]
    if state is not None:
        operands.insert(0, state)
        in_specs.insert(0, pl.BlockSpec((PAIR, HD, HD), lambda c: (c, 0, 0)))
    return pl.pallas_call(
        functools.partial(mixer_kernel, state is not None),
        grid=(HEADS // PAIR,),
        in_specs=in_specs,
        out_specs=pl.BlockSpec((rows, columns), lambda c: (0, c)),
        out_shape=jax.ShapeDtypeStruct((rows, width), jnp.bfloat16),
        scratch_shapes=[
            pltpu.VMEM((rows, width), jnp.bfloat16),
            pltpu.VMEM((2, 3, width, columns), jnp.bfloat16),
            pltpu.SemaphoreType.DMA((2,)),
            pltpu.SemaphoreType.DMA((2, 3)),
        ],
        compiler_params=pltpu.CompilerParams(vmem_limit_bytes=56 * MIB),
        cost_estimate=pl.CostEstimate(
            flops=2 * rows * width * 3 * width + 8 * rows * SPAN * width,
            bytes_accessed=2 * (3 * width * width + 2 * rows * width),
            transcendentals=rows * HEADS,
        ),
        name="mixer",
    )(*operands)


def incoming_state(tokens, w_lin, time_ranges):
    rows, width = tokens.shape
    packed = dot(tokens, w_lin[:, width:]).astype(jnp.bfloat16).reshape(rows, 2, HEADS, HD)
    block_total = jnp.einsum(
        "nhd,nhe->hde", packed[:, 0], packed[:, 1], preferred_element_type=jnp.float32
    )
    within = lax.axis_index("tm") // SB

    def advance_hop(turn_index, running_total):
        moved = shifted(running_total + block_total, "tm", SB)
        return jnp.where(within > 0, moved, 0.0)

    return lax.fori_loop(0, time_ranges - 1, advance_hop, jnp.zeros_like(block_total))


def pairs_kernel(hidden_ref, gain_ref, w_ref, normed_ref, *outs):
    widened = hidden_ref[...].astype(jnp.float32)
    mean_square = jnp.mean(widened * widened, axis=-1, keepdims=True)
    normed = (widened * lax.rsqrt(mean_square + epsilon) * gain_ref[...]).astype(jnp.bfloat16)
    normed_ref[...] = normed
    pairs = dot(normed, w_ref[...]).astype(jnp.bfloat16)
    offset = 0
    for out_ref in outs:
        for start in range(0, out_ref.shape[0], HD):
            here = slice(offset + start, offset + start + HD)
            for head in range(KVH):
                out_ref[start : start + HD, head_lanes(head)] = pairs[here, head_lanes(head)].T
        rows = out_ref.shape[0]
        out_ref[:, KVH * HD :] = pairs[offset : offset + rows, KVH * HD :]
        offset += rows


def make_pairs(hidden, gain, w_kv):
    rows, width = hidden.shape
    wide = w_kv.shape[1]
    return pl.pallas_call(
        pairs_kernel,
        out_shape=[
            jax.ShapeDtypeStruct((rows, width), jnp.bfloat16),
            jax.ShapeDtypeStruct((rows - LATE, wide), jnp.bfloat16),
            jax.ShapeDtypeStruct((LATE, wide), jnp.bfloat16),
        ],
        compiler_params=pltpu.CompilerParams(vmem_limit_bytes=16 * MIB),
        cost_estimate=pl.CostEstimate(
            flops=2 * rows * width * wide,
            bytes_accessed=2 * (2 * rows * width + width * wide + rows * wide),
            transcendentals=rows,
        ),
        name="pairs",
    )(hidden, gain, w_kv)


SCORE_SCALE = math.log2(math.e) / math.sqrt(HD)
GROUP = HEADS // KVH
LATE = 128


def keys_and_values(refs):
    both = []
    for head in range(KVH):
        keys, values = [], []
        for ref in refs:
            for start in range(0, ref.shape[0], HD):
                keys.append(ref[start : start + HD, head_lanes(head)])
            values.append(ref[:, head_lanes(KVH + head)])
        key = jnp.concatenate(keys, axis=1)
        value = jnp.concatenate(values, axis=0)
        both.append((key, jnp.concatenate([value, jnp.ones_like(value)], axis=1)))
    return both


def own_kernel(normed_ref, w_ref, first_ref, last_ref, query_ref, sum_ref, total_ref, top_ref):
    both = keys_and_values([first_ref, last_ref])
    columns = GROUP * HD

    def project(group):
        lanes = slice(group * columns, (group + 1) * columns)
        query = dot(normed_ref[...], w_ref[:, lanes]).astype(jnp.bfloat16)
        query_ref[:, lanes] = query
        return query

    queries = {0: project(0)}

    def scores_of(head):
        group = head // GROUP
        return dot(queries[group][:, head_lanes(head % GROUP)], both[group][0])

    scores = scores_of(0)
    for head in range(HEADS):
        if head % GROUP == 0 and head + GROUP < HEADS:
            queries[head // GROUP + 1] = project(head // GROUP + 1)
        upcoming = scores_of(head + 1) if head + 1 < HEADS else None
        lanes = head_lanes(head)
        largest = jnp.max(scores, axis=-1, keepdims=True)
        raised = jnp.exp2((scores - largest) * SCORE_SCALE).astype(jnp.bfloat16)
        summed = dot(raised, both[head // GROUP][1])
        sum_ref[:, lanes] = summed[:, :HD]
        total_ref[:, lanes] = summed[:, HD:]
        top_ref[:, lanes] = jnp.broadcast_to(largest * SCORE_SCALE, (scores.shape[0], HD))
        scores = upcoming


def own_frame(normed, w_query, first, last):
    rows, width = normed.shape
    return pl.pallas_call(
        own_kernel,
        out_shape=[jax.ShapeDtypeStruct((rows, width), jnp.bfloat16)]
        + [jax.ShapeDtypeStruct((rows, width), jnp.float32)] * 3,
        compiler_params=pltpu.CompilerParams(vmem_limit_bytes=32 * MIB),
        cost_estimate=pl.CostEstimate(
            flops=2 * rows * width * width + 4 * rows * rows * width,
            bytes_accessed=2 * width * width + 8 * rows * width,
            transcendentals=rows * rows * HEADS,
        ),
        name="own_frame",
    )(normed, w_query, first, last)


def earlier_kernel(last, query_ref, pairs_ref, sum_ref, total_ref, top_ref, *refs):
    both = keys_and_values([pairs_ref])
    barred = jnp.where(lax.axis_index("tm") > 0, 0.0, -jnp.inf)

    def scores_of(head):
        return dot(query_ref[:, head_lanes(head)], both[head // GROUP][0])

    copies = []
    scores = scores_of(0)
    for head in range(HEADS):
        lanes = head_lanes(head)
        upcoming = scores_of(head + 1) if head + 1 < HEADS else None
        before = top_ref[:, lanes]
        here = jnp.max(scores, axis=-1, keepdims=True) * SCORE_SCALE + barred
        largest = jnp.maximum(jnp.broadcast_to(here, before.shape), before)
        below = jnp.concatenate([largest - barred] * (scores.shape[1] // HD), axis=1)
        raised = jnp.exp2(scores * SCORE_SCALE - below).astype(jnp.bfloat16)
        summed = dot(raised, both[head // GROUP][1])
        share = jnp.exp2(before - largest)
        mixed = sum_ref[:, lanes] * share + summed[:, :HD]
        total = total_ref[:, lanes] * share + summed[:, HD:]
        if last:
            out_hbm, out_ref, sent = refs
            out_ref[:, lanes] = (mixed / total).astype(jnp.bfloat16)
            if head % 2:
                columns = slice((head - 1) * HD, (head + 1) * HD)
                copies.append(
                    pltpu.make_async_copy(
                        out_ref.at[:, columns], out_hbm.at[:, columns], sent.at[head // 2]
                    )
                )
                copies[-1].start()
        else:
            refs[0][:, lanes] = mixed
            refs[1][:, lanes] = total
            refs[2][:, lanes] = largest
        scores = upcoming
    for copy in copies:
        copy.wait()


def earlier_frame(last, query, pairs, *so_far):
    rows, width = query.shape
    if last:
        extra = dict(
            out_shape=jax.ShapeDtypeStruct((rows, width), jnp.bfloat16),
            out_specs=pl.BlockSpec(memory_space=pl.ANY),
            scratch_shapes=[
                pltpu.VMEM((rows, width), jnp.bfloat16),
                pltpu.SemaphoreType.DMA((HEADS // 2,)),
            ],
        )
    else:
        extra = dict(out_shape=[jax.ShapeDtypeStruct((rows, width), jnp.float32)] * 3)
    return pl.pallas_call(
        functools.partial(earlier_kernel, last),
        compiler_params=pltpu.CompilerParams(vmem_limit_bytes=32 * MIB),
        cost_estimate=pl.CostEstimate(
            flops=4 * rows * pairs.shape[0] * width,
            bytes_accessed=10 * rows * width,
            transcendentals=rows * pairs.shape[0] * HEADS,
        ),
        name="earlier_frame",
        **extra,
    )(query, pairs, *so_far)


def to_frames(hidden):
    rows, columns = hidden.shape
    teams = [[t * SB + s for s in range(SB)] for t in range(lax.axis_size("tm") // SB)]
    moved = lax.all_to_all(
        hidden.reshape(SB, rows // SB, columns), "tm", 0, 0, axis_index_groups=teams, tiled=True
    )
    return moved.reshape(rows, columns)


def body(space_time, w_lin, gain_lin, w_query, w_kv, frame_attention_gain):
    tokens = space_time[0]
    time_ranges = lax.axis_size("tm") // SB
    state = incoming_state(tokens, w_lin, time_ranges) if time_ranges > 1 else None
    hidden = mixer(tokens, w_lin, gain_lin, state)
    hidden, gain = lax.optimization_barrier((hidden, frame_attention_gain))
    frame_rows = to_frames(hidden)
    gain = gain.astype(jnp.float32).reshape(1, -1)
    normed, first, last = make_pairs(frame_rows, gain, w_kv)
    earlier_first = shifted(first, "tm", 1)
    earlier_last = shifted(last, "tm", 1)
    query, *so_far = own_frame(normed, w_query, first, last)
    so_far = earlier_frame(False, query, earlier_first, *so_far)
    attended = earlier_frame(True, query, earlier_last, *so_far)
    return attended[None]


def solution(mesh):
    placed = (P(("groups", "tm"), None, None), P(), P(), P(), P(), P())
    return jax.shard_map(
        body, mesh=mesh, in_specs=placed, out_specs=P(("groups", "tm"), None, None), check_vma=False
    )
```

```python
import functools
import math

import jax
import jax.numpy as jnp
from jax import lax
from jax.experimental import pallas as pl
from jax.experimental.pallas import tpu as pltpu
from jax.sharding import PartitionSpec as P

HEADS = 8
HD = 128
KVH = 2
SB = 16
SPAN = 128
PAIR = 4

epsilon = 1e-06
MIB = 1 << 20


def shifted(block, axis, distance):
    devices = range(lax.axis_size(axis))
    route = [(i - distance, i) for i in devices if i - distance in devices]
    return lax.ppermute(block, axis, route)


def dot(a, b):
    return jnp.dot(a, b, preferred_element_type=jnp.float32)


def dot_nt(a, b):
    return lax.dot_general(a, b, (((1,), (1,)), ((), ())), preferred_element_type=jnp.float32)


def dot_tn(a, b):
    return lax.dot_general(a, b, (((0,), (0,)), ((), ())), preferred_element_type=jnp.float32)


def head_lanes(head):
    return slice(head * HD, (head + 1) * HD)


def causal_mask():
    shape = (SPAN, SPAN)
    return lax.broadcasted_iota(jnp.int32, shape, 0) >= lax.broadcasted_iota(jnp.int32, shape, 1)


def mix_heads(query, key, value, states):
    rows = query.shape[0]
    causal = causal_mask()
    spans = [slice(start, start + SPAN) for start in range(0, rows, SPAN)]
    heads = range(query.shape[1] // HD)
    units = [(head, span) for head in heads for span in range(len(spans))]
    local, before, after, mixed = {}, {}, [], []
    for head, span in units:
        lanes, here = head_lanes(head), spans[span]
        scores = dot_nt(query[here, lanes], key[here, lanes])
        local[head, span] = jnp.where(causal, scores, 0.0).astype(jnp.bfloat16)
    for head in heads:
        lanes = head_lanes(head)
        state = states[head]
        for span, here in enumerate(spans):
            before[head, span] = state
            update = dot_tn(key[here, lanes], value[here, lanes])
            state = update if state is None else state + update
        after.append(state)
    for head, span in units:
        lanes, here = head_lanes(head), spans[span]
        if before[head, span] is None:
            out = dot(local[head, span], value[here, lanes])
        else:
            out = dot(
                jnp.concatenate([query[here, lanes], local[head, span]], axis=1),
                jnp.concatenate(
                    [before[head, span].astype(jnp.bfloat16), value[here, lanes]], axis=0
                ),
            )
        mixed.append((head, here, out))
    return mixed, after


def mixer_kernel(has_state, *refs):
    if has_state:
        state_ref, *refs = refs
    tokens_hbm, w_hbm, gain_ref, out_ref, tokens_ref, weights, tokens_in, weights_in = refs
    rows, width = tokens_ref.shape
    block = rows // 2
    columns = PAIR * HD
    step = pl.program_id(0)
    slot = lax.rem(step, 2)

    def token_copy(index):
        here = slice(index * block, (index + 1) * block)
        return pltpu.make_async_copy(
            tokens_hbm.at[here], tokens_ref.at[here], tokens_in.at[index]
        )

    def weight_copy(pair, to, part):
        start = pl.multiple_of(part * width + pair * columns, columns)
        return pltpu.make_async_copy(
            w_hbm.at[:, pl.ds(start, columns)], weights.at[to, part], weights_in.at[to, part]
        )

    @pl.when(step == 0)
    def _():
        weight_copy(0, 0, 0).start()
        token_copy(0).start()
        token_copy(1).start()
        weight_copy(0, 0, 1).start()
        weight_copy(0, 0, 2).start()

    @pl.when(step + 1 < pl.num_programs(0))
    def _():
        for part in range(3):
            weight_copy(step + 1, 1 - slot, part).start()

    @pl.when(step == 0)
    def _():
        token_copy(0).wait()
        token_copy(1).wait()

    states = [state_ref[head] if has_state else None for head in range(PAIR)]
    start = pl.multiple_of(step * columns, columns)
    gains = gain_ref[pl.ds(start, columns)].astype(jnp.float32).reshape(1, columns)

    packed = [[], []]
    for part in range(3):
        weight_copy(step, slot, part).wait()
        for index in range(2):
            tokens = tokens_ref[index * block : (index + 1) * block]
            packed[index].append(dot(tokens, weights[slot, part]).astype(jnp.bfloat16))

    def store(offset, mixed):
        for head, here, out in mixed:
            lanes = head_lanes(head)
            here = slice(offset + here.start, offset + here.stop)
            mean_square = jnp.mean(out * out, axis=-1, keepdims=True)
            normed = out * lax.rsqrt(mean_square + epsilon) * gains[:, lanes]
            there = pl.ds(pl.multiple_of(start + head * HD, HD), HD)
            residual = tokens_ref[here, there].astype(jnp.float32)
            out_ref[here, lanes] = (residual + normed).astype(jnp.bfloat16)

    for index in range(2):
        mixed, states = mix_heads(*packed[index], states)
        store(index * block, mixed)


def mixer(tokens, w_lin, gain_lin, state):
    rows, width = tokens.shape
    columns = PAIR * HD
    in_specs = [
        pl.BlockSpec(memory_space=pl.ANY),
        pl.BlockSpec(memory_space=pl.ANY),
        pl.BlockSpec(memory_space=pltpu.VMEM),
    ]
    operands = [tokens, w_lin, gain_lin]
    if state is not None:
        operands.insert(0, state)
        in_specs.insert(0, pl.BlockSpec((PAIR, HD, HD), lambda c: (c, 0, 0)))
    return pl.pallas_call(
        functools.partial(mixer_kernel, state is not None),
        grid=(HEADS // PAIR,),
        in_specs=in_specs,
        out_specs=pl.BlockSpec((rows, columns), lambda c: (0, c)),
        out_shape=jax.ShapeDtypeStruct((rows, width), jnp.bfloat16),
        scratch_shapes=[
            pltpu.VMEM((rows, width), jnp.bfloat16),
            pltpu.VMEM((2, 3, width, columns), jnp.bfloat16),
            pltpu.SemaphoreType.DMA((2,)),
            pltpu.SemaphoreType.DMA((2, 3)),
        ],
        compiler_params=pltpu.CompilerParams(vmem_limit_bytes=56 * MIB),
        cost_estimate=pl.CostEstimate(
            flops=2 * rows * width * 3 * width + 8 * rows * SPAN * width,
            bytes_accessed=2 * (3 * width * width + 2 * rows * width),
            transcendentals=rows * HEADS,
        ),
        name="mixer",
    )(*operands)


def incoming_state(tokens, w_lin, time_ranges):
    rows, width = tokens.shape
    packed = dot(tokens, w_lin[:, width:]).astype(jnp.bfloat16).reshape(rows, 2, HEADS, HD)
    block_total = jnp.einsum(
        "nhd,nhe->hde", packed[:, 0], packed[:, 1], preferred_element_type=jnp.float32
    )
    within = lax.axis_index("tm") // SB

    def advance_hop(turn_index, running_total):
        moved = shifted(running_total + block_total, "tm", SB)
        return jnp.where(within > 0, moved, 0.0)

    return lax.fori_loop(0, time_ranges - 1, advance_hop, jnp.zeros_like(block_total))


def pairs_kernel(hidden_ref, gain_ref, w_ref, normed_ref, *outs):
    widened = hidden_ref[...].astype(jnp.float32)
    mean_square = jnp.mean(widened * widened, axis=-1, keepdims=True)
    normed = (widened * lax.rsqrt(mean_square + epsilon) * gain_ref[...]).astype(jnp.bfloat16)
    normed_ref[...] = normed
    pairs = dot(normed, w_ref[...]).astype(jnp.bfloat16)
    offset = 0
    for out_ref in outs:
        for start in range(0, out_ref.shape[0], HD):
            here = slice(offset + start, offset + start + HD)
            for head in range(KVH):
                out_ref[start : start + HD, head_lanes(head)] = pairs[here, head_lanes(head)].T
        rows = out_ref.shape[0]
        out_ref[:, KVH * HD :] = pairs[offset : offset + rows, KVH * HD :]
        offset += rows


def make_pairs(hidden, gain, w_kv):
    rows, width = hidden.shape
    wide = w_kv.shape[1]
    return pl.pallas_call(
        pairs_kernel,
        out_shape=[
            jax.ShapeDtypeStruct((rows, width), jnp.bfloat16),
            jax.ShapeDtypeStruct((rows - LATE, wide), jnp.bfloat16),
            jax.ShapeDtypeStruct((LATE, wide), jnp.bfloat16),
        ],
        compiler_params=pltpu.CompilerParams(vmem_limit_bytes=16 * MIB),
        cost_estimate=pl.CostEstimate(
            flops=2 * rows * width * wide,
            bytes_accessed=2 * (2 * rows * width + width * wide + rows * wide),
            transcendentals=rows,
        ),
        name="pairs",
    )(hidden, gain, w_kv)


SCORE_SCALE = math.log2(math.e) / math.sqrt(HD)
GROUP = HEADS // KVH
LATE = 256


def keys_and_values(refs):
    both = []
    for head in range(KVH):
        keys, values = [], []
        for ref in refs:
            for start in range(0, ref.shape[0], HD):
                keys.append(ref[start : start + HD, head_lanes(head)])
            values.append(ref[:, head_lanes(KVH + head)])
        key = jnp.concatenate(keys, axis=1)
        value = jnp.concatenate(values, axis=0)
        both.append((key, jnp.concatenate([value, jnp.ones_like(value)], axis=1)))
    return both


def own_kernel(normed_ref, w_ref, first_ref, last_ref, query_ref, sum_ref, total_ref, top_ref):
    both = keys_and_values([first_ref, last_ref])
    columns = GROUP * HD

    def project(group):
        lanes = slice(group * columns, (group + 1) * columns)
        query = dot(normed_ref[...], w_ref[:, lanes]).astype(jnp.bfloat16)
        query_ref[:, lanes] = query
        return query

    queries = {0: project(0)}

    def scores_of(head):
        group = head // GROUP
        return dot(queries[group][:, head_lanes(head % GROUP)], both[group][0])

    scores = scores_of(0)
    for head in range(HEADS):
        if head % GROUP == 0 and head + GROUP < HEADS:
            queries[head // GROUP + 1] = project(head // GROUP + 1)
        upcoming = scores_of(head + 1) if head + 1 < HEADS else None
        lanes = head_lanes(head)
        largest = jnp.max(scores, axis=-1, keepdims=True)
        raised = jnp.exp2((scores - largest) * SCORE_SCALE).astype(jnp.bfloat16)
        summed = dot(raised, both[head // GROUP][1])
        sum_ref[:, lanes] = summed[:, :HD]
        total_ref[:, lanes] = summed[:, HD:]
        top_ref[:, lanes] = jnp.broadcast_to(largest * SCORE_SCALE, (scores.shape[0], HD))
        scores = upcoming


def own_frame(normed, w_query, first, last):
    rows, width = normed.shape
    return pl.pallas_call(
        own_kernel,
        out_shape=[jax.ShapeDtypeStruct((rows, width), jnp.bfloat16)]
        + [jax.ShapeDtypeStruct((rows, width), jnp.float32)] * 3,
        compiler_params=pltpu.CompilerParams(vmem_limit_bytes=32 * MIB),
        cost_estimate=pl.CostEstimate(
            flops=2 * rows * width * width + 4 * rows * rows * width,
            bytes_accessed=2 * width * width + 8 * rows * width,
            transcendentals=rows * rows * HEADS,
        ),
        name="own_frame",
    )(normed, w_query, first, last)


def earlier_kernel(last, query_ref, pairs_ref, sum_ref, total_ref, top_ref, *refs):
    both = keys_and_values([pairs_ref])
    barred = jnp.where(lax.axis_index("tm") > 0, 0.0, -jnp.inf)

    def scores_of(head):
        return dot(query_ref[:, head_lanes(head)], both[head // GROUP][0])

    copies = []
    scores = scores_of(0)
    for head in range(HEADS):
        lanes = head_lanes(head)
        upcoming = scores_of(head + 1) if head + 1 < HEADS else None
        before = top_ref[:, lanes]
        here = jnp.max(scores, axis=-1, keepdims=True) * SCORE_SCALE + barred
        largest = jnp.maximum(jnp.broadcast_to(here, before.shape), before)
        below = jnp.concatenate([largest - barred] * (scores.shape[1] // HD), axis=1)
        raised = jnp.exp2(scores * SCORE_SCALE - below).astype(jnp.bfloat16)
        summed = dot(raised, both[head // GROUP][1])
        share = jnp.exp2(before - largest)
        mixed = sum_ref[:, lanes] * share + summed[:, :HD]
        total = total_ref[:, lanes] * share + summed[:, HD:]
        if last:
            out_hbm, out_ref, sent = refs
            out_ref[:, lanes] = (mixed / total).astype(jnp.bfloat16)
            if head % 2:
                columns = slice((head - 1) * HD, (head + 1) * HD)
                copies.append(
                    pltpu.make_async_copy(
                        out_ref.at[:, columns], out_hbm.at[:, columns], sent.at[head // 2]
                    )
                )
                copies[-1].start()
        else:
            refs[0][:, lanes] = mixed
            refs[1][:, lanes] = total
            refs[2][:, lanes] = largest
        scores = upcoming
    for copy in copies:
        copy.wait()


def earlier_frame(last, query, pairs, *so_far):
    rows, width = query.shape
    if last:
        extra = dict(
            out_shape=jax.ShapeDtypeStruct((rows, width), jnp.bfloat16),
            out_specs=pl.BlockSpec(memory_space=pl.ANY),
            scratch_shapes=[
                pltpu.VMEM((rows, width), jnp.bfloat16),
                pltpu.SemaphoreType.DMA((HEADS // 2,)),
            ],
        )
    else:
        extra = dict(out_shape=[jax.ShapeDtypeStruct((rows, width), jnp.float32)] * 3)
    return pl.pallas_call(
        functools.partial(earlier_kernel, last),
        compiler_params=pltpu.CompilerParams(vmem_limit_bytes=32 * MIB),
        cost_estimate=pl.CostEstimate(
            flops=4 * rows * pairs.shape[0] * width,
            bytes_accessed=10 * rows * width,
            transcendentals=rows * pairs.shape[0] * HEADS,
        ),
        name="earlier_frame",
        **extra,
    )(query, pairs, *so_far)


def to_frames(hidden):
    rows, columns = hidden.shape
    teams = [[t * SB + s for s in range(SB)] for t in range(lax.axis_size("tm") // SB)]
    moved = lax.all_to_all(
        hidden.reshape(SB, rows // SB, columns), "tm", 0, 0, axis_index_groups=teams, tiled=True
    )
    return moved.reshape(rows, columns)


def body(space_time, w_lin, gain_lin, w_query, w_kv, frame_attention_gain):
    tokens = space_time[0]
    time_ranges = lax.axis_size("tm") // SB
    state = incoming_state(tokens, w_lin, time_ranges) if time_ranges > 1 else None
    hidden = mixer(tokens, w_lin, gain_lin, state)
    hidden, gain = lax.optimization_barrier((hidden, frame_attention_gain))
    frame_rows = to_frames(hidden)
    gain = gain.astype(jnp.float32).reshape(1, -1)
    normed, first, last = make_pairs(frame_rows, gain, w_kv)
    earlier_first = shifted(first, "tm", 1)
    earlier_last = shifted(last, "tm", 1)
    query, *so_far = own_frame(normed, w_query, first, last)
    so_far = earlier_frame(False, query, earlier_first, *so_far)
    attended = earlier_frame(True, query, earlier_last, *so_far)
    return attended[None]


def solution(mesh):
    placed = (P(("groups", "tm"), None, None), P(), P(), P(), P(), P())
    return jax.shard_map(
        body, mesh=mesh, in_specs=placed, out_specs=P(("groups", "tm"), None, None), check_vma=False
    )
```

```python
import functools
import math

import jax
import jax.numpy as jnp
from jax import lax
from jax.experimental import pallas as pl
from jax.experimental.pallas import tpu as pltpu
from jax.sharding import PartitionSpec as P

HEADS = 8
HD = 128
KVH = 2
SB = 16
SPAN = 128
PAIR = 4

epsilon = 1e-06
MIB = 1 << 20


def shifted(block, axis, distance):
    devices = range(lax.axis_size(axis))
    route = [(i - distance, i) for i in devices if i - distance in devices]
    return lax.ppermute(block, axis, route)


def dot(a, b):
    return jnp.dot(a, b, preferred_element_type=jnp.float32)


def dot_nt(a, b):
    return lax.dot_general(a, b, (((1,), (1,)), ((), ())), preferred_element_type=jnp.float32)


def dot_tn(a, b):
    return lax.dot_general(a, b, (((0,), (0,)), ((), ())), preferred_element_type=jnp.float32)


def head_lanes(head):
    return slice(head * HD, (head + 1) * HD)


def causal_mask():
    shape = (SPAN, SPAN)
    return lax.broadcasted_iota(jnp.int32, shape, 0) >= lax.broadcasted_iota(jnp.int32, shape, 1)


def mix_heads(query, key, value, states):
    rows = query.shape[0]
    causal = causal_mask()
    spans = [slice(start, start + SPAN) for start in range(0, rows, SPAN)]
    heads = range(query.shape[1] // HD)
    units = [(head, span) for head in heads for span in range(len(spans))]
    local, before, mixed = {}, {}, []
    for head, span in units:
        lanes, here = head_lanes(head), spans[span]
        scores = dot_nt(query[here, lanes], key[here, lanes])
        local[head, span] = jnp.where(causal, scores, 0.0).astype(jnp.bfloat16)
    for head in heads:
        lanes = head_lanes(head)
        state = states[head]
        for span, here in enumerate(spans):
            before[head, span] = state
            if span + 1 < len(spans):
                update = dot_tn(key[here, lanes], value[here, lanes])
                state = update if state is None else state + update
    for head, span in units:
        lanes, here = head_lanes(head), spans[span]
        if before[head, span] is None:
            out = dot(local[head, span], value[here, lanes])
        else:
            out = dot(
                jnp.concatenate([query[here, lanes], local[head, span]], axis=1),
                jnp.concatenate(
                    [before[head, span].astype(jnp.bfloat16), value[here, lanes]], axis=0
                ),
            )
        mixed.append((head, here, out))
    return mixed


def mixer_kernel(has_state, *refs):
    if has_state:
        state_ref, *refs = refs
    tokens_hbm, w_hbm, gain_ref, out_hbm, tokens_ref, weights, out_ref, *arrived = refs
    tokens_in, weights_in, sent = arrived
    rows, width = tokens_ref.shape
    columns = PAIR * HD
    groups = HEADS // PAIR

    copies = [[pltpu.make_async_copy(tokens_hbm, tokens_ref, tokens_in)]]
    for group in range(groups):
        here = []
        for part in range(3):
            start = part * width + group * columns
            here.append(
                pltpu.make_async_copy(
                    w_hbm.at[:, start : start + columns],
                    weights.at[group, part],
                    weights_in.at[group, part],
                )
            )
        copies.append(here)
    for copy in sum(copies, []):
        copy.start()
    gains = gain_ref[...].astype(jnp.float32).reshape(1, width)

    def project(group):
        tokens = tokens_ref[...]
        return [dot(tokens, weights[group, part]).astype(jnp.bfloat16) for part in range(3)]

    def mix(group, parts):
        start = group * columns
        heads = range(group * PAIR, (group + 1) * PAIR)
        states = [state_ref[head] if has_state else None for head in heads]
        for head, here, out in mix_heads(*parts, states):
            lanes = head_lanes(group * PAIR + head)
            mean_square = jnp.mean(out * out, axis=-1, keepdims=True)
            normed = out * lax.rsqrt(mean_square + epsilon) * gains[:, lanes]
            residual = tokens_ref[here, lanes].astype(jnp.float32)
            out_ref[here, lanes] = (residual + normed).astype(jnp.bfloat16)
        there = slice(start, start + columns)
        copy = pltpu.make_async_copy(out_ref.at[:, there], out_hbm.at[:, there], sent.at[group])
        copy.start()
        return copy

    for copy in copies[0] + copies[1]:
        copy.wait()
    parts = project(0)
    for copy in sum(copies[2:], []):
        copy.wait()
    leaving = []
    for group in range(groups):
        upcoming = project(group + 1) if group + 1 < groups else None
        leaving.append(mix(group, parts))
        parts = upcoming
    for copy in leaving:
        copy.wait()


def mixer(tokens, w_lin, gain_lin, state):
    rows, width = tokens.shape
    columns = PAIR * HD
    groups = HEADS // PAIR
    hbm = pl.BlockSpec(memory_space=pl.ANY)
    vmem = pl.BlockSpec(memory_space=pltpu.VMEM)
    in_specs = [hbm, hbm, vmem]
    operands = [tokens, w_lin, gain_lin]
    if state is not None:
        operands.insert(0, state)
        in_specs.insert(0, vmem)
    return pl.pallas_call(
        functools.partial(mixer_kernel, state is not None),
        in_specs=in_specs,
        out_specs=hbm,
        out_shape=jax.ShapeDtypeStruct((rows, width), jnp.bfloat16),
        scratch_shapes=[
            pltpu.VMEM((rows, width), jnp.bfloat16),
            pltpu.VMEM((groups, 3, width, columns), jnp.bfloat16),
            pltpu.VMEM((rows, width), jnp.bfloat16),
            pltpu.SemaphoreType.DMA,
            pltpu.SemaphoreType.DMA((groups, 3)),
            pltpu.SemaphoreType.DMA((groups,)),
        ],
        compiler_params=pltpu.CompilerParams(vmem_limit_bytes=56 * MIB),
        cost_estimate=pl.CostEstimate(
            flops=2 * rows * width * 3 * width + 8 * rows * SPAN * width,
            bytes_accessed=2 * (3 * width * width + 2 * rows * width),
            transcendentals=rows * HEADS,
        ),
        name="mixer",
    )(*operands)


def incoming_state(tokens, w_lin, time_ranges):
    rows, width = tokens.shape
    packed = dot(tokens, w_lin[:, width:]).astype(jnp.bfloat16).reshape(rows, 2, HEADS, HD)
    block_total = jnp.einsum(
        "nhd,nhe->hde", packed[:, 0], packed[:, 1], preferred_element_type=jnp.float32
    )
    within = lax.axis_index("tm") // SB

    def advance_hop(turn_index, running_total):
        moved = shifted(running_total + block_total, "tm", SB)
        return jnp.where(within > 0, moved, 0.0)

    return lax.fori_loop(0, time_ranges - 1, advance_hop, jnp.zeros_like(block_total))


def pairs_kernel(hidden_ref, gain_ref, w_ref, normed_ref, *outs):
    widened = hidden_ref[...].astype(jnp.float32)
    mean_square = jnp.mean(widened * widened, axis=-1, keepdims=True)
    normed = (widened * lax.rsqrt(mean_square + epsilon) * gain_ref[...]).astype(jnp.bfloat16)
    normed_ref[...] = normed
    pairs = dot(normed, w_ref[...]).astype(jnp.bfloat16)
    offset = 0
    for out_ref in outs:
        for start in range(0, out_ref.shape[0], HD):
            here = slice(offset + start, offset + start + HD)
            for head in range(KVH):
                out_ref[start : start + HD, head_lanes(head)] = pairs[here, head_lanes(head)].T
        rows = out_ref.shape[0]
        out_ref[:, KVH * HD :] = pairs[offset : offset + rows, KVH * HD :]
        offset += rows


def make_pairs(hidden, gain, w_kv):
    rows, width = hidden.shape
    wide = w_kv.shape[1]
    return pl.pallas_call(
        pairs_kernel,
        out_shape=[
            jax.ShapeDtypeStruct((rows, width), jnp.bfloat16),
            jax.ShapeDtypeStruct((rows - LATE, wide), jnp.bfloat16),
            jax.ShapeDtypeStruct((LATE, wide), jnp.bfloat16),
        ],
        compiler_params=pltpu.CompilerParams(vmem_limit_bytes=16 * MIB),
        cost_estimate=pl.CostEstimate(
            flops=2 * rows * width * wide,
            bytes_accessed=2 * (2 * rows * width + width * wide + rows * wide),
            transcendentals=rows,
        ),
        name="pairs",
    )(hidden, gain, w_kv)


SCORE_SCALE = math.log2(math.e) / math.sqrt(HD)
GROUP = HEADS // KVH
LATE = 256


def keys_and_values(refs):
    both = []
    for head in range(KVH):
        keys, values = [], []
        for ref in refs:
            for start in range(0, ref.shape[0], HD):
                keys.append(ref[start : start + HD, head_lanes(head)])
            values.append(ref[:, head_lanes(KVH + head)])
        key = jnp.concatenate(keys, axis=1)
        value = jnp.concatenate(values, axis=0)
        both.append((key, jnp.concatenate([value, jnp.ones_like(value)], axis=1)))
    return both


def own_kernel(normed_ref, w_ref, first_ref, last_ref, query_ref, sum_ref, total_ref, top_ref):
    both = keys_and_values([first_ref, last_ref])
    columns = GROUP * HD

    def project(group):
        lanes = slice(group * columns, (group + 1) * columns)
        query = dot(normed_ref[...], w_ref[:, lanes]).astype(jnp.bfloat16)
        query_ref[:, lanes] = query
        return query

    queries = {0: project(0)}

    def scores_of(head):
        group = head // GROUP
        return dot(queries[group][:, head_lanes(head % GROUP)], both[group][0])

    scores = scores_of(0)
    for head in range(HEADS):
        if head % GROUP == 0 and head + GROUP < HEADS:
            queries[head // GROUP + 1] = project(head // GROUP + 1)
        upcoming = scores_of(head + 1) if head + 1 < HEADS else None
        lanes = head_lanes(head)
        largest = jnp.max(scores, axis=-1, keepdims=True)
        raised = jnp.exp2((scores - largest) * SCORE_SCALE).astype(jnp.bfloat16)
        summed = dot(raised, both[head // GROUP][1])
        sum_ref[:, lanes] = summed[:, :HD]
        total_ref[:, lanes] = summed[:, HD:]
        top_ref[:, lanes] = jnp.broadcast_to(largest * SCORE_SCALE, (scores.shape[0], HD))
        scores = upcoming


def own_frame(normed, w_query, first, last):
    rows, width = normed.shape
    return pl.pallas_call(
        own_kernel,
        out_shape=[jax.ShapeDtypeStruct((rows, width), jnp.bfloat16)]
        + [jax.ShapeDtypeStruct((rows, width), jnp.float32)] * 3,
        compiler_params=pltpu.CompilerParams(vmem_limit_bytes=32 * MIB),
        cost_estimate=pl.CostEstimate(
            flops=2 * rows * width * width + 4 * rows * rows * width,
            bytes_accessed=2 * width * width + 8 * rows * width,
            transcendentals=rows * rows * HEADS,
        ),
        name="own_frame",
    )(normed, w_query, first, last)


def earlier_kernel(last, query_ref, pairs_ref, sum_ref, total_ref, top_ref, *refs):
    both = keys_and_values([pairs_ref])
    barred = jnp.where(lax.axis_index("tm") > 0, 0.0, -jnp.inf)

    def scores_of(head):
        return dot(query_ref[:, head_lanes(head)], both[head // GROUP][0])

    copies = []
    scores = scores_of(0)
    for head in range(HEADS):
        lanes = head_lanes(head)
        upcoming = scores_of(head + 1) if head + 1 < HEADS else None
        before = top_ref[:, lanes]
        here = jnp.max(scores, axis=-1, keepdims=True) * SCORE_SCALE + barred
        largest = jnp.maximum(jnp.broadcast_to(here, before.shape), before)
        below = jnp.concatenate([largest - barred] * (scores.shape[1] // HD), axis=1)
        raised = jnp.exp2(scores * SCORE_SCALE - below).astype(jnp.bfloat16)
        summed = dot(raised, both[head // GROUP][1])
        share = jnp.exp2(before - largest)
        mixed = sum_ref[:, lanes] * share + summed[:, :HD]
        total = total_ref[:, lanes] * share + summed[:, HD:]
        if last:
            out_hbm, out_ref, sent = refs
            out_ref[:, lanes] = (mixed / total).astype(jnp.bfloat16)
            if head % 2:
                columns = slice((head - 1) * HD, (head + 1) * HD)
                copies.append(
                    pltpu.make_async_copy(
                        out_ref.at[:, columns], out_hbm.at[:, columns], sent.at[head // 2]
                    )
                )
                copies[-1].start()
        else:
            refs[0][:, lanes] = mixed
            refs[1][:, lanes] = total
            refs[2][:, lanes] = largest
        scores = upcoming
    for copy in copies:
        copy.wait()


def earlier_frame(last, query, pairs, *so_far):
    rows, width = query.shape
    if last:
        extra = dict(
            out_shape=jax.ShapeDtypeStruct((rows, width), jnp.bfloat16),
            out_specs=pl.BlockSpec(memory_space=pl.ANY),
            scratch_shapes=[
                pltpu.VMEM((rows, width), jnp.bfloat16),
                pltpu.SemaphoreType.DMA((HEADS // 2,)),
            ],
        )
    else:
        extra = dict(out_shape=[jax.ShapeDtypeStruct((rows, width), jnp.float32)] * 3)
    return pl.pallas_call(
        functools.partial(earlier_kernel, last),
        compiler_params=pltpu.CompilerParams(vmem_limit_bytes=32 * MIB),
        cost_estimate=pl.CostEstimate(
            flops=4 * rows * pairs.shape[0] * width,
            bytes_accessed=10 * rows * width,
            transcendentals=rows * pairs.shape[0] * HEADS,
        ),
        name="earlier_frame",
        **extra,
    )(query, pairs, *so_far)


def to_frames(hidden):
    rows, columns = hidden.shape
    teams = [[t * SB + s for s in range(SB)] for t in range(lax.axis_size("tm") // SB)]
    moved = lax.all_to_all(
        hidden.reshape(SB, rows // SB, columns), "tm", 0, 0, axis_index_groups=teams, tiled=True
    )
    return moved.reshape(rows, columns)


def body(space_time, w_lin, gain_lin, w_query, w_kv, frame_attention_gain):
    tokens = space_time[0]
    time_ranges = lax.axis_size("tm") // SB
    state = incoming_state(tokens, w_lin, time_ranges) if time_ranges > 1 else None
    hidden = mixer(tokens, w_lin, gain_lin, state)
    hidden, gain = lax.optimization_barrier((hidden, frame_attention_gain))
    frame_rows = to_frames(hidden)
    gain = gain.astype(jnp.float32).reshape(1, -1)
    normed, first, last = make_pairs(frame_rows, gain, w_kv)
    earlier_first = shifted(first, "tm", 1)
    earlier_last = shifted(last, "tm", 1)
    query, *so_far = own_frame(normed, w_query, first, last)
    so_far = earlier_frame(False, query, earlier_first, *so_far)
    attended = earlier_frame(True, query, earlier_last, *so_far)
    return attended[None]


def solution(mesh):
    placed = (P(("groups", "tm"), None, None), P(), P(), P(), P(), P())
    return jax.shard_map(
        body, mesh=mesh, in_specs=placed, out_specs=P(("groups", "tm"), None, None), check_vma=False
    )
```

```python
import functools
import math

import jax
import jax.numpy as jnp
from jax import lax
from jax.experimental import pallas as pl
from jax.experimental.pallas import tpu as pltpu
from jax.sharding import PartitionSpec as P

HEADS = 8
HD = 128
KVH = 2
SB = 16
SPAN = 128
GROUPS = ((0, 2), (2, 6), (6, 8))

epsilon = 1e-06
MIB = 1 << 20


def shifted(block, axis, distance):
    devices = range(lax.axis_size(axis))
    route = [(i - distance, i) for i in devices if i - distance in devices]
    return lax.ppermute(block, axis, route)


def dot(a, b):
    return jnp.dot(a, b, preferred_element_type=jnp.float32)


def dot_nt(a, b):
    return lax.dot_general(a, b, (((1,), (1,)), ((), ())), preferred_element_type=jnp.float32)


def dot_tn(a, b):
    return lax.dot_general(a, b, (((0,), (0,)), ((), ())), preferred_element_type=jnp.float32)


def head_lanes(head):
    return slice(head * HD, (head + 1) * HD)


def causal_mask():
    shape = (SPAN, SPAN)
    return lax.broadcasted_iota(jnp.int32, shape, 0) >= lax.broadcasted_iota(jnp.int32, shape, 1)


def mix_heads(query, key, value, states):
    rows = query.shape[0]
    causal = causal_mask()
    spans = [slice(start, start + SPAN) for start in range(0, rows, SPAN)]
    heads = range(query.shape[1] // HD)
    units = [(head, span) for head in heads for span in range(len(spans))]
    local, before, mixed = {}, {}, []
    for head, span in units:
        lanes, here = head_lanes(head), spans[span]
        scores = dot_nt(query[here, lanes], key[here, lanes])
        local[head, span] = jnp.where(causal, scores, 0.0).astype(jnp.bfloat16)
    for head in heads:
        lanes = head_lanes(head)
        state = states[head]
        for span, here in enumerate(spans):
            before[head, span] = state
            if span + 1 < len(spans):
                update = dot_tn(key[here, lanes], value[here, lanes])
                state = update if state is None else state + update
    for head, span in units:
        lanes, here = head_lanes(head), spans[span]
        if before[head, span] is None:
            out = dot(local[head, span], value[here, lanes])
        else:
            out = dot(
                jnp.concatenate([query[here, lanes], local[head, span]], axis=1),
                jnp.concatenate(
                    [before[head, span].astype(jnp.bfloat16), value[here, lanes]], axis=0
                ),
            )
        mixed.append((head, here, out))
    return mixed


def mixer_kernel(has_state, *refs):
    if has_state:
        state_ref, *refs = refs
    tokens_hbm, w_hbm, gain_ref, out_hbm, tokens_ref, out_ref, *refs = refs
    *weights, tokens_in, weights_in, sent = refs
    rows, width = tokens_ref.shape

    first = [pltpu.make_async_copy(tokens_hbm, tokens_ref, tokens_in)]
    copies = []
    for index, (low, high) in enumerate(GROUPS):
        here = []
        for part in range(3):
            columns = slice(part * width + low * HD, part * width + high * HD)
            here.append(
                pltpu.make_async_copy(
                    w_hbm.at[:, columns], weights[index].at[part], weights_in.at[index, part]
                )
            )
        copies.append(here)
    for copy in first + sum(copies, []):
        copy.start()
    gains = gain_ref[...].astype(jnp.float32).reshape(1, width)

    def project(index):
        for copy in copies[index]:
            copy.wait()
        tokens = tokens_ref[...]
        return [dot(tokens, weights[index][part]).astype(jnp.bfloat16) for part in range(3)]

    def mix(index, parts):
        low, high = GROUPS[index]
        states = [state_ref[head] if has_state else None for head in range(low, high)]
        for head, here, out in mix_heads(*parts, states):
            lanes = head_lanes(low + head)
            mean_square = jnp.mean(out * out, axis=-1, keepdims=True)
            normed = out * lax.rsqrt(mean_square + epsilon) * gains[:, lanes]
            residual = tokens_ref[here, lanes].astype(jnp.float32)
            out_ref[here, lanes] = (residual + normed).astype(jnp.bfloat16)
        there = slice(low * HD, high * HD)
        copy = pltpu.make_async_copy(out_ref.at[:, there], out_hbm.at[:, there], sent.at[index])
        copy.start()
        return copy

    first[0].wait()
    parts = project(0)
    leaving = []
    for index in range(len(GROUPS)):
        upcoming = project(index + 1) if index + 1 < len(GROUPS) else None
        leaving.append(mix(index, parts))
        parts = upcoming
    for copy in leaving:
        copy.wait()


def mixer(tokens, w_lin, gain_lin, state):
    rows, width = tokens.shape
    hbm = pl.BlockSpec(memory_space=pl.ANY)
    vmem = pl.BlockSpec(memory_space=pltpu.VMEM)
    in_specs = [hbm, hbm, vmem]
    operands = [tokens, w_lin, gain_lin]
    if state is not None:
        operands.insert(0, state)
        in_specs.insert(0, vmem)
    return pl.pallas_call(
        functools.partial(mixer_kernel, state is not None),
        in_specs=in_specs,
        out_specs=hbm,
        out_shape=jax.ShapeDtypeStruct((rows, width), jnp.bfloat16),
        scratch_shapes=[pltpu.VMEM((rows, width), jnp.bfloat16)] * 2
        + [pltpu.VMEM((3, width, (high - low) * HD), jnp.bfloat16) for low, high in GROUPS]
        + [
            pltpu.SemaphoreType.DMA,
            pltpu.SemaphoreType.DMA((len(GROUPS), 3)),
            pltpu.SemaphoreType.DMA((len(GROUPS),)),
        ],
        compiler_params=pltpu.CompilerParams(vmem_limit_bytes=56 * MIB),
        cost_estimate=pl.CostEstimate(
            flops=2 * rows * width * 3 * width + 8 * rows * SPAN * width,
            bytes_accessed=2 * (3 * width * width + 2 * rows * width),
            transcendentals=rows * HEADS,
        ),
        name="mixer",
    )(*operands)


def incoming_state(tokens, w_lin, time_ranges):
    rows, width = tokens.shape
    packed = dot(tokens, w_lin[:, width:]).astype(jnp.bfloat16).reshape(rows, 2, HEADS, HD)
    block_total = jnp.einsum(
        "nhd,nhe->hde", packed[:, 0], packed[:, 1], preferred_element_type=jnp.float32
    )
    within = lax.axis_index("tm") // SB

    def advance_hop(turn_index, running_total):
        moved = shifted(running_total + block_total, "tm", SB)
        return jnp.where(within > 0, moved, 0.0)

    return lax.fori_loop(0, time_ranges - 1, advance_hop, jnp.zeros_like(block_total))


def pairs_kernel(hidden_ref, gain_ref, w_ref, normed_ref, *outs):
    widened = hidden_ref[...].astype(jnp.float32)
    mean_square = jnp.mean(widened * widened, axis=-1, keepdims=True)
    normed = (widened * lax.rsqrt(mean_square + epsilon) * gain_ref[...]).astype(jnp.bfloat16)
    normed_ref[...] = normed
    pairs = dot(normed, w_ref[...]).astype(jnp.bfloat16)
    for head, out_ref in enumerate(outs):
        for start in range(0, pairs.shape[0], HD):
            here = slice(start, start + HD)
            out_ref[here, :HD] = pairs[here, head_lanes(head)].T
        out_ref[:, HD:] = pairs[:, head_lanes(KVH + head)]


def make_pairs(hidden, gain, w_kv):
    rows, width = hidden.shape
    wide = w_kv.shape[1]
    return pl.pallas_call(
        pairs_kernel,
        out_shape=[jax.ShapeDtypeStruct((rows, width), jnp.bfloat16)]
        + [jax.ShapeDtypeStruct((rows, wide // KVH), jnp.bfloat16)] * KVH,
        compiler_params=pltpu.CompilerParams(vmem_limit_bytes=16 * MIB),
        cost_estimate=pl.CostEstimate(
            flops=2 * rows * width * wide,
            bytes_accessed=2 * (2 * rows * width + width * wide + rows * wide),
            transcendentals=rows,
        ),
        name="pairs",
    )(hidden, gain, w_kv)


SCORE_SCALE = math.log2(math.e) / math.sqrt(HD)
GROUP = HEADS // KVH


def key_and_value(ref):
    key = jnp.concatenate(
        [ref[start : start + HD, :HD] for start in range(0, ref.shape[0], HD)], axis=1
    )
    value = ref[:, HD:]
    return key, jnp.concatenate([value, jnp.ones_like(value)], axis=1)


def own_kernel(normed_ref, w_ref, *refs):
    both = [key_and_value(ref) for ref in refs[:KVH]]
    query_ref, sum_ref, total_ref, top_ref = refs[KVH:]
    columns = GROUP * HD

    def project(group):
        lanes = slice(group * columns, (group + 1) * columns)
        query = dot(normed_ref[...], w_ref[:, lanes]).astype(jnp.bfloat16)
        query_ref[:, lanes] = query
        return query

    queries = {0: project(0)}

    def scores_of(head):
        group = head // GROUP
        return dot(queries[group][:, head_lanes(head % GROUP)], both[group][0])

    scores = scores_of(0)
    for head in range(HEADS):
        if head % GROUP == 0 and head + GROUP < HEADS:
            queries[head // GROUP + 1] = project(head // GROUP + 1)
        upcoming = scores_of(head + 1) if head + 1 < HEADS else None
        lanes = head_lanes(head)
        largest = jnp.max(scores, axis=-1, keepdims=True)
        raised = jnp.exp2((scores - largest) * SCORE_SCALE).astype(jnp.bfloat16)
        summed = dot(raised, both[head // GROUP][1])
        sum_ref[:, lanes] = summed[:, :HD]
        total_ref[:, lanes] = summed[:, HD:]
        top_ref[:, lanes] = jnp.broadcast_to(largest * SCORE_SCALE, (scores.shape[0], HD))
        scores = upcoming


def own_frame(normed, w_query, pairs):
    rows, width = normed.shape
    return pl.pallas_call(
        own_kernel,
        out_shape=[jax.ShapeDtypeStruct((rows, width), jnp.bfloat16)]
        + [jax.ShapeDtypeStruct((rows, width), jnp.float32)] * 3,
        compiler_params=pltpu.CompilerParams(vmem_limit_bytes=32 * MIB),
        cost_estimate=pl.CostEstimate(
            flops=2 * rows * width * width + 4 * rows * rows * width,
            bytes_accessed=2 * width * width + 8 * rows * width,
            transcendentals=rows * rows * HEADS,
        ),
        name="own_frame",
    )(normed, w_query, *pairs)


def earlier_kernel(group, query_ref, pairs_ref, sum_ref, total_ref, top_ref, *refs):
    key, value = key_and_value(pairs_ref)
    barred = jnp.where(lax.axis_index("tm") > 0, 0.0, -jnp.inf)
    columns = GROUP * HD
    last = group == KVH - 1
    copies = []
    if last:
        *done_refs, out_hbm, out_ref, sent = refs

        def leave(source, start):
            there = out_hbm.at[:, start : start + source.shape[1]]
            copies.append(pltpu.make_async_copy(source, there, sent.at[len(copies)]))
            copies[-1].start()

        for index, ref in enumerate(done_refs):
            leave(ref, index * columns)
    else:
        (out_ref,) = refs

    def scores_of(head):
        return dot(query_ref[:, head_lanes(group * GROUP + head)], key)

    scores = scores_of(0)
    for head in range(GROUP):
        lanes = head_lanes(group * GROUP + head)
        upcoming = scores_of(head + 1) if head + 1 < GROUP else None
        before = top_ref[:, lanes]
        here = jnp.max(scores, axis=-1, keepdims=True) * SCORE_SCALE + barred
        largest = jnp.maximum(jnp.broadcast_to(here, before.shape), before)
        below = jnp.concatenate([largest - barred] * (scores.shape[1] // HD), axis=1)
        raised = jnp.exp2(scores * SCORE_SCALE - below).astype(jnp.bfloat16)
        summed = dot(raised, value)
        share = jnp.exp2(before - largest)
        mixed = sum_ref[:, lanes] * share + summed[:, :HD]
        total = total_ref[:, lanes] * share + summed[:, HD:]
        out_ref[:, head_lanes(head)] = (mixed / total).astype(jnp.bfloat16)
        if last and head % 2:
            start = (head - 1) * HD
            leave(out_ref.at[:, start : start + 2 * HD], group * columns + start)
        scores = upcoming
    for copy in copies:
        copy.wait()


def earlier_frame(group, query, pairs, so_far, done):
    rows, width = query.shape
    columns = GROUP * HD
    last = group == KVH - 1
    extra = dict(out_shape=jax.ShapeDtypeStruct((rows, columns), jnp.bfloat16))
    if last:
        extra = dict(
            out_shape=jax.ShapeDtypeStruct((rows, width), jnp.bfloat16),
            out_specs=pl.BlockSpec(memory_space=pl.ANY),
            scratch_shapes=[
                pltpu.VMEM((rows, columns), jnp.bfloat16),
                pltpu.SemaphoreType.DMA((KVH - 1 + GROUP // 2,)),
            ],
        )
    operands = [query, pairs, *so_far] + (done if last else [])
    return pl.pallas_call(
        functools.partial(earlier_kernel, group),
        compiler_params=pltpu.CompilerParams(vmem_limit_bytes=32 * MIB),
        cost_estimate=pl.CostEstimate(
            flops=4 * rows * rows * columns,
            bytes_accessed=20 * rows * columns,
            transcendentals=rows * rows * GROUP,
        ),
        name="earlier_frame",
        **extra,
    )(*operands)


def to_frames(hidden):
    rows, columns = hidden.shape
    teams = [[t * SB + s for s in range(SB)] for t in range(lax.axis_size("tm") // SB)]
    moved = lax.all_to_all(
        hidden.reshape(SB, rows // SB, columns), "tm", 0, 0, axis_index_groups=teams, tiled=True
    )
    return moved.reshape(rows, columns)


def body(space_time, w_lin, gain_lin, w_query, w_kv, frame_attention_gain):
    tokens = space_time[0]
    time_ranges = lax.axis_size("tm") // SB
    state = incoming_state(tokens, w_lin, time_ranges) if time_ranges > 1 else None
    hidden = mixer(tokens, w_lin, gain_lin, state)
    hidden, gain = lax.optimization_barrier((hidden, frame_attention_gain))
    frame_rows = to_frames(hidden)
    gain = gain.astype(jnp.float32).reshape(1, -1)
    normed, *pairs = make_pairs(frame_rows, gain, w_kv)
    earlier_pairs = [shifted(part, "tm", 1) for part in pairs]
    query, *so_far = own_frame(normed, w_query, pairs)
    done = []
    for group, part in enumerate(earlier_pairs):
        done.append(earlier_frame(group, query, part, so_far, done))
    return done[-1][None]


def solution(mesh):
    placed = (P(("groups", "tm"), None, None), P(), P(), P(), P(), P())
    return jax.shard_map(
        body, mesh=mesh, in_specs=placed, out_specs=P(("groups", "tm"), None, None), check_vma=False
    )
```

```python
import functools
import math

import jax
import jax.numpy as jnp
from jax import lax
from jax.experimental import pallas as pl
from jax.experimental.pallas import tpu as pltpu
from jax.sharding import PartitionSpec as P

HEADS = 8
HD = 128
KVH = 2
SB = 16
SPAN = 128
GROUPS = ((0, 4), (4, 8))

epsilon = 1e-06
MIB = 1 << 20


def shifted(block, axis, distance):
    devices = range(lax.axis_size(axis))
    route = [(i - distance, i) for i in devices if i - distance in devices]
    return lax.ppermute(block, axis, route)


def dot(a, b):
    return jnp.dot(a, b, preferred_element_type=jnp.float32)


def dot_nt(a, b):
    return lax.dot_general(a, b, (((1,), (1,)), ((), ())), preferred_element_type=jnp.float32)


def head_lanes(head):
    return slice(head * HD, (head + 1) * HD)


def causal_mask():
    shape = (SPAN, SPAN)
    return lax.broadcasted_iota(jnp.int32, shape, 0) >= lax.broadcasted_iota(jnp.int32, shape, 1)


def unit_matrix():
    shape = (HD, HD)
    same = lax.broadcasted_iota(jnp.int32, shape, 0) == lax.broadcasted_iota(jnp.int32, shape, 1)
    return jnp.where(same, 1.0, 0.0).astype(jnp.bfloat16)


def mean_of_squares(out):
    squares = out * out
    high = squares.astype(jnp.bfloat16)
    low = (squares - high.astype(jnp.float32)).astype(jnp.bfloat16)
    ones = jnp.ones((2 * HD, HD), jnp.bfloat16)
    return dot(jnp.concatenate([high, low], axis=1), ones) * (1.0 / HD)


def mix_heads(query, key, value, states):
    rows = query.shape[0]
    causal = causal_mask()
    spans = [slice(start, start + SPAN) for start in range(0, rows, SPAN)]
    heads = range(query.shape[1] // HD)
    units = [(head, span) for head in heads for span in range(len(spans))]
    local, before, mixed = {}, {}, []
    for head, span in units:
        lanes, here = head_lanes(head), spans[span]
        scores = dot_nt(query[here, lanes], key[here, lanes])
        local[head, span] = jnp.where(causal, scores, 0.0).astype(jnp.bfloat16)
    identity = unit_matrix()
    for head in heads:
        lanes = head_lanes(head)
        state = states[head]
        turned = dot_nt(identity, key[: rows - SPAN, lanes]).astype(jnp.bfloat16)
        for span, here in enumerate(spans):
            before[head, span] = state
            if span + 1 < len(spans):
                update = dot(turned[:, here], value[here, lanes])
                state = update if state is None else state + update
    for head, span in units:
        lanes, here = head_lanes(head), spans[span]
        if before[head, span] is None:
            out = dot(local[head, span], value[here, lanes])
        else:
            out = dot(
                jnp.concatenate([query[here, lanes], local[head, span]], axis=1),
                jnp.concatenate(
                    [before[head, span].astype(jnp.bfloat16), value[here, lanes]], axis=0
                ),
            )
        mixed.append((head, here, out))
    return mixed


def mixer_kernel(has_state, *refs):
    if has_state:
        state_ref, *refs = refs
    tokens_hbm, w_hbm, gain_ref, out_hbm, tokens_ref, out_ref, *refs = refs
    *weights, tokens_in, weights_in, sent = refs
    rows, width = tokens_ref.shape

    first = [pltpu.make_async_copy(tokens_hbm, tokens_ref, tokens_in)]
    copies = []
    for index, (low, high) in enumerate(GROUPS):
        here = []
        for part in range(3):
            columns = slice(part * width + low * HD, part * width + high * HD)
            here.append(
                pltpu.make_async_copy(
                    w_hbm.at[:, columns], weights[index].at[part], weights_in.at[index, part]
                )
            )
        copies.append(here)
    for copy in first + sum(copies, []):
        copy.start()
    gains = gain_ref[...].astype(jnp.float32).reshape(1, width)

    def project(index):
        for copy in copies[index]:
            copy.wait()
        tokens = tokens_ref[...]
        return [dot(tokens, weights[index][part]).astype(jnp.bfloat16) for part in range(3)]

    def mix(index, parts):
        low, high = GROUPS[index]
        states = [state_ref[head] if has_state else None for head in range(low, high)]
        for head, here, out in mix_heads(*parts, states):
            lanes = head_lanes(low + head)
            normed = out * lax.rsqrt(mean_of_squares(out) + epsilon) * gains[:, lanes]
            residual = tokens_ref[here, lanes].astype(jnp.float32)
            out_ref[here, lanes] = (residual + normed).astype(jnp.bfloat16)
        there = slice(low * HD, high * HD)
        copy = pltpu.make_async_copy(out_ref.at[:, there], out_hbm.at[:, there], sent.at[index])
        copy.start()
        return copy

    first[0].wait()
    parts = project(0)
    leaving = []
    for index in range(len(GROUPS)):
        upcoming = project(index + 1) if index + 1 < len(GROUPS) else None
        leaving.append(mix(index, parts))
        parts = upcoming
    for copy in leaving:
        copy.wait()


def mixer(tokens, w_lin, gain_lin, state):
    rows, width = tokens.shape
    hbm = pl.BlockSpec(memory_space=pl.ANY)
    vmem = pl.BlockSpec(memory_space=pltpu.VMEM)
    in_specs = [hbm, hbm, vmem]
    operands = [tokens, w_lin, gain_lin]
    if state is not None:
        operands.insert(0, state)
        in_specs.insert(0, vmem)
    return pl.pallas_call(
        functools.partial(mixer_kernel, state is not None),
        in_specs=in_specs,
        out_specs=hbm,
        out_shape=jax.ShapeDtypeStruct((rows, width), jnp.bfloat16),
        scratch_shapes=[pltpu.VMEM((rows, width), jnp.bfloat16)] * 2
        + [pltpu.VMEM((3, width, (high - low) * HD), jnp.bfloat16) for low, high in GROUPS]
        + [
            pltpu.SemaphoreType.DMA,
            pltpu.SemaphoreType.DMA((len(GROUPS), 3)),
            pltpu.SemaphoreType.DMA((len(GROUPS),)),
        ],
        compiler_params=pltpu.CompilerParams(vmem_limit_bytes=56 * MIB),
        cost_estimate=pl.CostEstimate(
            flops=2 * rows * width * 3 * width + 8 * rows * SPAN * width,
            bytes_accessed=2 * (3 * width * width + 2 * rows * width),
            transcendentals=rows * HEADS,
        ),
        name="mixer",
    )(*operands)


def incoming_state(tokens, w_lin, time_ranges):
    rows, width = tokens.shape
    packed = dot(tokens, w_lin[:, width:]).astype(jnp.bfloat16).reshape(rows, 2, HEADS, HD)
    block_total = jnp.einsum(
        "nhd,nhe->hde", packed[:, 0], packed[:, 1], preferred_element_type=jnp.float32
    )
    within = lax.axis_index("tm") // SB

    def advance_hop(turn_index, running_total):
        moved = shifted(running_total + block_total, "tm", SB)
        return jnp.where(within > 0, moved, 0.0)

    return lax.fori_loop(0, time_ranges - 1, advance_hop, jnp.zeros_like(block_total))


def pairs_kernel(hidden_ref, gain_ref, w_ref, normed_ref, *outs):
    widened = hidden_ref[...].astype(jnp.float32)
    mean_square = jnp.mean(widened * widened, axis=-1, keepdims=True)
    normed = (widened * lax.rsqrt(mean_square + epsilon) * gain_ref[...]).astype(jnp.bfloat16)
    normed_ref[...] = normed
    pairs = dot(normed, w_ref[...]).astype(jnp.bfloat16)
    for head, out_ref in enumerate(outs):
        for start in range(0, pairs.shape[0], HD):
            here = slice(start, start + HD)
            out_ref[here, :HD] = pairs[here, head_lanes(head)].T
        out_ref[:, HD:] = pairs[:, head_lanes(KVH + head)]


def make_pairs(hidden, gain, w_kv):
    rows, width = hidden.shape
    wide = w_kv.shape[1]
    return pl.pallas_call(
        pairs_kernel,
        out_shape=[jax.ShapeDtypeStruct((rows, width), jnp.bfloat16)]
        + [jax.ShapeDtypeStruct((rows, wide // KVH), jnp.bfloat16)] * KVH,
        compiler_params=pltpu.CompilerParams(vmem_limit_bytes=16 * MIB),
        cost_estimate=pl.CostEstimate(
            flops=2 * rows * width * wide,
            bytes_accessed=2 * (2 * rows * width + width * wide + rows * wide),
            transcendentals=rows,
        ),
        name="pairs",
    )(hidden, gain, w_kv)


SCORE_SCALE = math.log2(math.e) / math.sqrt(HD)
GROUP = HEADS // KVH


def key_and_value(ref):
    key = jnp.concatenate(
        [ref[start : start + HD, :HD] for start in range(0, ref.shape[0], HD)], axis=1
    )
    value = ref[:, HD:]
    return key, jnp.concatenate([value, jnp.ones_like(value)], axis=1)


def own_kernel(normed_ref, w_ref, *refs):
    both = [key_and_value(ref) for ref in refs[:KVH]]
    query_ref, sum_ref, total_ref, top_ref = refs[KVH:]
    columns = GROUP * HD

    def project(group):
        lanes = slice(group * columns, (group + 1) * columns)
        query = dot(normed_ref[...], w_ref[:, lanes]).astype(jnp.bfloat16)
        query_ref[:, lanes] = query
        return query

    queries = {0: project(0)}

    def scores_of(head):
        group = head // GROUP
        return dot(queries[group][:, head_lanes(head % GROUP)], both[group][0])

    scores = scores_of(0)
    for head in range(HEADS):
        if head % GROUP == 0 and head + GROUP < HEADS:
            queries[head // GROUP + 1] = project(head // GROUP + 1)
        upcoming = scores_of(head + 1) if head + 1 < HEADS else None
        lanes = head_lanes(head)
        largest = jnp.max(scores, axis=-1, keepdims=True)
        raised = jnp.exp2((scores - largest) * SCORE_SCALE).astype(jnp.bfloat16)
        summed = dot(raised, both[head // GROUP][1])
        sum_ref[:, lanes] = summed[:, :HD]
        total_ref[:, lanes] = summed[:, HD:]
        top_ref[:, lanes] = jnp.broadcast_to(largest * SCORE_SCALE, (scores.shape[0], HD))
        scores = upcoming


def own_frame(normed, w_query, pairs):
    rows, width = normed.shape
    return pl.pallas_call(
        own_kernel,
        out_shape=[jax.ShapeDtypeStruct((rows, width), jnp.bfloat16)]
        + [jax.ShapeDtypeStruct((rows, width), jnp.float32)] * 3,
        compiler_params=pltpu.CompilerParams(vmem_limit_bytes=32 * MIB),
        cost_estimate=pl.CostEstimate(
            flops=2 * rows * width * width + 4 * rows * rows * width,
            bytes_accessed=2 * width * width + 8 * rows * width,
            transcendentals=rows * rows * HEADS,
        ),
        name="own_frame",
    )(normed, w_query, *pairs)


def earlier_kernel(group, query_ref, pairs_ref, sum_ref, total_ref, top_ref, *refs):
    key, value = key_and_value(pairs_ref)
    barred = jnp.where(lax.axis_index("tm") > 0, 0.0, -jnp.inf)
    columns = GROUP * HD
    last = group == KVH - 1
    copies = []
    if last:
        *done_refs, out_hbm, out_ref, sent = refs

        def leave(source, start):
            there = out_hbm.at[:, start : start + source.shape[1]]
            copies.append(pltpu.make_async_copy(source, there, sent.at[len(copies)]))
            copies[-1].start()

        for index, ref in enumerate(done_refs):
            leave(ref, index * columns)
    else:
        (out_ref,) = refs

    def scores_of(head):
        return dot(query_ref[:, head_lanes(group * GROUP + head)], key)

    scores = scores_of(0)
    for head in range(GROUP):
        lanes = head_lanes(group * GROUP + head)
        upcoming = scores_of(head + 1) if head + 1 < GROUP else None
        before = top_ref[:, lanes]
        here = jnp.max(scores, axis=-1, keepdims=True) * SCORE_SCALE + barred
        largest = jnp.maximum(jnp.broadcast_to(here, before.shape), before)
        below = jnp.concatenate([largest - barred] * (scores.shape[1] // HD), axis=1)
        raised = jnp.exp2(scores * SCORE_SCALE - below).astype(jnp.bfloat16)
        summed = dot(raised, value)
        share = jnp.exp2(before - largest)
        mixed = sum_ref[:, lanes] * share + summed[:, :HD]
        total = total_ref[:, lanes] * share + summed[:, HD:]
        out_ref[:, head_lanes(head)] = (mixed / total).astype(jnp.bfloat16)
        if last and head % 2:
            start = (head - 1) * HD
            leave(out_ref.at[:, start : start + 2 * HD], group * columns + start)
        scores = upcoming
    for copy in copies:
        copy.wait()


def earlier_frame(group, query, pairs, so_far, done):
    rows, width = query.shape
    columns = GROUP * HD
    last = group == KVH - 1
    extra = dict(out_shape=jax.ShapeDtypeStruct((rows, columns), jnp.bfloat16))
    if last:
        extra = dict(
            out_shape=jax.ShapeDtypeStruct((rows, width), jnp.bfloat16),
            out_specs=pl.BlockSpec(memory_space=pl.ANY),
            scratch_shapes=[
                pltpu.VMEM((rows, columns), jnp.bfloat16),
                pltpu.SemaphoreType.DMA((KVH - 1 + GROUP // 2,)),
            ],
        )
    operands = [query, pairs, *so_far] + (done if last else [])
    return pl.pallas_call(
        functools.partial(earlier_kernel, group),
        compiler_params=pltpu.CompilerParams(vmem_limit_bytes=32 * MIB),
        cost_estimate=pl.CostEstimate(
            flops=4 * rows * rows * columns,
            bytes_accessed=20 * rows * columns,
            transcendentals=rows * rows * GROUP,
        ),
        name="earlier_frame",
        **extra,
    )(*operands)


def to_frames(hidden):
    rows, columns = hidden.shape
    teams = [[t * SB + s for s in range(SB)] for t in range(lax.axis_size("tm") // SB)]
    moved = lax.all_to_all(
        hidden.reshape(SB, rows // SB, columns), "tm", 0, 0, axis_index_groups=teams, tiled=True
    )
    return moved.reshape(rows, columns)


def body(space_time, w_lin, gain_lin, w_query, w_kv, frame_attention_gain):
    tokens = space_time[0]
    time_ranges = lax.axis_size("tm") // SB
    state = incoming_state(tokens, w_lin, time_ranges) if time_ranges > 1 else None
    hidden = mixer(tokens, w_lin, gain_lin, state)
    hidden, gain = lax.optimization_barrier((hidden, frame_attention_gain))
    frame_rows = to_frames(hidden)
    gain = gain.astype(jnp.float32).reshape(1, -1)
    normed, *pairs = make_pairs(frame_rows, gain, w_kv)
    earlier_pairs = [shifted(part, "tm", 1) for part in pairs]
    query, *so_far = own_frame(normed, w_query, pairs)
    done = []
    for group, part in enumerate(earlier_pairs):
        done.append(earlier_frame(group, query, part, so_far, done))
    return done[-1][None]


def solution(mesh):
    placed = (P(("groups", "tm"), None, None), P(), P(), P(), P(), P())
    return jax.shard_map(
        body, mesh=mesh, in_specs=placed, out_specs=P(("groups", "tm"), None, None), check_vma=False
    )
```

```python
import functools
import math

import jax
import jax.numpy as jnp
from jax import lax
from jax.experimental import pallas as pl
from jax.experimental.pallas import tpu as pltpu
from jax.sharding import PartitionSpec as P

HEADS = 8
HD = 128
KVH = 2
SB = 16
SPAN = 128
GROUPS = ((0, 4), (4, 8))
APART = (0, 10, 11, 9, 2, 12, 6, 13, 3, 7, 1, 14, 4, 15, 8, 5)

epsilon = 1e-06
MIB = 1 << 20


def shifted(block, axis, distance):
    devices = range(lax.axis_size(axis))
    route = [(i - distance, i) for i in devices if i - distance in devices]
    return lax.ppermute(block, axis, route)


def dot(a, b):
    return jnp.dot(a, b, preferred_element_type=jnp.float32)


def dot_nt(a, b):
    return lax.dot_general(a, b, (((1,), (1,)), ((), ())), preferred_element_type=jnp.float32)


def dot_tn(a, b):
    return lax.dot_general(a, b, (((0,), (0,)), ((), ())), preferred_element_type=jnp.float32)


def head_lanes(head):
    return slice(head * HD, (head + 1) * HD)


def causal_mask():
    shape = (SPAN, SPAN)
    return lax.broadcasted_iota(jnp.int32, shape, 0) >= lax.broadcasted_iota(jnp.int32, shape, 1)


def mix_heads(query, key, value, states):
    rows = query.shape[0]
    causal = causal_mask()
    spans = [slice(start, start + SPAN) for start in range(0, rows, SPAN)]
    heads = range(query.shape[1] // HD)
    units = [(head, span) for head in heads for span in range(len(spans))]
    local, before, mixed = {}, {}, []
    for head, span in units:
        lanes, here = head_lanes(head), spans[span]
        scores = dot_nt(query[here, lanes], key[here, lanes])
        local[head, span] = jnp.where(causal, scores, 0.0).astype(jnp.bfloat16)
    for head in heads:
        lanes = head_lanes(head)
        state = states[head]
        for span, here in enumerate(spans):
            before[head, span] = state
            if span + 1 < len(spans):
                update = dot_tn(key[here, lanes], value[here, lanes])
                state = update if state is None else state + update
    for head, span in units:
        lanes, here = head_lanes(head), spans[span]
        if before[head, span] is None:
            out = dot(local[head, span], value[here, lanes])
        else:
            out = dot(
                jnp.concatenate([query[here, lanes], local[head, span]], axis=1),
                jnp.concatenate(
                    [before[head, span].astype(jnp.bfloat16), value[here, lanes]], axis=0
                ),
            )
        mixed.append((head, here, out))
    return mixed


def mixer_kernel(has_state, *refs):
    if has_state:
        state_ref, *refs = refs
    tokens_hbm, w_hbm, gain_ref, *refs = refs
    tiles, (tokens_ref, out_ref, *weights, tokens_in, weights_in, sent) = refs[:SB], refs[SB:]
    rows, width = tokens_ref.shape
    size = rows // SB
    place = lax.rem(lax.axis_index("tm"), SB)

    first = [pltpu.make_async_copy(tokens_hbm, tokens_ref, tokens_in)]
    copies = []
    for index, (low, high) in enumerate(GROUPS):
        here = []
        for part in range(3):
            columns = slice(part * width + low * HD, part * width + high * HD)
            here.append(
                pltpu.make_async_copy(
                    w_hbm.at[:, columns], weights[index].at[part], weights_in.at[index, part]
                )
            )
        copies.append(here)
    for copy in first + sum(copies, []):
        copy.start()
    gains = gain_ref[...].astype(jnp.float32).reshape(1, width)

    leaving = []

    def project(index):
        for copy in copies[index]:
            copy.wait()
        tokens = tokens_ref[...]
        return [dot(tokens, weights[index][part]).astype(jnp.bfloat16) for part in range(3)]

    def mix(index, parts):
        low, high = GROUPS[index]
        states = [state_ref[head] if has_state else None for head in range(low, high)]
        for head, here, out in mix_heads(*parts, states):
            lanes = head_lanes(low + head)
            mean_square = jnp.mean(out * out, axis=-1, keepdims=True)
            normed = out * lax.rsqrt(mean_square + epsilon) * gains[:, lanes]
            residual = tokens_ref[here, lanes].astype(jnp.float32)
            out_ref[here, lanes] = (residual + normed).astype(jnp.bfloat16)
        lanes = slice(low * HD, high * HD)
        for slot, (apart, tile) in enumerate(zip(APART, tiles)):
            here = pl.ds(pl.multiple_of((place ^ apart) * size, size), size)
            copy = pltpu.make_async_copy(
                out_ref.at[here, lanes], tile.at[:, lanes], sent.at[index, slot]
            )
            copy.start()
            leaving.append(copy)

    first[0].wait()
    parts = project(0)
    for index in range(len(GROUPS)):
        upcoming = project(index + 1) if index + 1 < len(GROUPS) else None
        mix(index, parts)
        parts = upcoming
    for copy in leaving:
        copy.wait()


def mixer(tokens, w_lin, gain_lin, state):
    rows, width = tokens.shape
    hbm = pl.BlockSpec(memory_space=pl.ANY)
    vmem = pl.BlockSpec(memory_space=pltpu.VMEM)
    in_specs = [hbm, hbm, vmem]
    operands = [tokens, w_lin, gain_lin]
    if state is not None:
        operands.insert(0, state)
        in_specs.insert(0, vmem)
    return pl.pallas_call(
        functools.partial(mixer_kernel, state is not None),
        in_specs=in_specs,
        out_specs=[hbm] * SB,
        out_shape=[jax.ShapeDtypeStruct((rows // SB, width), jnp.bfloat16)] * SB,
        scratch_shapes=[pltpu.VMEM((rows, width), jnp.bfloat16)] * 2
        + [pltpu.VMEM((3, width, (high - low) * HD), jnp.bfloat16) for low, high in GROUPS]
        + [
            pltpu.SemaphoreType.DMA,
            pltpu.SemaphoreType.DMA((len(GROUPS), 3)),
            pltpu.SemaphoreType.DMA((len(GROUPS), SB)),
        ],
        compiler_params=pltpu.CompilerParams(vmem_limit_bytes=56 * MIB),
        cost_estimate=pl.CostEstimate(
            flops=2 * rows * width * 3 * width + 8 * rows * SPAN * width,
            bytes_accessed=2 * (3 * width * width + 2 * rows * width),
            transcendentals=rows * HEADS,
        ),
        name="mixer",
    )(*operands)


def incoming_state(tokens, w_lin, time_ranges):
    rows, width = tokens.shape
    packed = dot(tokens, w_lin[:, width:]).astype(jnp.bfloat16).reshape(rows, 2, HEADS, HD)
    block_total = jnp.einsum(
        "nhd,nhe->hde", packed[:, 0], packed[:, 1], preferred_element_type=jnp.float32
    )
    within = lax.axis_index("tm") // SB

    def advance_hop(turn_index, running_total):
        moved = shifted(running_total + block_total, "tm", SB)
        return jnp.where(within > 0, moved, 0.0)

    return lax.fori_loop(0, time_ranges - 1, advance_hop, jnp.zeros_like(block_total))


def pairs_kernel(gain_ref, w_ref, *refs):
    tiles, normed_ref, outs = refs[:SB], refs[SB], refs[SB + 1 :]
    gain = gain_ref[...].astype(jnp.float32).reshape(1, -1)
    widened = jnp.concatenate([tile[...] for tile in tiles], axis=0).astype(jnp.float32)
    mean_square = jnp.mean(widened * widened, axis=-1, keepdims=True)
    normed = (widened * lax.rsqrt(mean_square + epsilon) * gain).astype(jnp.bfloat16)
    normed_ref[...] = normed
    pairs = dot(normed, w_ref[...]).astype(jnp.bfloat16)
    for head, out_ref in enumerate(outs):
        for start in range(0, pairs.shape[0], HD):
            here = slice(start, start + HD)
            out_ref[here, :HD] = pairs[here, head_lanes(head)].T
        out_ref[:, HD:] = pairs[:, head_lanes(KVH + head)]


def make_pairs(tiles, gain, w_kv):
    width, wide = w_kv.shape
    rows = sum(tile.shape[0] for tile in tiles)
    return pl.pallas_call(
        pairs_kernel,
        out_shape=[jax.ShapeDtypeStruct((rows, width), jnp.bfloat16)]
        + [jax.ShapeDtypeStruct((rows, wide // KVH), jnp.bfloat16)] * KVH,
        compiler_params=pltpu.CompilerParams(vmem_limit_bytes=16 * MIB),
        cost_estimate=pl.CostEstimate(
            flops=2 * rows * width * wide,
            bytes_accessed=2 * (2 * rows * width + width * wide + rows * wide),
            transcendentals=rows,
        ),
        name="pairs",
    )(gain, w_kv, *tiles)


SCORE_SCALE = math.log2(math.e) / math.sqrt(HD)
GROUP = HEADS // KVH


def key_and_value(ref):
    key = jnp.concatenate(
        [ref[start : start + HD, :HD] for start in range(0, ref.shape[0], HD)], axis=1
    )
    value = ref[:, HD:]
    return key, jnp.concatenate([value, jnp.ones_like(value)], axis=1)


def own_kernel(normed_ref, w_ref, *refs):
    both = [key_and_value(ref) for ref in refs[:KVH]]
    query_ref, sum_ref, total_ref, top_ref = refs[KVH:]
    columns = GROUP * HD

    def project(group):
        lanes = slice(group * columns, (group + 1) * columns)
        query = dot(normed_ref[...], w_ref[:, lanes]).astype(jnp.bfloat16)
        query_ref[:, lanes] = query
        return query

    queries = {0: project(0)}

    def scores_of(head):
        group = head // GROUP
        return dot(queries[group][:, head_lanes(head % GROUP)], both[group][0])

    scores = scores_of(0)
    for head in range(HEADS):
        if head % GROUP == 0 and head + GROUP < HEADS:
            queries[head // GROUP + 1] = project(head // GROUP + 1)
        upcoming = scores_of(head + 1) if head + 1 < HEADS else None
        lanes = head_lanes(head)
        largest = jnp.max(scores, axis=-1, keepdims=True)
        raised = jnp.exp2((scores - largest) * SCORE_SCALE).astype(jnp.bfloat16)
        summed = dot(raised, both[head // GROUP][1])
        sum_ref[:, lanes] = summed[:, :HD]
        total_ref[:, lanes] = summed[:, HD:]
        top_ref[:, lanes] = jnp.broadcast_to(largest * SCORE_SCALE, (scores.shape[0], HD))
        scores = upcoming


def own_frame(normed, w_query, pairs):
    rows, width = normed.shape
    return pl.pallas_call(
        own_kernel,
        out_shape=[jax.ShapeDtypeStruct((rows, width), jnp.bfloat16)]
        + [jax.ShapeDtypeStruct((rows, width), jnp.float32)] * 3,
        compiler_params=pltpu.CompilerParams(vmem_limit_bytes=32 * MIB),
        cost_estimate=pl.CostEstimate(
            flops=2 * rows * width * width + 4 * rows * rows * width,
            bytes_accessed=2 * width * width + 8 * rows * width,
            transcendentals=rows * rows * HEADS,
        ),
        name="own_frame",
    )(normed, w_query, *pairs)


def earlier_kernel(group, query_ref, pairs_ref, sum_ref, total_ref, top_ref, *refs):
    key, value = key_and_value(pairs_ref)
    index = lax.axis_index("tm")
    barred = jnp.where(index > 0, 0.0, -jnp.inf)
    place = lax.rem(index, SB)
    size = query_ref.shape[0] // SB
    columns = GROUP * HD
    last = group == KVH - 1
    copies = []
    if last:
        *done_refs, out_hbm, out_ref, sent = refs

        def leave(source, start):
            there = out_hbm.at[:, start : start + source.shape[1]]
            copies.append(pltpu.make_async_copy(source, there, sent.at[len(copies)]))
            copies[-1].start()

        for part, ref in enumerate(done_refs):
            leave(ref, part * columns)
    else:
        (out_ref,) = refs

    def scores_of(head):
        return dot(query_ref[:, head_lanes(group * GROUP + head)], key)

    scores = scores_of(0)
    for head in range(GROUP):
        lanes = head_lanes(group * GROUP + head)
        upcoming = scores_of(head + 1) if head + 1 < GROUP else None
        before = top_ref[:, lanes]
        here = jnp.max(scores, axis=-1, keepdims=True) * SCORE_SCALE + barred
        largest = jnp.maximum(jnp.broadcast_to(here, before.shape), before)
        below = jnp.concatenate([largest - barred] * (scores.shape[1] // HD), axis=1)
        raised = jnp.exp2(scores * SCORE_SCALE - below).astype(jnp.bfloat16)
        summed = dot(raised, value)
        share = jnp.exp2(before - largest)
        mixed = sum_ref[:, lanes] * share + summed[:, :HD]
        total = total_ref[:, lanes] * share + summed[:, HD:]
        mixed = (mixed / total).astype(jnp.bfloat16)
        for slot, apart in enumerate(APART):
            there = pl.ds(pl.multiple_of((place ^ apart) * size, size), size)
            out_ref[there, head_lanes(head)] = mixed[slot * size : (slot + 1) * size]
        if last and head % 2:
            start = (head - 1) * HD
            leave(out_ref.at[:, start : start + 2 * HD], group * columns + start)
        scores = upcoming
    for copy in copies:
        copy.wait()


def earlier_frame(group, query, pairs, so_far, done):
    rows, width = query.shape
    columns = GROUP * HD
    last = group == KVH - 1
    extra = dict(out_shape=jax.ShapeDtypeStruct((rows, columns), jnp.bfloat16))
    if last:
        extra = dict(
            out_shape=jax.ShapeDtypeStruct((rows, width), jnp.bfloat16),
            out_specs=pl.BlockSpec(memory_space=pl.ANY),
            scratch_shapes=[
                pltpu.VMEM((rows, columns), jnp.bfloat16),
                pltpu.SemaphoreType.DMA((KVH - 1 + GROUP // 2,)),
            ],
        )
    operands = [query, pairs, *so_far] + (done if last else [])
    return pl.pallas_call(
        functools.partial(earlier_kernel, group),
        compiler_params=pltpu.CompilerParams(vmem_limit_bytes=32 * MIB),
        cost_estimate=pl.CostEstimate(
            flops=4 * rows * rows * columns,
            bytes_accessed=20 * rows * columns,
            transcendentals=rows * rows * GROUP,
        ),
        name="earlier_frame",
        **extra,
    )(*operands)


def swap(tile, apart):
    devices = lax.axis_size("tm")
    route = [(i, i - i % SB + (i % SB ^ apart)) for i in range(devices)]
    return lax.ppermute(tile, "tm", route)


def body(space_time, w_lin, gain_lin, w_query, w_kv, frame_attention_gain):
    tokens = space_time[0]
    time_ranges = lax.axis_size("tm") // SB
    state = incoming_state(tokens, w_lin, time_ranges) if time_ranges > 1 else None
    tiles = list(mixer(tokens, w_lin, gain_lin, state))
    tiles[0], w_query, w_kv, frame_attention_gain = lax.optimization_barrier(
        (tiles[0], w_query, w_kv, frame_attention_gain)
    )
    tiles = [swap(tile, apart) if apart else tile for apart, tile in zip(APART, tiles)]
    normed, *pairs = make_pairs(tiles, frame_attention_gain, w_kv)
    earlier_pairs = [shifted(part, "tm", 1) for part in pairs]
    query, *so_far = own_frame(normed, w_query, pairs)
    done = []
    for group, part in enumerate(earlier_pairs):
        done.append(earlier_frame(group, query, part, so_far, done))
    return done[-1][None]


def solution(mesh):
    placed = (P(("groups", "tm"), None, None), P(), P(), P(), P(), P())
    return jax.shard_map(
        body, mesh=mesh, in_specs=placed, out_specs=P(("groups", "tm"), None, None), check_vma=False
    )
```

```python
import functools
import math

import jax
import jax.numpy as jnp
from jax import lax
from jax.experimental import pallas as pl
from jax.experimental.pallas import tpu as pltpu
from jax.sharding import PartitionSpec as P

HEADS = 8
HD = 128
KVH = 2
SB = 16
SPAN = 128
GROUPS = ((0, 4), (4, 8))
PLANE = 4
HOPS = (
    (0, 0), (1, 0), (2, 0), (1, 2),
    (2, 2), (0, 2), (3, 0), (3, 3),
    (0, 3), (3, 1), (3, 2), (1, 3),
    (2, 3), (0, 1), (1, 1), (2, 1),
)


def place_after(place, hop, back=False):
    planes = SB // PLANE
    turn = planes - hop[0] if back else hop[0]
    if isinstance(place, int):
        return (place // PLANE + turn) % planes * PLANE + (place % PLANE ^ hop[1])
    plane = lax.rem(lax.div(place, PLANE) + turn, planes)
    return plane * PLANE + (lax.rem(place, PLANE) ^ hop[1])


epsilon = 1e-06
MIB = 1 << 20


def shifted(block, axis, distance):
    devices = range(lax.axis_size(axis))
    route = [(i - distance, i) for i in devices if i - distance in devices]
    return lax.ppermute(block, axis, route)


def dot(a, b):
    return jnp.dot(a, b, preferred_element_type=jnp.float32)


def dot_nt(a, b):
    return lax.dot_general(a, b, (((1,), (1,)), ((), ())), preferred_element_type=jnp.float32)


def dot_tn(a, b):
    return lax.dot_general(a, b, (((0,), (0,)), ((), ())), preferred_element_type=jnp.float32)


def head_lanes(head):
    return slice(head * HD, (head + 1) * HD)


def causal_mask():
    shape = (SPAN, SPAN)
    return lax.broadcasted_iota(jnp.int32, shape, 0) >= lax.broadcasted_iota(jnp.int32, shape, 1)


def mix_heads(query, key, value, states):
    rows = query.shape[0]
    causal = causal_mask()
    spans = [slice(start, start + SPAN) for start in range(0, rows, SPAN)]
    heads = range(query.shape[1] // HD)
    units = [(head, span) for head in heads for span in range(len(spans))]
    local, before, mixed = {}, {}, []
    for head, span in units:
        lanes, here = head_lanes(head), spans[span]
        scores = dot_nt(query[here, lanes], key[here, lanes])
        local[head, span] = jnp.where(causal, scores, 0.0).astype(jnp.bfloat16)
    for head in heads:
        lanes = head_lanes(head)
        state = states[head]
        for span, here in enumerate(spans):
            before[head, span] = state
            if span + 1 < len(spans):
                update = dot_tn(key[here, lanes], value[here, lanes])
                state = update if state is None else state + update
    for head, span in units:
        lanes, here = head_lanes(head), spans[span]
        if before[head, span] is None:
            out = dot(local[head, span], value[here, lanes])
        else:
            out = dot(
                jnp.concatenate([query[here, lanes], local[head, span]], axis=1),
                jnp.concatenate(
                    [before[head, span].astype(jnp.bfloat16), value[here, lanes]], axis=0
                ),
            )
        mixed.append((head, here, out))
    return mixed


def mixer_kernel(has_state, *refs):
    if has_state:
        state_ref, *refs = refs
    tokens_hbm, w_hbm, gain_ref, *refs = refs
    tiles, (tokens_ref, out_ref, *weights, tokens_in, weights_in, sent) = refs[:SB], refs[SB:]
    rows, width = tokens_ref.shape
    size = rows // SB
    place = lax.rem(lax.axis_index("tm"), SB)

    first = [pltpu.make_async_copy(tokens_hbm, tokens_ref, tokens_in)]
    copies = []
    for index, (low, high) in enumerate(GROUPS):
        here = []
        for part in range(3):
            columns = slice(part * width + low * HD, part * width + high * HD)
            here.append(
                pltpu.make_async_copy(
                    w_hbm.at[:, columns], weights[index].at[part], weights_in.at[index, part]
                )
            )
        copies.append(here)
    for copy in first + sum(copies, []):
        copy.start()
    gains = gain_ref[...].astype(jnp.float32).reshape(1, width)

    def project(index):
        for copy in copies[index]:
            copy.wait()
        tokens = tokens_ref[...]
        return [dot(tokens, weights[index][part]).astype(jnp.bfloat16) for part in range(3)]

    def mix(index, parts):
        low, high = GROUPS[index]
        states = [state_ref[head] if has_state else None for head in range(low, high)]
        for head, here, out in mix_heads(*parts, states):
            lanes = head_lanes(low + head)
            mean_square = jnp.mean(out * out, axis=-1, keepdims=True)
            normed = out * lax.rsqrt(mean_square + epsilon) * gains[:, lanes]
            residual = tokens_ref[here, lanes].astype(jnp.float32)
            out_ref[here, lanes] = (residual + normed).astype(jnp.bfloat16)

    first[0].wait()
    parts = project(0)
    for index in range(len(GROUPS)):
        upcoming = project(index + 1) if index + 1 < len(GROUPS) else None
        mix(index, parts)
        parts = upcoming
    leaving = []
    for slot, (hop, tile) in enumerate(zip(HOPS, tiles)):
        here = pl.ds(pl.multiple_of(place_after(place, hop) * size, size), size)
        leaving.append(pltpu.make_async_copy(out_ref.at[here], tile, sent.at[slot]))
        leaving[-1].start()
    for copy in leaving:
        copy.wait()


def mixer(tokens, w_lin, gain_lin, state):
    rows, width = tokens.shape
    hbm = pl.BlockSpec(memory_space=pl.ANY)
    vmem = pl.BlockSpec(memory_space=pltpu.VMEM)
    in_specs = [hbm, hbm, vmem]
    operands = [tokens, w_lin, gain_lin]
    if state is not None:
        operands.insert(0, state)
        in_specs.insert(0, vmem)
    return pl.pallas_call(
        functools.partial(mixer_kernel, state is not None),
        in_specs=in_specs,
        out_specs=[hbm] * SB,
        out_shape=[jax.ShapeDtypeStruct((rows // SB, width), jnp.bfloat16)] * SB,
        scratch_shapes=[pltpu.VMEM((rows, width), jnp.bfloat16)] * 2
        + [pltpu.VMEM((3, width, (high - low) * HD), jnp.bfloat16) for low, high in GROUPS]
        + [
            pltpu.SemaphoreType.DMA,
            pltpu.SemaphoreType.DMA((len(GROUPS), 3)),
            pltpu.SemaphoreType.DMA((SB,)),
        ],
        compiler_params=pltpu.CompilerParams(vmem_limit_bytes=56 * MIB),
        cost_estimate=pl.CostEstimate(
            flops=2 * rows * width * 3 * width + 8 * rows * SPAN * width,
            bytes_accessed=2 * (3 * width * width + 2 * rows * width),
            transcendentals=rows * HEADS,
        ),
        name="mixer",
    )(*operands)


def incoming_state(tokens, w_lin, time_ranges):
    rows, width = tokens.shape
    packed = dot(tokens, w_lin[:, width:]).astype(jnp.bfloat16).reshape(rows, 2, HEADS, HD)
    block_total = jnp.einsum(
        "nhd,nhe->hde", packed[:, 0], packed[:, 1], preferred_element_type=jnp.float32
    )
    within = lax.axis_index("tm") // SB

    def advance_hop(turn_index, running_total):
        moved = shifted(running_total + block_total, "tm", SB)
        return jnp.where(within > 0, moved, 0.0)

    return lax.fori_loop(0, time_ranges - 1, advance_hop, jnp.zeros_like(block_total))


def pairs_kernel(gain_ref, w_ref, *refs):
    tiles, normed_ref, outs = refs[:SB], refs[SB], refs[SB + 1 :]
    gain = gain_ref[...].astype(jnp.float32).reshape(1, -1)
    widened = jnp.concatenate([tile[...] for tile in tiles], axis=0).astype(jnp.float32)
    mean_square = jnp.mean(widened * widened, axis=-1, keepdims=True)
    normed = (widened * lax.rsqrt(mean_square + epsilon) * gain).astype(jnp.bfloat16)
    normed_ref[...] = normed
    pairs = dot(normed, w_ref[...]).astype(jnp.bfloat16)
    for head, out_ref in enumerate(outs):
        for start in range(0, pairs.shape[0], HD):
            here = slice(start, start + HD)
            out_ref[here, :HD] = pairs[here, head_lanes(head)].T
        out_ref[:, HD:] = pairs[:, head_lanes(KVH + head)]


def make_pairs(tiles, gain, w_kv):
    width, wide = w_kv.shape
    rows = sum(tile.shape[0] for tile in tiles)
    return pl.pallas_call(
        pairs_kernel,
        out_shape=[jax.ShapeDtypeStruct((rows, width), jnp.bfloat16)]
        + [jax.ShapeDtypeStruct((rows, wide // KVH), jnp.bfloat16)] * KVH,
        compiler_params=pltpu.CompilerParams(vmem_limit_bytes=16 * MIB),
        cost_estimate=pl.CostEstimate(
            flops=2 * rows * width * wide,
            bytes_accessed=2 * (2 * rows * width + width * wide + rows * wide),
            transcendentals=rows,
        ),
        name="pairs",
    )(gain, w_kv, *tiles)


SCORE_SCALE = math.log2(math.e) / math.sqrt(HD)
GROUP = HEADS // KVH


def key_and_value(ref):
    key = jnp.concatenate(
        [ref[start : start + HD, :HD] for start in range(0, ref.shape[0], HD)], axis=1
    )
    value = ref[:, HD:]
    return key, jnp.concatenate([value, jnp.ones_like(value)], axis=1)


def own_kernel(normed_ref, w_ref, *refs):
    both = [key_and_value(ref) for ref in refs[:KVH]]
    query_ref, sum_ref, total_ref, top_ref = refs[KVH:]
    columns = GROUP * HD

    def project(group):
        lanes = slice(group * columns, (group + 1) * columns)
        query = dot(normed_ref[...], w_ref[:, lanes]).astype(jnp.bfloat16)
        query_ref[:, lanes] = query
        return query

    queries = {0: project(0)}

    def scores_of(head):
        group = head // GROUP
        return dot(queries[group][:, head_lanes(head % GROUP)], both[group][0])

    scores = scores_of(0)
    for head in range(HEADS):
        if head % GROUP == 0 and head + GROUP < HEADS:
            queries[head // GROUP + 1] = project(head // GROUP + 1)
        upcoming = scores_of(head + 1) if head + 1 < HEADS else None
        lanes = head_lanes(head)
        largest = jnp.max(scores, axis=-1, keepdims=True)
        raised = jnp.exp2((scores - largest) * SCORE_SCALE).astype(jnp.bfloat16)
        summed = dot(raised, both[head // GROUP][1])
        sum_ref[:, lanes] = summed[:, :HD]
        total_ref[:, lanes] = summed[:, HD:]
        top_ref[:, lanes] = jnp.broadcast_to(largest * SCORE_SCALE, (scores.shape[0], HD))
        scores = upcoming


def own_frame(normed, w_query, pairs):
    rows, width = normed.shape
    return pl.pallas_call(
        own_kernel,
        out_shape=[jax.ShapeDtypeStruct((rows, width), jnp.bfloat16)]
        + [jax.ShapeDtypeStruct((rows, width), jnp.float32)] * 3,
        compiler_params=pltpu.CompilerParams(vmem_limit_bytes=32 * MIB),
        cost_estimate=pl.CostEstimate(
            flops=2 * rows * width * width + 4 * rows * rows * width,
            bytes_accessed=2 * width * width + 8 * rows * width,
            transcendentals=rows * rows * HEADS,
        ),
        name="own_frame",
    )(normed, w_query, *pairs)


def earlier_kernel(group, query_ref, pairs_ref, sum_ref, total_ref, top_ref, *refs):
    key, value = key_and_value(pairs_ref)
    index = lax.axis_index("tm")
    barred = jnp.where(index > 0, 0.0, -jnp.inf)
    place = lax.rem(index, SB)
    size = query_ref.shape[0] // SB
    starts = [pl.multiple_of(place_after(place, hop, True) * size, size) for hop in HOPS]
    columns = GROUP * HD
    last = group == KVH - 1
    copies = []
    if last:
        *done_refs, out_hbm, out_ref, sent = refs

        def leave(source, start):
            there = out_hbm.at[:, start : start + source.shape[1]]
            copies.append(pltpu.make_async_copy(source, there, sent.at[len(copies)]))
            copies[-1].start()

        for part, ref in enumerate(done_refs):
            leave(ref, part * columns)
    else:
        (out_ref,) = refs

    def scores_of(head):
        return dot(query_ref[:, head_lanes(group * GROUP + head)], key)

    scores = scores_of(0)
    for head in range(GROUP):
        lanes = head_lanes(group * GROUP + head)
        upcoming = scores_of(head + 1) if head + 1 < GROUP else None
        before = top_ref[:, lanes]
        here = jnp.max(scores, axis=-1, keepdims=True) * SCORE_SCALE + barred
        largest = jnp.maximum(jnp.broadcast_to(here, before.shape), before)
        below = jnp.concatenate([largest - barred] * (scores.shape[1] // HD), axis=1)
        raised = jnp.exp2(scores * SCORE_SCALE - below).astype(jnp.bfloat16)
        summed = dot(raised, value)
        share = jnp.exp2(before - largest)
        mixed = sum_ref[:, lanes] * share + summed[:, :HD]
        total = total_ref[:, lanes] * share + summed[:, HD:]
        mixed = (mixed / total).astype(jnp.bfloat16)
        for slot, start in enumerate(starts):
            there = pl.ds(start, size)
            out_ref[there, head_lanes(head)] = mixed[slot * size : (slot + 1) * size]
        if last and head % 2:
            start = (head - 1) * HD
            leave(out_ref.at[:, start : start + 2 * HD], group * columns + start)
        scores = upcoming
    for copy in copies:
        copy.wait()


def earlier_frame(group, query, pairs, so_far, done):
    rows, width = query.shape
    columns = GROUP * HD
    last = group == KVH - 1
    extra = dict(out_shape=jax.ShapeDtypeStruct((rows, columns), jnp.bfloat16))
    if last:
        extra = dict(
            out_shape=jax.ShapeDtypeStruct((rows, width), jnp.bfloat16),
            out_specs=pl.BlockSpec(memory_space=pl.ANY),
            scratch_shapes=[
                pltpu.VMEM((rows, columns), jnp.bfloat16),
                pltpu.SemaphoreType.DMA((KVH - 1 + GROUP // 2,)),
            ],
        )
    operands = [query, pairs, *so_far] + (done if last else [])
    return pl.pallas_call(
        functools.partial(earlier_kernel, group),
        compiler_params=pltpu.CompilerParams(vmem_limit_bytes=32 * MIB),
        cost_estimate=pl.CostEstimate(
            flops=4 * rows * rows * columns,
            bytes_accessed=20 * rows * columns,
            transcendentals=rows * rows * GROUP,
        ),
        name="earlier_frame",
        **extra,
    )(*operands)


def send(tile, hop):
    devices = lax.axis_size("tm")
    route = [(i, i - i % SB + place_after(i % SB, hop)) for i in range(devices)]
    return lax.ppermute(tile, "tm", route)


def body(space_time, w_lin, gain_lin, w_query, w_kv, frame_attention_gain):
    tokens = space_time[0]
    time_ranges = lax.axis_size("tm") // SB
    state = incoming_state(tokens, w_lin, time_ranges) if time_ranges > 1 else None
    tiles = list(mixer(tokens, w_lin, gain_lin, state))
    tiles[0], w_query, w_kv, frame_attention_gain = lax.optimization_barrier(
        (tiles[0], w_query, w_kv, frame_attention_gain)
    )
    tiles = [send(tile, hop) if any(hop) else tile for hop, tile in zip(HOPS, tiles)]
    normed, *pairs = make_pairs(tiles, frame_attention_gain, w_kv)
    earlier_pairs = [shifted(part, "tm", 1) for part in pairs]
    query, *so_far = own_frame(normed, w_query, pairs)
    done = []
    for group, part in enumerate(earlier_pairs):
        done.append(earlier_frame(group, query, part, so_far, done))
    return done[-1][None]


def solution(mesh):
    placed = (P(("groups", "tm"), None, None), P(), P(), P(), P(), P())
    return jax.shard_map(
        body, mesh=mesh, in_specs=placed, out_specs=P(("groups", "tm"), None, None), check_vma=False
    )
```

```python
import functools
import math

import jax
import jax.numpy as jnp
from jax import lax
from jax.experimental import pallas as pl
from jax.experimental.pallas import tpu as pltpu
from jax.sharding import PartitionSpec as P

HEADS = 8
HD = 128
KVH = 2
SB = 16
SPAN = 128
GROUPS = ((0, 4), (4, 8))
APART = (0, 10, 11, 14, 4, 15, 8, 5, 9, 2, 12, 6, 13, 3, 7, 1)
EARLY = SB // 2

epsilon = 1e-06
MIB = 1 << 20


def shifted(block, axis, distance):
    devices = range(lax.axis_size(axis))
    route = [(i - distance, i) for i in devices if i - distance in devices]
    return lax.ppermute(block, axis, route)


def dot(a, b):
    return jnp.dot(a, b, preferred_element_type=jnp.float32)


def dot_nt(a, b):
    return lax.dot_general(a, b, (((1,), (1,)), ((), ())), preferred_element_type=jnp.float32)


def dot_tn(a, b):
    return lax.dot_general(a, b, (((0,), (0,)), ((), ())), preferred_element_type=jnp.float32)


def head_lanes(head):
    return slice(head * HD, (head + 1) * HD)


def causal_mask():
    shape = (SPAN, SPAN)
    return lax.broadcasted_iota(jnp.int32, shape, 0) >= lax.broadcasted_iota(jnp.int32, shape, 1)


def mix_heads(query, key, value, states):
    rows = query.shape[0]
    causal = causal_mask()
    spans = [slice(start, start + SPAN) for start in range(0, rows, SPAN)]
    heads = range(query.shape[1] // HD)
    units = [(head, span) for head in heads for span in range(len(spans))]
    local, before, mixed = {}, {}, []
    for head, span in units:
        lanes, here = head_lanes(head), spans[span]
        scores = dot_nt(query[here, lanes], key[here, lanes])
        local[head, span] = jnp.where(causal, scores, 0.0).astype(jnp.bfloat16)
    for head in heads:
        lanes = head_lanes(head)
        state = states[head]
        for span, here in enumerate(spans):
            before[head, span] = state
            if span + 1 < len(spans):
                update = dot_tn(key[here, lanes], value[here, lanes])
                state = update if state is None else state + update
    for head, span in units:
        lanes, here = head_lanes(head), spans[span]
        if before[head, span] is None:
            out = dot(local[head, span], value[here, lanes])
        else:
            out = dot(
                jnp.concatenate([query[here, lanes], local[head, span]], axis=1),
                jnp.concatenate(
                    [before[head, span].astype(jnp.bfloat16), value[here, lanes]], axis=0
                ),
            )
        mixed.append((head, here, out))
    return mixed


def mixer_kernel(has_state, *refs):
    if has_state:
        state_ref, *refs = refs
    tokens_hbm, w_hbm, gain_ref, *refs = refs
    tiles, (tokens_ref, out_ref, *weights, tokens_in, weights_in, sent) = refs[:SB], refs[SB:]
    rows, width = tokens_ref.shape
    size = rows // SB
    place = lax.rem(lax.axis_index("tm"), SB)

    first = [pltpu.make_async_copy(tokens_hbm, tokens_ref, tokens_in)]
    copies = []
    for index, (low, high) in enumerate(GROUPS):
        here = []
        for part in range(3):
            columns = slice(part * width + low * HD, part * width + high * HD)
            here.append(
                pltpu.make_async_copy(
                    w_hbm.at[:, columns], weights[index].at[part], weights_in.at[index, part]
                )
            )
        copies.append(here)
    for copy in first + sum(copies, []):
        copy.start()
    gains = gain_ref[...].astype(jnp.float32).reshape(1, width)

    leaving = []

    def project(index):
        for copy in copies[index]:
            copy.wait()
        tokens = tokens_ref[...]
        return [dot(tokens, weights[index][part]).astype(jnp.bfloat16) for part in range(3)]

    def mix(index, parts):
        low, high = GROUPS[index]
        states = [state_ref[head] if has_state else None for head in range(low, high)]
        for head, here, out in mix_heads(*parts, states):
            lanes = head_lanes(low + head)
            mean_square = jnp.mean(out * out, axis=-1, keepdims=True)
            normed = out * lax.rsqrt(mean_square + epsilon) * gains[:, lanes]
            residual = tokens_ref[here, lanes].astype(jnp.float32)
            out_ref[here, lanes] = (residual + normed).astype(jnp.bfloat16)
        lanes = slice(low * HD, high * HD)
        for slot, (apart, tile) in enumerate(zip(APART, tiles)):
            here = pl.ds(pl.multiple_of((place ^ apart) * size, size), size)
            copy = pltpu.make_async_copy(
                out_ref.at[here, lanes], tile.at[:, lanes], sent.at[index, slot]
            )
            copy.start()
            leaving.append(copy)

    first[0].wait()
    parts = project(0)
    for index in range(len(GROUPS)):
        upcoming = project(index + 1) if index + 1 < len(GROUPS) else None
        mix(index, parts)
        parts = upcoming
    for copy in leaving:
        copy.wait()


def mixer(tokens, w_lin, gain_lin, state):
    rows, width = tokens.shape
    hbm = pl.BlockSpec(memory_space=pl.ANY)
    vmem = pl.BlockSpec(memory_space=pltpu.VMEM)
    in_specs = [hbm, hbm, vmem]
    operands = [tokens, w_lin, gain_lin]
    if state is not None:
        operands.insert(0, state)
        in_specs.insert(0, vmem)
    return pl.pallas_call(
        functools.partial(mixer_kernel, state is not None),
        in_specs=in_specs,
        out_specs=[hbm] * SB,
        out_shape=[jax.ShapeDtypeStruct((rows // SB, width), jnp.bfloat16)] * SB,
        scratch_shapes=[pltpu.VMEM((rows, width), jnp.bfloat16)] * 2
        + [pltpu.VMEM((3, width, (high - low) * HD), jnp.bfloat16) for low, high in GROUPS]
        + [
            pltpu.SemaphoreType.DMA,
            pltpu.SemaphoreType.DMA((len(GROUPS), 3)),
            pltpu.SemaphoreType.DMA((len(GROUPS), SB)),
        ],
        compiler_params=pltpu.CompilerParams(vmem_limit_bytes=62 * MIB),
        cost_estimate=pl.CostEstimate(
            flops=2 * rows * width * 3 * width + 8 * rows * SPAN * width,
            bytes_accessed=2 * (3 * width * width + 2 * rows * width),
            transcendentals=rows * HEADS,
        ),
        name="mixer",
    )(*operands)


def incoming_state(tokens, w_lin, time_ranges):
    rows, width = tokens.shape
    packed = dot(tokens, w_lin[:, width:]).astype(jnp.bfloat16).reshape(rows, 2, HEADS, HD)
    block_total = jnp.einsum(
        "nhd,nhe->hde", packed[:, 0], packed[:, 1], preferred_element_type=jnp.float32
    )
    within = lax.axis_index("tm") // SB

    def advance_hop(turn_index, running_total):
        moved = shifted(running_total + block_total, "tm", SB)
        return jnp.where(within > 0, moved, 0.0)

    return lax.fori_loop(0, time_ranges - 1, advance_hop, jnp.zeros_like(block_total))


def norm_rows(gain_ref, tiles):
    gain = gain_ref[...].astype(jnp.float32).reshape(1, -1)
    widened = jnp.concatenate([tile[...] for tile in tiles], axis=0).astype(jnp.float32)
    mean_square = jnp.mean(widened * widened, axis=-1, keepdims=True)
    return (widened * lax.rsqrt(mean_square + epsilon) * gain).astype(jnp.bfloat16)


def write_pairs(normed, w_ref, offset, outs):
    pairs = dot(normed, w_ref[...]).astype(jnp.bfloat16)
    rows = pairs.shape[0]
    for head, out_ref in enumerate(outs):
        for start in range(0, rows, HD):
            there = slice(offset + start, offset + start + HD)
            out_ref[there, :HD] = pairs[start : start + HD, head_lanes(head)].T
        out_ref[offset : offset + rows, HD:] = pairs[:, head_lanes(KVH + head)]


def early_kernel(gain_ref, w_kv_ref, w_query_ref, *refs):
    tiles, query_ref, outs = refs[:EARLY], refs[EARLY], refs[EARLY + 1 :]
    normed = norm_rows(gain_ref, tiles)
    write_pairs(normed, w_kv_ref, 0, outs)
    query_ref[...] = dot(normed, w_query_ref[...]).astype(jnp.bfloat16)


def pairs_kernel(gain_ref, w_kv_ref, *refs):
    late = SB - EARLY
    tiles, done, normed_ref, outs = refs[:late], refs[late:-KVH - 1], refs[-KVH - 1], refs[-KVH:]
    normed = norm_rows(gain_ref, tiles)
    normed_ref[...] = normed
    rows = done[0].shape[0]
    for done_ref, out_ref in zip(done, outs):
        out_ref[:rows] = done_ref[...]
    write_pairs(normed, w_kv_ref, rows, outs)


def make_early(tiles, gain, w_kv, w_query):
    width, wide = w_kv.shape
    rows = sum(tile.shape[0] for tile in tiles)
    return pl.pallas_call(
        early_kernel,
        out_shape=[jax.ShapeDtypeStruct((rows, w_query.shape[1]), jnp.bfloat16)]
        + [jax.ShapeDtypeStruct((rows, wide // KVH), jnp.bfloat16)] * KVH,
        compiler_params=pltpu.CompilerParams(vmem_limit_bytes=16 * MIB),
        cost_estimate=pl.CostEstimate(
            flops=2 * rows * width * (wide + width),
            bytes_accessed=2 * (2 * rows * width + width * wide + width * width),
            transcendentals=rows,
        ),
        name="early_rows",
    )(gain, w_kv, w_query, *tiles)


def make_pairs(tiles, gain, w_kv, done):
    width, wide = w_kv.shape
    rows = sum(tile.shape[0] for tile in tiles)
    total = rows + done[0].shape[0]
    return pl.pallas_call(
        pairs_kernel,
        out_shape=[jax.ShapeDtypeStruct((rows, width), jnp.bfloat16)]
        + [jax.ShapeDtypeStruct((total, wide // KVH), jnp.bfloat16)] * KVH,
        compiler_params=pltpu.CompilerParams(vmem_limit_bytes=16 * MIB),
        cost_estimate=pl.CostEstimate(
            flops=2 * rows * width * wide,
            bytes_accessed=2 * (2 * rows * width + width * wide + rows * wide),
            transcendentals=rows,
        ),
        name="pairs",
    )(gain, w_kv, *tiles, *done)


SCORE_SCALE = math.log2(math.e) / math.sqrt(HD)
GROUP = HEADS // KVH


def key_and_value(ref):
    key = jnp.concatenate(
        [ref[start : start + HD, :HD] for start in range(0, ref.shape[0], HD)], axis=1
    )
    value = ref[:, HD:]
    return key, jnp.concatenate([value, jnp.ones_like(value)], axis=1)


def own_kernel(normed_ref, w_ref, early_ref, *refs):
    both = [key_and_value(ref) for ref in refs[:KVH]]
    query_ref, sum_ref, total_ref, top_ref = refs[KVH:]
    columns = GROUP * HD

    def project(group):
        lanes = slice(group * columns, (group + 1) * columns)
        late = dot(normed_ref[...], w_ref[:, lanes]).astype(jnp.bfloat16)
        query = jnp.concatenate([early_ref[:, lanes], late], axis=0)
        query_ref[:, lanes] = query
        return query

    queries = {0: project(0)}

    def scores_of(head):
        group = head // GROUP
        return dot(queries[group][:, head_lanes(head % GROUP)], both[group][0])

    scores = scores_of(0)
    for head in range(HEADS):
        if head % GROUP == 0 and head + GROUP < HEADS:
            queries[head // GROUP + 1] = project(head // GROUP + 1)
        upcoming = scores_of(head + 1) if head + 1 < HEADS else None
        lanes = head_lanes(head)
        largest = jnp.max(scores, axis=-1, keepdims=True)
        raised = jnp.exp2((scores - largest) * SCORE_SCALE).astype(jnp.bfloat16)
        summed = dot(raised, both[head // GROUP][1])
        sum_ref[:, lanes] = summed[:, :HD]
        total_ref[:, lanes] = summed[:, HD:]
        top_ref[:, lanes] = jnp.broadcast_to(largest * SCORE_SCALE, (scores.shape[0], HD))
        scores = upcoming


def own_frame(normed, w_query, early, pairs):
    rows, width = pairs[0].shape[0], normed.shape[1]
    return pl.pallas_call(
        own_kernel,
        out_shape=[jax.ShapeDtypeStruct((rows, width), jnp.bfloat16)]
        + [jax.ShapeDtypeStruct((rows, width), jnp.float32)] * 3,
        compiler_params=pltpu.CompilerParams(vmem_limit_bytes=32 * MIB),
        cost_estimate=pl.CostEstimate(
            flops=2 * rows * width * width + 4 * rows * rows * width,
            bytes_accessed=2 * width * width + 8 * rows * width,
            transcendentals=rows * rows * HEADS,
        ),
        name="own_frame",
    )(normed, w_query, early, *pairs)


def earlier_kernel(group, query_ref, pairs_ref, sum_ref, total_ref, top_ref, *refs):
    key, value = key_and_value(pairs_ref)
    index = lax.axis_index("tm")
    barred = jnp.where(index > 0, 0.0, -jnp.inf)
    place = lax.rem(index, SB)
    size = query_ref.shape[0] // SB
    columns = GROUP * HD
    last = group == KVH - 1
    copies = []
    if last:
        *done_refs, out_hbm, out_ref, sent = refs

        def leave(source, start):
            there = out_hbm.at[:, start : start + source.shape[1]]
            copies.append(pltpu.make_async_copy(source, there, sent.at[len(copies)]))
            copies[-1].start()

        for part, ref in enumerate(done_refs):
            leave(ref, part * columns)
    else:
        (out_ref,) = refs

    def scores_of(head):
        return dot(query_ref[:, head_lanes(group * GROUP + head)], key)

    scores = scores_of(0)
    for head in range(GROUP):
        lanes = head_lanes(group * GROUP + head)
        upcoming = scores_of(head + 1) if head + 1 < GROUP else None
        before = top_ref[:, lanes]
        here = jnp.max(scores, axis=-1, keepdims=True) * SCORE_SCALE + barred
        largest = jnp.maximum(jnp.broadcast_to(here, before.shape), before)
        below = jnp.concatenate([largest - barred] * (scores.shape[1] // HD), axis=1)
        raised = jnp.exp2(scores * SCORE_SCALE - below).astype(jnp.bfloat16)
        summed = dot(raised, value)
        share = jnp.exp2(before - largest)
        mixed = sum_ref[:, lanes] * share + summed[:, :HD]
        total = total_ref[:, lanes] * share + summed[:, HD:]
        mixed = (mixed / total).astype(jnp.bfloat16)
        for slot, apart in enumerate(APART):
            there = pl.ds(pl.multiple_of((place ^ apart) * size, size), size)
            out_ref[there, head_lanes(head)] = mixed[slot * size : (slot + 1) * size]
        if last and head % 2:
            start = (head - 1) * HD
            leave(out_ref.at[:, start : start + 2 * HD], group * columns + start)
        scores = upcoming
    for copy in copies:
        copy.wait()


def earlier_frame(group, query, pairs, so_far, done):
    rows, width = query.shape
    columns = GROUP * HD
    last = group == KVH - 1
    extra = dict(out_shape=jax.ShapeDtypeStruct((rows, columns), jnp.bfloat16))
    if last:
        extra = dict(
            out_shape=jax.ShapeDtypeStruct((rows, width), jnp.bfloat16),
            out_specs=pl.BlockSpec(memory_space=pl.ANY),
            scratch_shapes=[
                pltpu.VMEM((rows, columns), jnp.bfloat16),
                pltpu.SemaphoreType.DMA((KVH - 1 + GROUP // 2,)),
            ],
        )
    operands = [query, pairs, *so_far] + (done if last else [])
    return pl.pallas_call(
        functools.partial(earlier_kernel, group),
        compiler_params=pltpu.CompilerParams(vmem_limit_bytes=32 * MIB),
        cost_estimate=pl.CostEstimate(
            flops=4 * rows * rows * columns,
            bytes_accessed=20 * rows * columns,
            transcendentals=rows * rows * GROUP,
        ),
        name="earlier_frame",
        **extra,
    )(*operands)


def swap(tile, apart):
    devices = lax.axis_size("tm")
    route = [(i, i - i % SB + (i % SB ^ apart)) for i in range(devices)]
    return lax.ppermute(tile, "tm", route)


def body(space_time, w_lin, gain_lin, w_query, w_kv, frame_attention_gain):
    tokens = space_time[0]
    time_ranges = lax.axis_size("tm") // SB
    state = incoming_state(tokens, w_lin, time_ranges) if time_ranges > 1 else None
    tiles = mixer(tokens, w_lin, gain_lin, state)
    tiles = [swap(tile, apart) if apart else tile for apart, tile in zip(APART, tiles)]
    early, *done = make_early(tiles[:EARLY], frame_attention_gain, w_kv, w_query)
    normed, *pairs = make_pairs(tiles[EARLY:], frame_attention_gain, w_kv, done)
    earlier_pairs = [shifted(part, "tm", 1) for part in pairs]
    query, *so_far = own_frame(normed, w_query, early, pairs)
    done = []
    for group, part in enumerate(earlier_pairs):
        done.append(earlier_frame(group, query, part, so_far, done))
    return done[-1][None]


def solution(mesh):
    placed = (P(("groups", "tm"), None, None), P(), P(), P(), P(), P())
    return jax.shard_map(
        body, mesh=mesh, in_specs=placed, out_specs=P(("groups", "tm"), None, None), check_vma=False
    )
```

```python
import functools
import math

import jax
import jax.numpy as jnp
from jax import lax
from jax.experimental import pallas as pl
from jax.experimental.pallas import tpu as pltpu
from jax.sharding import PartitionSpec as P

HEADS = 8
HD = 128
KVH = 2
SB = 16
SPAN = 128
GROUPS = ((0, 4), (4, 8))
APART = (0, 5, 11, 8, 4, 14, 10, 15, 9, 2, 12, 6, 13, 3, 7, 1)
EARLY = SB // 2

epsilon = 1e-06
MIB = 1 << 20


def shifted(block, axis, distance):
    devices = range(lax.axis_size(axis))
    route = [(i - distance, i) for i in devices if i - distance in devices]
    return lax.ppermute(block, axis, route)


def dot(a, b):
    return jnp.dot(a, b, preferred_element_type=jnp.float32)


def dot_nt(a, b):
    return lax.dot_general(a, b, (((1,), (1,)), ((), ())), preferred_element_type=jnp.float32)


def dot_tn(a, b):
    return lax.dot_general(a, b, (((0,), (0,)), ((), ())), preferred_element_type=jnp.float32)


def head_lanes(head):
    return slice(head * HD, (head + 1) * HD)


def causal_mask():
    shape = (SPAN, SPAN)
    return lax.broadcasted_iota(jnp.int32, shape, 0) >= lax.broadcasted_iota(jnp.int32, shape, 1)


def mix_heads(query, key, value, states):
    rows = query.shape[0]
    causal = causal_mask()
    spans = [slice(start, start + SPAN) for start in range(0, rows, SPAN)]
    heads = range(query.shape[1] // HD)
    units = [(head, span) for head in heads for span in range(len(spans))]
    local, before, mixed = {}, {}, []
    for head, span in units:
        lanes, here = head_lanes(head), spans[span]
        scores = dot_nt(query[here, lanes], key[here, lanes])
        local[head, span] = jnp.where(causal, scores, 0.0).astype(jnp.bfloat16)
    for head in heads:
        lanes = head_lanes(head)
        state = states[head]
        for span, here in enumerate(spans):
            before[head, span] = state
            if span + 1 < len(spans):
                update = dot_tn(key[here, lanes], value[here, lanes])
                state = update if state is None else state + update
    for head, span in units:
        lanes, here = head_lanes(head), spans[span]
        if before[head, span] is None:
            out = dot(local[head, span], value[here, lanes])
        else:
            out = dot(
                jnp.concatenate([query[here, lanes], local[head, span]], axis=1),
                jnp.concatenate(
                    [before[head, span].astype(jnp.bfloat16), value[here, lanes]], axis=0
                ),
            )
        mixed.append((head, here, out))
    return mixed


def mixer_kernel(has_state, *refs):
    if has_state:
        state_ref, *refs = refs
    tokens_hbm, w_hbm, gain_ref, *refs = refs
    tiles, (tokens_ref, out_ref, *weights, tokens_in, weights_in, sent) = refs[:SB], refs[SB:]
    rows, width = tokens_ref.shape
    size = rows // SB
    place = lax.rem(lax.axis_index("tm"), SB)

    first = [pltpu.make_async_copy(tokens_hbm, tokens_ref, tokens_in)]
    copies = []
    for index, (low, high) in enumerate(GROUPS):
        here = []
        for part in range(3):
            columns = slice(part * width + low * HD, part * width + high * HD)
            here.append(
                pltpu.make_async_copy(
                    w_hbm.at[:, columns], weights[index].at[part], weights_in.at[index, part]
                )
            )
        copies.append(here)
    for copy in first + sum(copies, []):
        copy.start()
    gains = gain_ref[...].astype(jnp.float32).reshape(1, width)

    leaving = []

    def project(index):
        for copy in copies[index]:
            copy.wait()
        tokens = tokens_ref[...]
        return [dot(tokens, weights[index][part]).astype(jnp.bfloat16) for part in range(3)]

    def mix(index, parts):
        low, high = GROUPS[index]
        states = [state_ref[head] if has_state else None for head in range(low, high)]
        for head, here, out in mix_heads(*parts, states):
            lanes = head_lanes(low + head)
            mean_square = jnp.mean(out * out, axis=-1, keepdims=True)
            normed = out * lax.rsqrt(mean_square + epsilon) * gains[:, lanes]
            residual = tokens_ref[here, lanes].astype(jnp.float32)
            out_ref[here, lanes] = (residual + normed).astype(jnp.bfloat16)
        lanes = slice(low * HD, high * HD)
        for slot, (apart, tile) in enumerate(zip(APART, tiles)):
            here = pl.ds(pl.multiple_of((place ^ apart) * size, size), size)
            copy = pltpu.make_async_copy(
                out_ref.at[here, lanes], tile.at[:, lanes], sent.at[index, slot]
            )
            copy.start()
            leaving.append(copy)

    first[0].wait()
    parts = project(0)
    for index in range(len(GROUPS)):
        upcoming = project(index + 1) if index + 1 < len(GROUPS) else None
        mix(index, parts)
        parts = upcoming
    for copy in leaving:
        copy.wait()


def mixer(tokens, w_lin, gain_lin, state):
    rows, width = tokens.shape
    hbm = pl.BlockSpec(memory_space=pl.ANY)
    vmem = pl.BlockSpec(memory_space=pltpu.VMEM)
    in_specs = [hbm, hbm, vmem]
    operands = [tokens, w_lin, gain_lin]
    if state is not None:
        operands.insert(0, state)
        in_specs.insert(0, vmem)
    return pl.pallas_call(
        functools.partial(mixer_kernel, state is not None),
        in_specs=in_specs,
        out_specs=[hbm] * SB,
        out_shape=[jax.ShapeDtypeStruct((rows // SB, width), jnp.bfloat16)] * SB,
        scratch_shapes=[pltpu.VMEM((rows, width), jnp.bfloat16)] * 2
        + [pltpu.VMEM((3, width, (high - low) * HD), jnp.bfloat16) for low, high in GROUPS]
        + [
            pltpu.SemaphoreType.DMA,
            pltpu.SemaphoreType.DMA((len(GROUPS), 3)),
            pltpu.SemaphoreType.DMA((len(GROUPS), SB)),
        ],
        compiler_params=pltpu.CompilerParams(vmem_limit_bytes=60 * MIB),
        cost_estimate=pl.CostEstimate(
            flops=2 * rows * width * 3 * width + 8 * rows * SPAN * width,
            bytes_accessed=2 * (3 * width * width + 2 * rows * width),
            transcendentals=rows * HEADS,
        ),
        name="mixer",
    )(*operands)


def incoming_state(tokens, w_lin, time_ranges):
    rows, width = tokens.shape
    packed = dot(tokens, w_lin[:, width:]).astype(jnp.bfloat16).reshape(rows, 2, HEADS, HD)
    block_total = jnp.einsum(
        "nhd,nhe->hde", packed[:, 0], packed[:, 1], preferred_element_type=jnp.float32
    )
    within = lax.axis_index("tm") // SB

    def advance_hop(turn_index, running_total):
        moved = shifted(running_total + block_total, "tm", SB)
        return jnp.where(within > 0, moved, 0.0)

    return lax.fori_loop(0, time_ranges - 1, advance_hop, jnp.zeros_like(block_total))


def norm_rows(gain_ref, tiles):
    gain = gain_ref[...].astype(jnp.float32).reshape(1, -1)
    widened = jnp.concatenate([tile[...] for tile in tiles], axis=0).astype(jnp.float32)
    mean_square = jnp.mean(widened * widened, axis=-1, keepdims=True)
    return (widened * lax.rsqrt(mean_square + epsilon) * gain).astype(jnp.bfloat16)


def write_pairs(normed, w_ref, offset, outs):
    pairs = dot(normed, w_ref[...]).astype(jnp.bfloat16)
    rows = pairs.shape[0]
    for head, out_ref in enumerate(outs):
        for start in range(0, rows, HD):
            there = slice(offset + start, offset + start + HD)
            out_ref[there, :HD] = pairs[start : start + HD, head_lanes(head)].T
        out_ref[offset : offset + rows, HD:] = pairs[:, head_lanes(KVH + head)]


def early_kernel(gain_ref, w_kv_ref, w_query_ref, *refs):
    tiles, query_ref, outs = refs[:EARLY], refs[EARLY], refs[EARLY + 1 :]
    normed = norm_rows(gain_ref, tiles)
    write_pairs(normed, w_kv_ref, 0, outs)
    query_ref[...] = dot(normed, w_query_ref[...]).astype(jnp.bfloat16)


def pairs_kernel(gain_ref, w_kv_ref, *refs):
    late = SB - EARLY
    tiles, done, normed_ref, outs = refs[:late], refs[late:-KVH - 1], refs[-KVH - 1], refs[-KVH:]
    normed = norm_rows(gain_ref, tiles)
    normed_ref[...] = normed
    rows = done[0].shape[0]
    for done_ref, out_ref in zip(done, outs):
        out_ref[:rows] = done_ref[...]
    write_pairs(normed, w_kv_ref, rows, outs)


def make_early(tiles, gain, w_kv, w_query):
    width, wide = w_kv.shape
    rows = sum(tile.shape[0] for tile in tiles)
    return pl.pallas_call(
        early_kernel,
        out_shape=[jax.ShapeDtypeStruct((rows, w_query.shape[1]), jnp.bfloat16)]
        + [jax.ShapeDtypeStruct((rows, wide // KVH), jnp.bfloat16)] * KVH,
        compiler_params=pltpu.CompilerParams(vmem_limit_bytes=16 * MIB),
        cost_estimate=pl.CostEstimate(
            flops=2 * rows * width * (wide + width),
            bytes_accessed=2 * (2 * rows * width + width * wide + width * width),
            transcendentals=rows,
        ),
        name="early_rows",
    )(gain, w_kv, w_query, *tiles)


def make_pairs(tiles, gain, w_kv, done):
    width, wide = w_kv.shape
    rows = sum(tile.shape[0] for tile in tiles)
    total = rows + done[0].shape[0]
    return pl.pallas_call(
        pairs_kernel,
        out_shape=[jax.ShapeDtypeStruct((rows, width), jnp.bfloat16)]
        + [jax.ShapeDtypeStruct((total, wide // KVH), jnp.bfloat16)] * KVH,
        compiler_params=pltpu.CompilerParams(vmem_limit_bytes=16 * MIB),
        cost_estimate=pl.CostEstimate(
            flops=2 * rows * width * wide,
            bytes_accessed=2 * (2 * rows * width + width * wide + rows * wide),
            transcendentals=rows,
        ),
        name="pairs",
    )(gain, w_kv, *tiles, *done)


SCORE_SCALE = math.log2(math.e) / math.sqrt(HD)
GROUP = HEADS // KVH


def key_and_value(ref):
    key = jnp.concatenate(
        [ref[start : start + HD, :HD] for start in range(0, ref.shape[0], HD)], axis=1
    )
    value = ref[:, HD:]
    return key, jnp.concatenate([value, jnp.ones_like(value)], axis=1)


def own_kernel(normed_ref, w_ref, early_ref, *refs):
    both = [key_and_value(ref) for ref in refs[:KVH]]
    query_ref, sum_ref, total_ref, top_ref = refs[KVH:]
    columns = GROUP * HD

    def project(group):
        lanes = slice(group * columns, (group + 1) * columns)
        late = dot(normed_ref[...], w_ref[:, lanes]).astype(jnp.bfloat16)
        query = jnp.concatenate([early_ref[:, lanes], late], axis=0)
        query_ref[:, lanes] = query
        return query

    queries = {0: project(0)}

    def scores_of(head):
        group = head // GROUP
        return dot(queries[group][:, head_lanes(head % GROUP)], both[group][0])

    scores = scores_of(0)
    for head in range(HEADS):
        if head % GROUP == 0 and head + GROUP < HEADS:
            queries[head // GROUP + 1] = project(head // GROUP + 1)
        upcoming = scores_of(head + 1) if head + 1 < HEADS else None
        lanes = head_lanes(head)
        largest = jnp.max(scores, axis=-1, keepdims=True)
        raised = jnp.exp2((scores - largest) * SCORE_SCALE).astype(jnp.bfloat16)
        summed = dot(raised, both[head // GROUP][1])
        sum_ref[:, lanes] = summed[:, :HD]
        total_ref[:, lanes] = summed[:, HD:]
        top_ref[:, lanes] = jnp.broadcast_to(largest * SCORE_SCALE, (scores.shape[0], HD))
        scores = upcoming


def own_frame(normed, w_query, early, pairs):
    rows, width = pairs[0].shape[0], normed.shape[1]
    return pl.pallas_call(
        own_kernel,
        out_shape=[jax.ShapeDtypeStruct((rows, width), jnp.bfloat16)]
        + [jax.ShapeDtypeStruct((rows, width), jnp.float32)] * 3,
        compiler_params=pltpu.CompilerParams(vmem_limit_bytes=32 * MIB),
        cost_estimate=pl.CostEstimate(
            flops=2 * rows * width * width + 4 * rows * rows * width,
            bytes_accessed=2 * width * width + 8 * rows * width,
            transcendentals=rows * rows * HEADS,
        ),
        name="own_frame",
    )(normed, w_query, early, *pairs)


def earlier_kernel(group, query_ref, pairs_ref, sum_ref, total_ref, top_ref, *refs):
    key, value = key_and_value(pairs_ref)
    index = lax.axis_index("tm")
    barred = jnp.where(index > 0, 0.0, -jnp.inf)
    place = lax.rem(index, SB)
    size = query_ref.shape[0] // SB
    columns = GROUP * HD
    last = group == KVH - 1
    copies = []
    if last:
        *done_refs, out_hbm, out_ref, sent = refs

        def leave(source, start):
            there = out_hbm.at[:, start : start + source.shape[1]]
            copies.append(pltpu.make_async_copy(source, there, sent.at[len(copies)]))
            copies[-1].start()

        for part, ref in enumerate(done_refs):
            leave(ref, part * columns)
    else:
        (out_ref,) = refs

    def scores_of(head):
        return dot(query_ref[:, head_lanes(group * GROUP + head)], key)

    scores = scores_of(0)
    for head in range(GROUP):
        lanes = head_lanes(group * GROUP + head)
        upcoming = scores_of(head + 1) if head + 1 < GROUP else None
        before = top_ref[:, lanes]
        here = jnp.max(scores, axis=-1, keepdims=True) * SCORE_SCALE + barred
        largest = jnp.maximum(jnp.broadcast_to(here, before.shape), before)
        below = jnp.concatenate([largest - barred] * (scores.shape[1] // HD), axis=1)
        raised = jnp.exp2(scores * SCORE_SCALE - below).astype(jnp.bfloat16)
        summed = dot(raised, value)
        share = jnp.exp2(before - largest)
        mixed = sum_ref[:, lanes] * share + summed[:, :HD]
        total = total_ref[:, lanes] * share + summed[:, HD:]
        mixed = (mixed / total).astype(jnp.bfloat16)
        for slot, apart in enumerate(APART):
            there = pl.ds(pl.multiple_of((place ^ apart) * size, size), size)
            out_ref[there, head_lanes(head)] = mixed[slot * size : (slot + 1) * size]
        if last and head % 2:
            start = (head - 1) * HD
            leave(out_ref.at[:, start : start + 2 * HD], group * columns + start)
        scores = upcoming
    for copy in copies:
        copy.wait()


def earlier_frame(group, query, pairs, so_far, done):
    rows, width = query.shape
    columns = GROUP * HD
    last = group == KVH - 1
    extra = dict(out_shape=jax.ShapeDtypeStruct((rows, columns), jnp.bfloat16))
    if last:
        extra = dict(
            out_shape=jax.ShapeDtypeStruct((rows, width), jnp.bfloat16),
            out_specs=pl.BlockSpec(memory_space=pl.ANY),
            scratch_shapes=[
                pltpu.VMEM((rows, columns), jnp.bfloat16),
                pltpu.SemaphoreType.DMA((KVH - 1 + GROUP // 2,)),
            ],
        )
    operands = [query, pairs, *so_far] + (done if last else [])
    return pl.pallas_call(
        functools.partial(earlier_kernel, group),
        compiler_params=pltpu.CompilerParams(vmem_limit_bytes=32 * MIB),
        cost_estimate=pl.CostEstimate(
            flops=4 * rows * rows * columns,
            bytes_accessed=20 * rows * columns,
            transcendentals=rows * rows * GROUP,
        ),
        name="earlier_frame",
        **extra,
    )(*operands)


def swap(tile, apart):
    devices = lax.axis_size("tm")
    route = [(i, i - i % SB + (i % SB ^ apart)) for i in range(devices)]
    return lax.ppermute(tile, "tm", route)


def body(space_time, w_lin, gain_lin, w_query, w_kv, frame_attention_gain):
    tokens = space_time[0]
    time_ranges = lax.axis_size("tm") // SB
    state = incoming_state(tokens, w_lin, time_ranges) if time_ranges > 1 else None
    tiles = mixer(tokens, w_lin, gain_lin, state)
    tiles = [swap(tile, apart) if apart else tile for apart, tile in zip(APART, tiles)]
    early, *done = make_early(tiles[:EARLY], frame_attention_gain, w_kv, w_query)
    normed, *pairs = make_pairs(tiles[EARLY:], frame_attention_gain, w_kv, done)
    earlier_pairs = [shifted(part, "tm", 1) for part in pairs]
    query, *so_far = own_frame(normed, w_query, early, pairs)
    done = []
    for group, part in enumerate(earlier_pairs):
        done.append(earlier_frame(group, query, part, so_far, done))
    return done[-1][None]


def solution(mesh):
    placed = (P(("groups", "tm"), None, None), P(), P(), P(), P(), P())
    return jax.shard_map(
        body, mesh=mesh, in_specs=placed, out_specs=P(("groups", "tm"), None, None), check_vma=False
    )
```

```python
import functools
import math

import jax
import jax.numpy as jnp
from jax import lax
from jax.experimental import pallas as pl
from jax.experimental.pallas import tpu as pltpu
from jax.sharding import PartitionSpec as P

HEADS = 8
HD = 128
KVH = 2
SB = 16
SPAN = 128
GROUPS = ((0, 4), (4, 8))
APART = (0, 5, 11, 8, 4, 14, 10, 15, 9, 12, 13, 6, 7, 2, 3, 1)
EARLY = SB // 2

epsilon = 1e-06
MIB = 1 << 20


def shifted(block, axis, distance):
    devices = range(lax.axis_size(axis))
    route = [(i - distance, i) for i in devices if i - distance in devices]
    return lax.ppermute(block, axis, route)


def dot(a, b):
    return jnp.dot(a, b, preferred_element_type=jnp.float32)


def dot_nt(a, b):
    return lax.dot_general(a, b, (((1,), (1,)), ((), ())), preferred_element_type=jnp.float32)


def dot_tn(a, b):
    return lax.dot_general(a, b, (((0,), (0,)), ((), ())), preferred_element_type=jnp.float32)


def head_lanes(head):
    return slice(head * HD, (head + 1) * HD)


def causal_mask():
    shape = (SPAN, SPAN)
    return lax.broadcasted_iota(jnp.int32, shape, 0) >= lax.broadcasted_iota(jnp.int32, shape, 1)


def mix_heads(query, key, value, states):
    rows = query.shape[0]
    causal = causal_mask()
    spans = [slice(start, start + SPAN) for start in range(0, rows, SPAN)]
    heads = range(query.shape[1] // HD)
    units = [(head, span) for head in heads for span in range(len(spans))]
    local, before, mixed = {}, {}, []
    for head, span in units:
        lanes, here = head_lanes(head), spans[span]
        scores = dot_nt(query[here, lanes], key[here, lanes])
        local[head, span] = jnp.where(causal, scores, 0.0).astype(jnp.bfloat16)
    for head in heads:
        lanes = head_lanes(head)
        state = states[head]
        for span, here in enumerate(spans):
            before[head, span] = state
            if span + 1 < len(spans):
                update = dot_tn(key[here, lanes], value[here, lanes])
                state = update if state is None else state + update
    for head, span in units:
        lanes, here = head_lanes(head), spans[span]
        if before[head, span] is None:
            out = dot(local[head, span], value[here, lanes])
        else:
            out = dot(
                jnp.concatenate([query[here, lanes], local[head, span]], axis=1),
                jnp.concatenate(
                    [before[head, span].astype(jnp.bfloat16), value[here, lanes]], axis=0
                ),
            )
        mixed.append((head, here, out))
    return mixed


def mixer_kernel(has_state, *refs):
    if has_state:
        state_ref, *refs = refs
    tokens_hbm, w_hbm, gain_ref, *refs = refs
    tiles, (tokens_ref, out_ref, *weights, tokens_in, weights_in, sent) = refs[:SB], refs[SB:]
    rows, width = tokens_ref.shape
    size = rows // SB
    place = lax.rem(lax.axis_index("tm"), SB)

    first = [pltpu.make_async_copy(tokens_hbm, tokens_ref, tokens_in)]
    copies = []
    for index, (low, high) in enumerate(GROUPS):
        here = []
        for part in range(3):
            columns = slice(part * width + low * HD, part * width + high * HD)
            here.append(
                pltpu.make_async_copy(
                    w_hbm.at[:, columns], weights[index].at[part], weights_in.at[index, part]
                )
            )
        copies.append(here)
    for copy in first + sum(copies, []):
        copy.start()
    gains = gain_ref[...].astype(jnp.float32).reshape(1, width)

    leaving = []

    def project(index):
        for copy in copies[index]:
            copy.wait()
        tokens = tokens_ref[...]
        return [dot(tokens, weights[index][part]).astype(jnp.bfloat16) for part in range(3)]

    def mix(index, parts):
        low, high = GROUPS[index]
        states = [state_ref[head] if has_state else None for head in range(low, high)]
        for head, here, out in mix_heads(*parts, states):
            lanes = head_lanes(low + head)
            mean_square = jnp.mean(out * out, axis=-1, keepdims=True)
            normed = out * lax.rsqrt(mean_square + epsilon) * gains[:, lanes]
            residual = tokens_ref[here, lanes].astype(jnp.float32)
            out_ref[here, lanes] = (residual + normed).astype(jnp.bfloat16)
        lanes = slice(low * HD, high * HD)
        for slot, (apart, tile) in enumerate(zip(APART, tiles)):
            here = pl.ds(pl.multiple_of((place ^ apart) * size, size), size)
            copy = pltpu.make_async_copy(
                out_ref.at[here, lanes], tile.at[:, lanes], sent.at[index, slot]
            )
            copy.start()
            leaving.append(copy)

    first[0].wait()
    parts = project(0)
    for index in range(len(GROUPS)):
        upcoming = project(index + 1) if index + 1 < len(GROUPS) else None
        mix(index, parts)
        parts = upcoming
    for copy in leaving:
        copy.wait()


def mixer(tokens, w_lin, gain_lin, state):
    rows, width = tokens.shape
    hbm = pl.BlockSpec(memory_space=pl.ANY)
    vmem = pl.BlockSpec(memory_space=pltpu.VMEM)
    in_specs = [hbm, hbm, vmem]
    operands = [tokens, w_lin, gain_lin]
    if state is not None:
        operands.insert(0, state)
        in_specs.insert(0, vmem)
    return pl.pallas_call(
        functools.partial(mixer_kernel, state is not None),
        in_specs=in_specs,
        out_specs=[hbm] * SB,
        out_shape=[jax.ShapeDtypeStruct((rows // SB, width), jnp.bfloat16)] * SB,
        scratch_shapes=[pltpu.VMEM((rows, width), jnp.bfloat16)] * 2
        + [pltpu.VMEM((3, width, (high - low) * HD), jnp.bfloat16) for low, high in GROUPS]
        + [
            pltpu.SemaphoreType.DMA,
            pltpu.SemaphoreType.DMA((len(GROUPS), 3)),
            pltpu.SemaphoreType.DMA((len(GROUPS), SB)),
        ],
        compiler_params=pltpu.CompilerParams(vmem_limit_bytes=60 * MIB),
        cost_estimate=pl.CostEstimate(
            flops=2 * rows * width * 3 * width + 8 * rows * SPAN * width,
            bytes_accessed=2 * (3 * width * width + 2 * rows * width),
            transcendentals=rows * HEADS,
        ),
        name="mixer",
    )(*operands)


def incoming_state(tokens, w_lin, time_ranges):
    rows, width = tokens.shape
    packed = dot(tokens, w_lin[:, width:]).astype(jnp.bfloat16).reshape(rows, 2, HEADS, HD)
    block_total = jnp.einsum(
        "nhd,nhe->hde", packed[:, 0], packed[:, 1], preferred_element_type=jnp.float32
    )
    within = lax.axis_index("tm") // SB

    def advance_hop(turn_index, running_total):
        moved = shifted(running_total + block_total, "tm", SB)
        return jnp.where(within > 0, moved, 0.0)

    return lax.fori_loop(0, time_ranges - 1, advance_hop, jnp.zeros_like(block_total))


def norm_rows(gain_ref, tiles):
    gain = gain_ref[...].astype(jnp.float32).reshape(1, -1)
    widened = jnp.concatenate([tile[...] for tile in tiles], axis=0).astype(jnp.float32)
    mean_square = jnp.mean(widened * widened, axis=-1, keepdims=True)
    return (widened * lax.rsqrt(mean_square + epsilon) * gain).astype(jnp.bfloat16)


def write_pairs(normed, w_ref, offset, outs):
    pairs = dot(normed, w_ref[...]).astype(jnp.bfloat16)
    rows = pairs.shape[0]
    for head, out_ref in enumerate(outs):
        for start in range(0, rows, HD):
            there = slice(offset + start, offset + start + HD)
            out_ref[there, :HD] = pairs[start : start + HD, head_lanes(head)].T
        out_ref[offset : offset + rows, HD:] = pairs[:, head_lanes(KVH + head)]


def early_kernel(gain_ref, w_kv_ref, w_query_ref, *refs):
    tiles, query_ref, outs = refs[:EARLY], refs[EARLY], refs[EARLY + 1 :]
    normed = norm_rows(gain_ref, tiles)
    write_pairs(normed, w_kv_ref, 0, outs)
    query_ref[...] = dot(normed, w_query_ref[...]).astype(jnp.bfloat16)


def pairs_kernel(gain_ref, w_kv_ref, *refs):
    late = SB - EARLY
    tiles, done, normed_ref, outs = refs[:late], refs[late:-KVH - 1], refs[-KVH - 1], refs[-KVH:]
    normed = norm_rows(gain_ref, tiles)
    normed_ref[...] = normed
    rows = done[0].shape[0]
    for done_ref, out_ref in zip(done, outs):
        out_ref[:rows] = done_ref[...]
    write_pairs(normed, w_kv_ref, rows, outs)


def make_early(tiles, gain, w_kv, w_query):
    width, wide = w_kv.shape
    rows = sum(tile.shape[0] for tile in tiles)
    return pl.pallas_call(
        early_kernel,
        out_shape=[jax.ShapeDtypeStruct((rows, w_query.shape[1]), jnp.bfloat16)]
        + [jax.ShapeDtypeStruct((rows, wide // KVH), jnp.bfloat16)] * KVH,
        compiler_params=pltpu.CompilerParams(vmem_limit_bytes=16 * MIB),
        cost_estimate=pl.CostEstimate(
            flops=2 * rows * width * (wide + width),
            bytes_accessed=2 * (2 * rows * width + width * wide + width * width),
            transcendentals=rows,
        ),
        name="early_rows",
    )(gain, w_kv, w_query, *tiles)


def make_pairs(tiles, gain, w_kv, done):
    width, wide = w_kv.shape
    rows = sum(tile.shape[0] for tile in tiles)
    total = rows + done[0].shape[0]
    return pl.pallas_call(
        pairs_kernel,
        out_shape=[jax.ShapeDtypeStruct((rows, width), jnp.bfloat16)]
        + [jax.ShapeDtypeStruct((total, wide // KVH), jnp.bfloat16)] * KVH,
        compiler_params=pltpu.CompilerParams(vmem_limit_bytes=16 * MIB),
        cost_estimate=pl.CostEstimate(
            flops=2 * rows * width * wide,
            bytes_accessed=2 * (2 * rows * width + width * wide + rows * wide),
            transcendentals=rows,
        ),
        name="pairs",
    )(gain, w_kv, *tiles, *done)


SCORE_SCALE = math.log2(math.e) / math.sqrt(HD)
GROUP = HEADS // KVH


def key_and_value(ref):
    key = jnp.concatenate(
        [ref[start : start + HD, :HD] for start in range(0, ref.shape[0], HD)], axis=1
    )
    value = ref[:, HD:]
    return key, jnp.concatenate([value, jnp.ones_like(value)], axis=1)


def own_kernel(normed_ref, w_ref, early_ref, *refs):
    both = [key_and_value(ref) for ref in refs[:KVH]]
    query_ref, sum_ref, total_ref, top_ref = refs[KVH:]
    columns = GROUP * HD

    def project(group):
        lanes = slice(group * columns, (group + 1) * columns)
        late = dot(normed_ref[...], w_ref[:, lanes]).astype(jnp.bfloat16)
        query = jnp.concatenate([early_ref[:, lanes], late], axis=0)
        query_ref[:, lanes] = query
        return query

    queries = {0: project(0)}

    def scores_of(head):
        group = head // GROUP
        return dot(queries[group][:, head_lanes(head % GROUP)], both[group][0])

    scores = scores_of(0)
    for head in range(HEADS):
        if head % GROUP == 0 and head + GROUP < HEADS:
            queries[head // GROUP + 1] = project(head // GROUP + 1)
        upcoming = scores_of(head + 1) if head + 1 < HEADS else None
        lanes = head_lanes(head)
        largest = jnp.max(scores, axis=-1, keepdims=True)
        raised = jnp.exp2((scores - largest) * SCORE_SCALE).astype(jnp.bfloat16)
        summed = dot(raised, both[head // GROUP][1])
        sum_ref[:, lanes] = summed[:, :HD]
        total_ref[:, lanes] = summed[:, HD:]
        top_ref[:, lanes] = jnp.broadcast_to(largest * SCORE_SCALE, (scores.shape[0], HD))
        scores = upcoming


def own_frame(normed, w_query, early, pairs):
    rows, width = pairs[0].shape[0], normed.shape[1]
    return pl.pallas_call(
        own_kernel,
        out_shape=[jax.ShapeDtypeStruct((rows, width), jnp.bfloat16)]
        + [jax.ShapeDtypeStruct((rows, width), jnp.float32)] * 3,
        compiler_params=pltpu.CompilerParams(vmem_limit_bytes=32 * MIB),
        cost_estimate=pl.CostEstimate(
            flops=2 * rows * width * width + 4 * rows * rows * width,
            bytes_accessed=2 * width * width + 8 * rows * width,
            transcendentals=rows * rows * HEADS,
        ),
        name="own_frame",
    )(normed, w_query, early, *pairs)


def earlier_kernel(group, query_ref, pairs_ref, sum_ref, total_ref, top_ref, *refs):
    key, value = key_and_value(pairs_ref)
    index = lax.axis_index("tm")
    barred = jnp.where(index > 0, 0.0, -jnp.inf)
    place = lax.rem(index, SB)
    size = query_ref.shape[0] // SB
    columns = GROUP * HD
    last = group == KVH - 1
    copies = []
    if last:
        *done_refs, out_hbm, out_ref, sent = refs

        def leave(source, start):
            there = out_hbm.at[:, start : start + source.shape[1]]
            copies.append(pltpu.make_async_copy(source, there, sent.at[len(copies)]))
            copies[-1].start()

        for part, ref in enumerate(done_refs):
            leave(ref, part * columns)
    else:
        (out_ref,) = refs

    def scores_of(head):
        return dot(query_ref[:, head_lanes(group * GROUP + head)], key)

    scores = scores_of(0)
    for head in range(GROUP):
        lanes = head_lanes(group * GROUP + head)
        upcoming = scores_of(head + 1) if head + 1 < GROUP else None
        before = top_ref[:, lanes]
        here = jnp.max(scores, axis=-1, keepdims=True) * SCORE_SCALE + barred
        largest = jnp.maximum(jnp.broadcast_to(here, before.shape), before)
        below = jnp.concatenate([largest - barred] * (scores.shape[1] // HD), axis=1)
        raised = jnp.exp2(scores * SCORE_SCALE - below).astype(jnp.bfloat16)
        summed = dot(raised, value)
        share = jnp.exp2(before - largest)
        mixed = sum_ref[:, lanes] * share + summed[:, :HD]
        total = total_ref[:, lanes] * share + summed[:, HD:]
        mixed = (mixed / total).astype(jnp.bfloat16)
        for slot, apart in enumerate(APART):
            there = pl.ds(pl.multiple_of((place ^ apart) * size, size), size)
            out_ref[there, head_lanes(head)] = mixed[slot * size : (slot + 1) * size]
        if last and head % 2:
            start = (head - 1) * HD
            leave(out_ref.at[:, start : start + 2 * HD], group * columns + start)
        scores = upcoming
    for copy in copies:
        copy.wait()


def earlier_frame(group, query, pairs, so_far, done):
    rows, width = query.shape
    columns = GROUP * HD
    last = group == KVH - 1
    extra = dict(out_shape=jax.ShapeDtypeStruct((rows, columns), jnp.bfloat16))
    if last:
        extra = dict(
            out_shape=jax.ShapeDtypeStruct((rows, width), jnp.bfloat16),
            out_specs=pl.BlockSpec(memory_space=pl.ANY),
            scratch_shapes=[
                pltpu.VMEM((rows, columns), jnp.bfloat16),
                pltpu.SemaphoreType.DMA((KVH - 1 + GROUP // 2,)),
            ],
        )
    operands = [query, pairs, *so_far] + (done if last else [])
    return pl.pallas_call(
        functools.partial(earlier_kernel, group),
        compiler_params=pltpu.CompilerParams(vmem_limit_bytes=32 * MIB),
        cost_estimate=pl.CostEstimate(
            flops=4 * rows * rows * columns,
            bytes_accessed=20 * rows * columns,
            transcendentals=rows * rows * GROUP,
        ),
        name="earlier_frame",
        **extra,
    )(*operands)


def swap(tile, apart):
    devices = lax.axis_size("tm")
    route = [(i, i - i % SB + (i % SB ^ apart)) for i in range(devices)]
    return lax.ppermute(tile, "tm", route)


def body(space_time, w_lin, gain_lin, w_query, w_kv, frame_attention_gain):
    tokens = space_time[0]
    time_ranges = lax.axis_size("tm") // SB
    state = incoming_state(tokens, w_lin, time_ranges) if time_ranges > 1 else None
    tiles = mixer(tokens, w_lin, gain_lin, state)
    tiles = [swap(tile, apart) if apart else tile for apart, tile in zip(APART, tiles)]
    early, *done = make_early(tiles[:EARLY], frame_attention_gain, w_kv, w_query)
    normed, *pairs = make_pairs(tiles[EARLY:], frame_attention_gain, w_kv, done)
    earlier_pairs = [shifted(part, "tm", 1) for part in pairs]
    query, *so_far = own_frame(normed, w_query, early, pairs)
    done = []
    for group, part in enumerate(earlier_pairs):
        done.append(earlier_frame(group, query, part, so_far, done))
    return done[-1][None]


def solution(mesh):
    placed = (P(("groups", "tm"), None, None), P(), P(), P(), P(), P())
    return jax.shard_map(
        body, mesh=mesh, in_specs=placed, out_specs=P(("groups", "tm"), None, None), check_vma=False
    )
```

```python
import functools
import math

import jax
import jax.numpy as jnp
from jax import lax
from jax.experimental import pallas as pl
from jax.experimental.pallas import tpu as pltpu
from jax.sharding import PartitionSpec as P

HEADS = 8
HD = 128
KVH = 2
SB = 16
SPAN = 128
GROUPS = ((0, 4), (4, 8))
APART = (0, 5, 11, 9, 2, 12, 6, 8, 4, 14, 10, 15, 13, 3, 7, 1)
EARLY = SB - 4

epsilon = 1e-06
MIB = 1 << 20


def shifted(block, axis, distance):
    devices = range(lax.axis_size(axis))
    route = [(i - distance, i) for i in devices if i - distance in devices]
    return lax.ppermute(block, axis, route)


def dot(a, b):
    return jnp.dot(a, b, preferred_element_type=jnp.float32)


def dot_nt(a, b):
    return lax.dot_general(a, b, (((1,), (1,)), ((), ())), preferred_element_type=jnp.float32)


def dot_tn(a, b):
    return lax.dot_general(a, b, (((0,), (0,)), ((), ())), preferred_element_type=jnp.float32)


def head_lanes(head):
    return slice(head * HD, (head + 1) * HD)


def causal_mask():
    shape = (SPAN, SPAN)
    return lax.broadcasted_iota(jnp.int32, shape, 0) >= lax.broadcasted_iota(jnp.int32, shape, 1)


def mix_heads(query, key, value, states):
    rows = query.shape[0]
    causal = causal_mask()
    spans = [slice(start, start + SPAN) for start in range(0, rows, SPAN)]
    heads = range(query.shape[1] // HD)
    units = [(head, span) for head in heads for span in range(len(spans))]
    local, before, mixed = {}, {}, []
    for head, span in units:
        lanes, here = head_lanes(head), spans[span]
        scores = dot_nt(query[here, lanes], key[here, lanes])
        local[head, span] = jnp.where(causal, scores, 0.0).astype(jnp.bfloat16)
    for head in heads:
        lanes = head_lanes(head)
        state = states[head]
        for span, here in enumerate(spans):
            before[head, span] = state
            if span + 1 < len(spans):
                update = dot_tn(key[here, lanes], value[here, lanes])
                state = update if state is None else state + update
    for head, span in units:
        lanes, here = head_lanes(head), spans[span]
        if before[head, span] is None:
            out = dot(local[head, span], value[here, lanes])
        else:
            out = dot(
                jnp.concatenate([query[here, lanes], local[head, span]], axis=1),
                jnp.concatenate(
                    [before[head, span].astype(jnp.bfloat16), value[here, lanes]], axis=0
                ),
            )
        mixed.append((head, here, out))
    return mixed


def mixer_kernel(has_state, *refs):
    if has_state:
        state_ref, *refs = refs
    tokens_hbm, w_hbm, gain_ref, *refs = refs
    tiles, (tokens_ref, out_ref, *weights, tokens_in, weights_in, sent) = refs[:SB], refs[SB:]
    rows, width = tokens_ref.shape
    size = rows // SB
    place = lax.rem(lax.axis_index("tm"), SB)

    first = [pltpu.make_async_copy(tokens_hbm, tokens_ref, tokens_in)]
    copies = []
    for index, (low, high) in enumerate(GROUPS):
        here = []
        for part in range(3):
            columns = slice(part * width + low * HD, part * width + high * HD)
            here.append(
                pltpu.make_async_copy(
                    w_hbm.at[:, columns], weights[index].at[part], weights_in.at[index, part]
                )
            )
        copies.append(here)
    for copy in first + sum(copies, []):
        copy.start()
    gains = gain_ref[...].astype(jnp.float32).reshape(1, width)

    leaving = []

    def project(index):
        for copy in copies[index]:
            copy.wait()
        tokens = tokens_ref[...]
        return [dot(tokens, weights[index][part]).astype(jnp.bfloat16) for part in range(3)]

    def mix(index, parts):
        low, high = GROUPS[index]
        states = [state_ref[head] if has_state else None for head in range(low, high)]
        for head, here, out in mix_heads(*parts, states):
            lanes = head_lanes(low + head)
            mean_square = jnp.mean(out * out, axis=-1, keepdims=True)
            normed = out * lax.rsqrt(mean_square + epsilon) * gains[:, lanes]
            residual = tokens_ref[here, lanes].astype(jnp.float32)
            out_ref[here, lanes] = (residual + normed).astype(jnp.bfloat16)
        lanes = slice(low * HD, high * HD)
        for slot, (apart, tile) in enumerate(zip(APART, tiles)):
            here = pl.ds(pl.multiple_of((place ^ apart) * size, size), size)
            copy = pltpu.make_async_copy(
                out_ref.at[here, lanes], tile.at[:, lanes], sent.at[index, slot]
            )
            copy.start()
            leaving.append(copy)

    first[0].wait()
    parts = project(0)
    for index in range(len(GROUPS)):
        upcoming = project(index + 1) if index + 1 < len(GROUPS) else None
        mix(index, parts)
        parts = upcoming
    for copy in leaving:
        copy.wait()


def mixer(tokens, w_lin, gain_lin, state):
    rows, width = tokens.shape
    hbm = pl.BlockSpec(memory_space=pl.ANY)
    vmem = pl.BlockSpec(memory_space=pltpu.VMEM)
    in_specs = [hbm, hbm, vmem]
    operands = [tokens, w_lin, gain_lin]
    if state is not None:
        operands.insert(0, state)
        in_specs.insert(0, vmem)
    return pl.pallas_call(
        functools.partial(mixer_kernel, state is not None),
        in_specs=in_specs,
        out_specs=[hbm] * SB,
        out_shape=[jax.ShapeDtypeStruct((rows // SB, width), jnp.bfloat16)] * SB,
        scratch_shapes=[pltpu.VMEM((rows, width), jnp.bfloat16)] * 2
        + [pltpu.VMEM((3, width, (high - low) * HD), jnp.bfloat16) for low, high in GROUPS]
        + [
            pltpu.SemaphoreType.DMA,
            pltpu.SemaphoreType.DMA((len(GROUPS), 3)),
            pltpu.SemaphoreType.DMA((len(GROUPS), SB)),
        ],
        compiler_params=pltpu.CompilerParams(vmem_limit_bytes=60 * MIB),
        cost_estimate=pl.CostEstimate(
            flops=2 * rows * width * 3 * width + 8 * rows * SPAN * width,
            bytes_accessed=2 * (3 * width * width + 2 * rows * width),
            transcendentals=rows * HEADS,
        ),
        name="mixer",
    )(*operands)


def incoming_state(tokens, w_lin, time_ranges):
    rows, width = tokens.shape
    packed = dot(tokens, w_lin[:, width:]).astype(jnp.bfloat16).reshape(rows, 2, HEADS, HD)
    block_total = jnp.einsum(
        "nhd,nhe->hde", packed[:, 0], packed[:, 1], preferred_element_type=jnp.float32
    )
    within = lax.axis_index("tm") // SB

    def advance_hop(turn_index, running_total):
        moved = shifted(running_total + block_total, "tm", SB)
        return jnp.where(within > 0, moved, 0.0)

    return lax.fori_loop(0, time_ranges - 1, advance_hop, jnp.zeros_like(block_total))


def norm_rows(gain_ref, tiles):
    gain = gain_ref[...].astype(jnp.float32).reshape(1, -1)
    widened = jnp.concatenate([tile[...] for tile in tiles], axis=0).astype(jnp.float32)
    mean_square = jnp.mean(widened * widened, axis=-1, keepdims=True)
    return (widened * lax.rsqrt(mean_square + epsilon) * gain).astype(jnp.bfloat16)


def write_pairs(normed, w_ref, offset, outs):
    pairs = dot(normed, w_ref[...]).astype(jnp.bfloat16)
    rows = pairs.shape[0]
    for head, out_ref in enumerate(outs):
        for start in range(0, rows, HD):
            there = slice(offset + start, offset + start + HD)
            out_ref[there, :HD] = pairs[start : start + HD, head_lanes(head)].T
        out_ref[offset : offset + rows, HD:] = pairs[:, head_lanes(KVH + head)]


def early_kernel(gain_ref, w_kv_ref, w_query_ref, *refs):
    tiles, query_ref, outs = refs[:EARLY], refs[EARLY], refs[EARLY + 1 :]
    normed = norm_rows(gain_ref, tiles)
    write_pairs(normed, w_kv_ref, 0, outs)
    query_ref[...] = dot(normed, w_query_ref[...]).astype(jnp.bfloat16)


def pairs_kernel(gain_ref, w_kv_ref, *refs):
    late = SB - EARLY
    tiles, done, normed_ref, outs = refs[:late], refs[late:-KVH - 1], refs[-KVH - 1], refs[-KVH:]
    normed = norm_rows(gain_ref, tiles)
    normed_ref[...] = normed
    rows = done[0].shape[0]
    for done_ref, out_ref in zip(done, outs):
        out_ref[:rows] = done_ref[...]
    write_pairs(normed, w_kv_ref, rows, outs)


def make_early(tiles, gain, w_kv, w_query):
    width, wide = w_kv.shape
    rows = sum(tile.shape[0] for tile in tiles)
    return pl.pallas_call(
        early_kernel,
        out_shape=[jax.ShapeDtypeStruct((rows, w_query.shape[1]), jnp.bfloat16)]
        + [jax.ShapeDtypeStruct((rows, wide // KVH), jnp.bfloat16)] * KVH,
        compiler_params=pltpu.CompilerParams(vmem_limit_bytes=16 * MIB),
        cost_estimate=pl.CostEstimate(
            flops=2 * rows * width * (wide + width),
            bytes_accessed=2 * (2 * rows * width + width * wide + width * width),
            transcendentals=rows,
        ),
        name="early_rows",
    )(gain, w_kv, w_query, *tiles)


def make_pairs(tiles, gain, w_kv, done):
    width, wide = w_kv.shape
    rows = sum(tile.shape[0] for tile in tiles)
    total = rows + done[0].shape[0]
    return pl.pallas_call(
        pairs_kernel,
        out_shape=[jax.ShapeDtypeStruct((rows, width), jnp.bfloat16)]
        + [jax.ShapeDtypeStruct((total, wide // KVH), jnp.bfloat16)] * KVH,
        compiler_params=pltpu.CompilerParams(vmem_limit_bytes=16 * MIB),
        cost_estimate=pl.CostEstimate(
            flops=2 * rows * width * wide,
            bytes_accessed=2 * (2 * rows * width + width * wide + rows * wide),
            transcendentals=rows,
        ),
        name="pairs",
    )(gain, w_kv, *tiles, *done)


SCORE_SCALE = math.log2(math.e) / math.sqrt(HD)
GROUP = HEADS // KVH


def key_and_value(ref):
    key = jnp.concatenate(
        [ref[start : start + HD, :HD] for start in range(0, ref.shape[0], HD)], axis=1
    )
    value = ref[:, HD:]
    return key, jnp.concatenate([value, jnp.ones_like(value)], axis=1)


def own_kernel(normed_ref, w_ref, early_ref, *refs):
    both = [key_and_value(ref) for ref in refs[:KVH]]
    query_ref, sum_ref, total_ref, top_ref = refs[KVH:]
    columns = GROUP * HD

    def project(group):
        lanes = slice(group * columns, (group + 1) * columns)
        late = dot(normed_ref[...], w_ref[:, lanes]).astype(jnp.bfloat16)
        query = jnp.concatenate([early_ref[:, lanes], late], axis=0)
        query_ref[:, lanes] = query
        return query

    queries = {0: project(0)}

    def scores_of(head):
        group = head // GROUP
        return dot(queries[group][:, head_lanes(head % GROUP)], both[group][0])

    scores = scores_of(0)
    for head in range(HEADS):
        if head % GROUP == 0 and head + GROUP < HEADS:
            queries[head // GROUP + 1] = project(head // GROUP + 1)
        upcoming = scores_of(head + 1) if head + 1 < HEADS else None
        lanes = head_lanes(head)
        largest = jnp.max(scores, axis=-1, keepdims=True)
        raised = jnp.exp2((scores - largest) * SCORE_SCALE).astype(jnp.bfloat16)
        summed = dot(raised, both[head // GROUP][1])
        sum_ref[:, lanes] = summed[:, :HD]
        total_ref[:, lanes] = summed[:, HD:]
        top_ref[:, lanes] = jnp.broadcast_to(largest * SCORE_SCALE, (scores.shape[0], HD))
        scores = upcoming


def own_frame(normed, w_query, early, pairs):
    rows, width = pairs[0].shape[0], normed.shape[1]
    return pl.pallas_call(
        own_kernel,
        out_shape=[jax.ShapeDtypeStruct((rows, width), jnp.bfloat16)]
        + [jax.ShapeDtypeStruct((rows, width), jnp.float32)] * 3,
        compiler_params=pltpu.CompilerParams(vmem_limit_bytes=32 * MIB),
        cost_estimate=pl.CostEstimate(
            flops=2 * rows * width * width + 4 * rows * rows * width,
            bytes_accessed=2 * width * width + 8 * rows * width,
            transcendentals=rows * rows * HEADS,
        ),
        name="own_frame",
    )(normed, w_query, early, *pairs)


def earlier_kernel(group, query_ref, pairs_ref, sum_ref, total_ref, top_ref, *refs):
    key, value = key_and_value(pairs_ref)
    index = lax.axis_index("tm")
    barred = jnp.where(index > 0, 0.0, -jnp.inf)
    place = lax.rem(index, SB)
    size = query_ref.shape[0] // SB
    columns = GROUP * HD
    last = group == KVH - 1
    copies = []
    if last:
        *done_refs, out_hbm, out_ref, sent = refs

        def leave(source, start):
            there = out_hbm.at[:, start : start + source.shape[1]]
            copies.append(pltpu.make_async_copy(source, there, sent.at[len(copies)]))
            copies[-1].start()

        for part, ref in enumerate(done_refs):
            leave(ref, part * columns)
    else:
        (out_ref,) = refs

    def scores_of(head):
        return dot(query_ref[:, head_lanes(group * GROUP + head)], key)

    scores = scores_of(0)
    for head in range(GROUP):
        lanes = head_lanes(group * GROUP + head)
        upcoming = scores_of(head + 1) if head + 1 < GROUP else None
        before = top_ref[:, lanes]
        here = jnp.max(scores, axis=-1, keepdims=True) * SCORE_SCALE + barred
        largest = jnp.maximum(jnp.broadcast_to(here, before.shape), before)
        below = jnp.concatenate([largest - barred] * (scores.shape[1] // HD), axis=1)
        raised = jnp.exp2(scores * SCORE_SCALE - below).astype(jnp.bfloat16)
        summed = dot(raised, value)
        share = jnp.exp2(before - largest)
        mixed = sum_ref[:, lanes] * share + summed[:, :HD]
        total = total_ref[:, lanes] * share + summed[:, HD:]
        mixed = (mixed / total).astype(jnp.bfloat16)
        for slot, apart in enumerate(APART):
            there = pl.ds(pl.multiple_of((place ^ apart) * size, size), size)
            out_ref[there, head_lanes(head)] = mixed[slot * size : (slot + 1) * size]
        if last and head % 2:
            start = (head - 1) * HD
            leave(out_ref.at[:, start : start + 2 * HD], group * columns + start)
        scores = upcoming
    for copy in copies:
        copy.wait()


def earlier_frame(group, query, pairs, so_far, done):
    rows, width = query.shape
    columns = GROUP * HD
    last = group == KVH - 1
    extra = dict(out_shape=jax.ShapeDtypeStruct((rows, columns), jnp.bfloat16))
    if last:
        extra = dict(
            out_shape=jax.ShapeDtypeStruct((rows, width), jnp.bfloat16),
            out_specs=pl.BlockSpec(memory_space=pl.ANY),
            scratch_shapes=[
                pltpu.VMEM((rows, columns), jnp.bfloat16),
                pltpu.SemaphoreType.DMA((KVH - 1 + GROUP // 2,)),
            ],
        )
    operands = [query, pairs, *so_far] + (done if last else [])
    return pl.pallas_call(
        functools.partial(earlier_kernel, group),
        compiler_params=pltpu.CompilerParams(vmem_limit_bytes=32 * MIB),
        cost_estimate=pl.CostEstimate(
            flops=4 * rows * rows * columns,
            bytes_accessed=20 * rows * columns,
            transcendentals=rows * rows * GROUP,
        ),
        name="earlier_frame",
        **extra,
    )(*operands)


def swap(tile, apart):
    devices = lax.axis_size("tm")
    route = [(i, i - i % SB + (i % SB ^ apart)) for i in range(devices)]
    return lax.ppermute(tile, "tm", route)


def body(space_time, w_lin, gain_lin, w_query, w_kv, frame_attention_gain):
    tokens = space_time[0]
    time_ranges = lax.axis_size("tm") // SB
    state = incoming_state(tokens, w_lin, time_ranges) if time_ranges > 1 else None
    tiles = mixer(tokens, w_lin, gain_lin, state)
    tiles = [swap(tile, apart) if apart else tile for apart, tile in zip(APART, tiles)]
    early, *done = make_early(tiles[:EARLY], frame_attention_gain, w_kv, w_query)
    normed, *pairs = make_pairs(tiles[EARLY:], frame_attention_gain, w_kv, done)
    earlier_pairs = [shifted(part, "tm", 1) for part in pairs]
    query, *so_far = own_frame(normed, w_query, early, pairs)
    done = []
    for group, part in enumerate(earlier_pairs):
        done.append(earlier_frame(group, query, part, so_far, done))
    return done[-1][None]


def solution(mesh):
    placed = (P(("groups", "tm"), None, None), P(), P(), P(), P(), P())
    return jax.shard_map(
        body, mesh=mesh, in_specs=placed, out_specs=P(("groups", "tm"), None, None), check_vma=False
    )
```

```python
import functools
import math

import jax
import jax.numpy as jnp
from jax import lax
from jax.experimental import pallas as pl
from jax.experimental.pallas import tpu as pltpu
from jax.sharding import PartitionSpec as P

HEADS = 8
HD = 128
KVH = 2
SB = 16
SPAN = 128
GROUPS = ((0, 4), (4, 8))
APART = (0, 5, 11, 9, 2, 12, 6, 8, 4, 14, 10, 15, 13, 7, 3, 1)
EARLY = SB - 4

epsilon = 1e-06
MIB = 1 << 20


def shifted(block, axis, distance):
    devices = range(lax.axis_size(axis))
    route = [(i - distance, i) for i in devices if i - distance in devices]
    return lax.ppermute(block, axis, route)


def dot(a, b):
    return jnp.dot(a, b, preferred_element_type=jnp.float32)


def dot_nt(a, b):
    return lax.dot_general(a, b, (((1,), (1,)), ((), ())), preferred_element_type=jnp.float32)


def dot_tn(a, b):
    return lax.dot_general(a, b, (((0,), (0,)), ((), ())), preferred_element_type=jnp.float32)


def head_lanes(head):
    return slice(head * HD, (head + 1) * HD)


def causal_mask():
    shape = (SPAN, SPAN)
    return lax.broadcasted_iota(jnp.int32, shape, 0) >= lax.broadcasted_iota(jnp.int32, shape, 1)


def mix_heads(query, key, value, states):
    rows = query.shape[0]
    causal = causal_mask()
    spans = [slice(start, start + SPAN) for start in range(0, rows, SPAN)]
    heads = range(query.shape[1] // HD)
    units = [(head, span) for head in heads for span in range(len(spans))]
    local, before, mixed = {}, {}, []
    for head, span in units:
        lanes, here = head_lanes(head), spans[span]
        scores = dot_nt(query[here, lanes], key[here, lanes])
        local[head, span] = jnp.where(causal, scores, 0.0).astype(jnp.bfloat16)
    for head in heads:
        lanes = head_lanes(head)
        state = states[head]
        for span, here in enumerate(spans):
            before[head, span] = state
            if span + 1 < len(spans):
                update = dot_tn(key[here, lanes], value[here, lanes])
                state = update if state is None else state + update
    for head, span in units:
        lanes, here = head_lanes(head), spans[span]
        if before[head, span] is None:
            out = dot(local[head, span], value[here, lanes])
        else:
            out = dot(
                jnp.concatenate([query[here, lanes], local[head, span]], axis=1),
                jnp.concatenate(
                    [before[head, span].astype(jnp.bfloat16), value[here, lanes]], axis=0
                ),
            )
        mixed.append((head, here, out))
    return mixed


def mixer_kernel(has_state, *refs):
    if has_state:
        state_ref, *refs = refs
    tokens_hbm, w_hbm, gain_ref, *refs = refs
    tiles, (tokens_ref, out_ref, *weights, tokens_in, weights_in, sent) = refs[:SB], refs[SB:]
    rows, width = tokens_ref.shape
    size = rows // SB
    place = lax.rem(lax.axis_index("tm"), SB)

    first = [pltpu.make_async_copy(tokens_hbm, tokens_ref, tokens_in)]
    copies = []
    for index, (low, high) in enumerate(GROUPS):
        here = []
        for part in range(3):
            columns = slice(part * width + low * HD, part * width + high * HD)
            here.append(
                pltpu.make_async_copy(
                    w_hbm.at[:, columns], weights[index].at[part], weights_in.at[index, part]
                )
            )
        copies.append(here)
    for copy in first + sum(copies, []):
        copy.start()
    gains = gain_ref[...].astype(jnp.float32).reshape(1, width)

    leaving = []

    def project(index):
        for copy in copies[index]:
            copy.wait()
        tokens = tokens_ref[...]
        return [dot(tokens, weights[index][part]).astype(jnp.bfloat16) for part in range(3)]

    def mix(index, parts):
        low, high = GROUPS[index]
        states = [state_ref[head] if has_state else None for head in range(low, high)]
        for head, here, out in mix_heads(*parts, states):
            lanes = head_lanes(low + head)
            mean_square = jnp.mean(out * out, axis=-1, keepdims=True)
            normed = out * lax.rsqrt(mean_square + epsilon) * gains[:, lanes]
            residual = tokens_ref[here, lanes].astype(jnp.float32)
            out_ref[here, lanes] = (residual + normed).astype(jnp.bfloat16)
        lanes = slice(low * HD, high * HD)
        for slot, (apart, tile) in enumerate(zip(APART, tiles)):
            here = pl.ds(pl.multiple_of((place ^ apart) * size, size), size)
            copy = pltpu.make_async_copy(
                out_ref.at[here, lanes], tile.at[:, lanes], sent.at[index, slot]
            )
            copy.start()
            leaving.append(copy)

    first[0].wait()
    parts = project(0)
    for index in range(len(GROUPS)):
        upcoming = project(index + 1) if index + 1 < len(GROUPS) else None
        mix(index, parts)
        parts = upcoming
    for copy in leaving:
        copy.wait()


def mixer(tokens, w_lin, gain_lin, state):
    rows, width = tokens.shape
    hbm = pl.BlockSpec(memory_space=pl.ANY)
    vmem = pl.BlockSpec(memory_space=pltpu.VMEM)
    in_specs = [hbm, hbm, vmem]
    operands = [tokens, w_lin, gain_lin]
    if state is not None:
        operands.insert(0, state)
        in_specs.insert(0, vmem)
    return pl.pallas_call(
        functools.partial(mixer_kernel, state is not None),
        in_specs=in_specs,
        out_specs=[hbm] * SB,
        out_shape=[jax.ShapeDtypeStruct((rows // SB, width), jnp.bfloat16)] * SB,
        scratch_shapes=[pltpu.VMEM((rows, width), jnp.bfloat16)] * 2
        + [pltpu.VMEM((3, width, (high - low) * HD), jnp.bfloat16) for low, high in GROUPS]
        + [
            pltpu.SemaphoreType.DMA,
            pltpu.SemaphoreType.DMA((len(GROUPS), 3)),
            pltpu.SemaphoreType.DMA((len(GROUPS), SB)),
        ],
        compiler_params=pltpu.CompilerParams(vmem_limit_bytes=60 * MIB),
        cost_estimate=pl.CostEstimate(
            flops=2 * rows * width * 3 * width + 8 * rows * SPAN * width,
            bytes_accessed=2 * (3 * width * width + 2 * rows * width),
            transcendentals=rows * HEADS,
        ),
        name="mixer",
    )(*operands)


def incoming_state(tokens, w_lin, time_ranges):
    rows, width = tokens.shape
    packed = dot(tokens, w_lin[:, width:]).astype(jnp.bfloat16).reshape(rows, 2, HEADS, HD)
    block_total = jnp.einsum(
        "nhd,nhe->hde", packed[:, 0], packed[:, 1], preferred_element_type=jnp.float32
    )
    within = lax.axis_index("tm") // SB

    def advance_hop(turn_index, running_total):
        moved = shifted(running_total + block_total, "tm", SB)
        return jnp.where(within > 0, moved, 0.0)

    return lax.fori_loop(0, time_ranges - 1, advance_hop, jnp.zeros_like(block_total))


def norm_rows(gain_ref, tiles):
    gain = gain_ref[...].astype(jnp.float32).reshape(1, -1)
    widened = jnp.concatenate([tile[...] for tile in tiles], axis=0).astype(jnp.float32)
    mean_square = jnp.mean(widened * widened, axis=-1, keepdims=True)
    return (widened * lax.rsqrt(mean_square + epsilon) * gain).astype(jnp.bfloat16)


def write_pairs(normed, w_ref, offset, outs):
    pairs = dot(normed, w_ref[...]).astype(jnp.bfloat16)
    rows = pairs.shape[0]
    for head, out_ref in enumerate(outs):
        for start in range(0, rows, HD):
            there = slice(offset + start, offset + start + HD)
            out_ref[there, :HD] = pairs[start : start + HD, head_lanes(head)].T
        out_ref[offset : offset + rows, HD:] = pairs[:, head_lanes(KVH + head)]


def early_kernel(gain_ref, w_kv_ref, w_query_ref, *refs):
    tiles, query_ref, outs = refs[:EARLY], refs[EARLY], refs[EARLY + 1 :]
    normed = norm_rows(gain_ref, tiles)
    write_pairs(normed, w_kv_ref, 0, outs)
    query_ref[...] = dot(normed, w_query_ref[...]).astype(jnp.bfloat16)


def pairs_kernel(gain_ref, w_kv_ref, *refs):
    late = SB - EARLY
    tiles, done, normed_ref, outs = refs[:late], refs[late:-KVH - 1], refs[-KVH - 1], refs[-KVH:]
    normed = norm_rows(gain_ref, tiles)
    normed_ref[...] = normed
    rows = done[0].shape[0]
    for done_ref, out_ref in zip(done, outs):
        out_ref[:rows] = done_ref[...]
    write_pairs(normed, w_kv_ref, rows, outs)


def make_early(tiles, gain, w_kv, w_query):
    width, wide = w_kv.shape
    rows = sum(tile.shape[0] for tile in tiles)
    return pl.pallas_call(
        early_kernel,
        out_shape=[jax.ShapeDtypeStruct((rows, w_query.shape[1]), jnp.bfloat16)]
        + [jax.ShapeDtypeStruct((rows, wide // KVH), jnp.bfloat16)] * KVH,
        compiler_params=pltpu.CompilerParams(vmem_limit_bytes=16 * MIB),
        cost_estimate=pl.CostEstimate(
            flops=2 * rows * width * (wide + width),
            bytes_accessed=2 * (2 * rows * width + width * wide + width * width),
            transcendentals=rows,
        ),
        name="early_rows",
    )(gain, w_kv, w_query, *tiles)


def make_pairs(tiles, gain, w_kv, done):
    width, wide = w_kv.shape
    rows = sum(tile.shape[0] for tile in tiles)
    total = rows + done[0].shape[0]
    return pl.pallas_call(
        pairs_kernel,
        out_shape=[jax.ShapeDtypeStruct((rows, width), jnp.bfloat16)]
        + [jax.ShapeDtypeStruct((total, wide // KVH), jnp.bfloat16)] * KVH,
        compiler_params=pltpu.CompilerParams(vmem_limit_bytes=16 * MIB),
        cost_estimate=pl.CostEstimate(
            flops=2 * rows * width * wide,
            bytes_accessed=2 * (2 * rows * width + width * wide + rows * wide),
            transcendentals=rows,
        ),
        name="pairs",
    )(gain, w_kv, *tiles, *done)


SCORE_SCALE = math.log2(math.e) / math.sqrt(HD)
GROUP = HEADS // KVH


def key_and_value(ref):
    key = jnp.concatenate(
        [ref[start : start + HD, :HD] for start in range(0, ref.shape[0], HD)], axis=1
    )
    value = ref[:, HD:]
    return key, jnp.concatenate([value, jnp.ones_like(value)], axis=1)


def own_kernel(normed_ref, w_ref, early_ref, *refs):
    both = [key_and_value(ref) for ref in refs[:KVH]]
    query_ref, sum_ref, total_ref, top_ref = refs[KVH:]
    columns = GROUP * HD

    def project(group):
        lanes = slice(group * columns, (group + 1) * columns)
        late = dot(normed_ref[...], w_ref[:, lanes]).astype(jnp.bfloat16)
        query = jnp.concatenate([early_ref[:, lanes], late], axis=0)
        query_ref[:, lanes] = query
        return query

    queries = {0: project(0)}

    def scores_of(head):
        group = head // GROUP
        return dot(queries[group][:, head_lanes(head % GROUP)], both[group][0])

    scores = scores_of(0)
    for head in range(HEADS):
        if head % GROUP == 0 and head + GROUP < HEADS:
            queries[head // GROUP + 1] = project(head // GROUP + 1)
        upcoming = scores_of(head + 1) if head + 1 < HEADS else None
        lanes = head_lanes(head)
        largest = jnp.max(scores, axis=-1, keepdims=True)
        raised = jnp.exp2((scores - largest) * SCORE_SCALE).astype(jnp.bfloat16)
        summed = dot(raised, both[head // GROUP][1])
        sum_ref[:, lanes] = summed[:, :HD]
        total_ref[:, lanes] = summed[:, HD:]
        top_ref[:, lanes] = jnp.broadcast_to(largest * SCORE_SCALE, (scores.shape[0], HD))
        scores = upcoming


def own_frame(normed, w_query, early, pairs):
    rows, width = pairs[0].shape[0], normed.shape[1]
    return pl.pallas_call(
        own_kernel,
        out_shape=[jax.ShapeDtypeStruct((rows, width), jnp.bfloat16)]
        + [jax.ShapeDtypeStruct((rows, width), jnp.float32)] * 3,
        compiler_params=pltpu.CompilerParams(vmem_limit_bytes=32 * MIB),
        cost_estimate=pl.CostEstimate(
            flops=2 * rows * width * width + 4 * rows * rows * width,
            bytes_accessed=2 * width * width + 8 * rows * width,
            transcendentals=rows * rows * HEADS,
        ),
        name="own_frame",
    )(normed, w_query, early, *pairs)


def earlier_kernel(group, query_ref, pairs_ref, sum_ref, total_ref, top_ref, *refs):
    key, value = key_and_value(pairs_ref)
    index = lax.axis_index("tm")
    barred = jnp.where(index > 0, 0.0, -jnp.inf)
    place = lax.rem(index, SB)
    size = query_ref.shape[0] // SB
    columns = GROUP * HD
    last = group == KVH - 1
    copies = []
    if last:
        *done_refs, out_hbm, out_ref, sent = refs

        def leave(source, start):
            there = out_hbm.at[:, start : start + source.shape[1]]
            copies.append(pltpu.make_async_copy(source, there, sent.at[len(copies)]))
            copies[-1].start()

        for part, ref in enumerate(done_refs):
            leave(ref, part * columns)
    else:
        (out_ref,) = refs

    def scores_of(head):
        return dot(query_ref[:, head_lanes(group * GROUP + head)], key)

    scores = scores_of(0)
    for head in range(GROUP):
        lanes = head_lanes(group * GROUP + head)
        upcoming = scores_of(head + 1) if head + 1 < GROUP else None
        before = top_ref[:, lanes]
        here = jnp.max(scores, axis=-1, keepdims=True) * SCORE_SCALE + barred
        largest = jnp.maximum(jnp.broadcast_to(here, before.shape), before)
        below = jnp.concatenate([largest - barred] * (scores.shape[1] // HD), axis=1)
        raised = jnp.exp2(scores * SCORE_SCALE - below).astype(jnp.bfloat16)
        summed = dot(raised, value)
        share = jnp.exp2(before - largest)
        mixed = sum_ref[:, lanes] * share + summed[:, :HD]
        total = total_ref[:, lanes] * share + summed[:, HD:]
        mixed = (mixed / total).astype(jnp.bfloat16)
        for slot, apart in enumerate(APART):
            there = pl.ds(pl.multiple_of((place ^ apart) * size, size), size)
            out_ref[there, head_lanes(head)] = mixed[slot * size : (slot + 1) * size]
        if last and head % 2:
            start = (head - 1) * HD
            leave(out_ref.at[:, start : start + 2 * HD], group * columns + start)
        scores = upcoming
    for copy in copies:
        copy.wait()


def earlier_frame(group, query, pairs, so_far, done):
    rows, width = query.shape
    columns = GROUP * HD
    last = group == KVH - 1
    extra = dict(out_shape=jax.ShapeDtypeStruct((rows, columns), jnp.bfloat16))
    if last:
        extra = dict(
            out_shape=jax.ShapeDtypeStruct((rows, width), jnp.bfloat16),
            out_specs=pl.BlockSpec(memory_space=pl.ANY),
            scratch_shapes=[
                pltpu.VMEM((rows, columns), jnp.bfloat16),
                pltpu.SemaphoreType.DMA((KVH - 1 + GROUP // 2,)),
            ],
        )
    operands = [query, pairs, *so_far] + (done if last else [])
    return pl.pallas_call(
        functools.partial(earlier_kernel, group),
        compiler_params=pltpu.CompilerParams(vmem_limit_bytes=32 * MIB),
        cost_estimate=pl.CostEstimate(
            flops=4 * rows * rows * columns,
            bytes_accessed=20 * rows * columns,
            transcendentals=rows * rows * GROUP,
        ),
        name="earlier_frame",
        **extra,
    )(*operands)


def swap(tile, apart):
    devices = lax.axis_size("tm")
    route = [(i, i - i % SB + (i % SB ^ apart)) for i in range(devices)]
    return lax.ppermute(tile, "tm", route)


def body(space_time, w_lin, gain_lin, w_query, w_kv, frame_attention_gain):
    tokens = space_time[0]
    time_ranges = lax.axis_size("tm") // SB
    state = incoming_state(tokens, w_lin, time_ranges) if time_ranges > 1 else None
    tiles = mixer(tokens, w_lin, gain_lin, state)
    tiles = [swap(tile, apart) if apart else tile for apart, tile in zip(APART, tiles)]
    early, *done = make_early(tiles[:EARLY], frame_attention_gain, w_kv, w_query)
    normed, *pairs = make_pairs(tiles[EARLY:], frame_attention_gain, w_kv, done)
    earlier_pairs = [shifted(part, "tm", 1) for part in pairs]
    query, *so_far = own_frame(normed, w_query, early, pairs)
    done = []
    for group, part in enumerate(earlier_pairs):
        done.append(earlier_frame(group, query, part, so_far, done))
    return done[-1][None]


def solution(mesh):
    placed = (P(("groups", "tm"), None, None), P(), P(), P(), P(), P())
    return jax.shard_map(
        body, mesh=mesh, in_specs=placed, out_specs=P(("groups", "tm"), None, None), check_vma=False
    )
```

```python
import functools
import math

import jax
import jax.numpy as jnp
from jax import lax
from jax.experimental import pallas as pl
from jax.experimental.pallas import tpu as pltpu
from jax.sharding import PartitionSpec as P

HEADS = 8
HD = 128
KVH = 2
SB = 16
SPAN = 128
GROUPS = ((0, 4), (4, 8))
APART = (0, 5, 11, 9, 7, 12, 6, 8, 4, 14, 10, 15, 13, 2, 3, 1)
EARLY = SB - 4

epsilon = 1e-06
MIB = 1 << 20


def shifted(block, axis, distance):
    devices = range(lax.axis_size(axis))
    route = [(i - distance, i) for i in devices if i - distance in devices]
    return lax.ppermute(block, axis, route)


def dot(a, b):
    return jnp.dot(a, b, preferred_element_type=jnp.float32)


def dot_nt(a, b):
    return lax.dot_general(a, b, (((1,), (1,)), ((), ())), preferred_element_type=jnp.float32)


def dot_tn(a, b):
    return lax.dot_general(a, b, (((0,), (0,)), ((), ())), preferred_element_type=jnp.float32)


def head_lanes(head):
    return slice(head * HD, (head + 1) * HD)


def causal_mask():
    shape = (SPAN, SPAN)
    return lax.broadcasted_iota(jnp.int32, shape, 0) >= lax.broadcasted_iota(jnp.int32, shape, 1)


def mix_heads(query, key, value, states):
    rows = query.shape[0]
    causal = causal_mask()
    spans = [slice(start, start + SPAN) for start in range(0, rows, SPAN)]
    heads = range(query.shape[1] // HD)
    units = [(head, span) for head in heads for span in range(len(spans))]
    local, before, mixed = {}, {}, []
    for head, span in units:
        lanes, here = head_lanes(head), spans[span]
        scores = dot_nt(query[here, lanes], key[here, lanes])
        local[head, span] = jnp.where(causal, scores, 0.0).astype(jnp.bfloat16)
    for head in heads:
        lanes = head_lanes(head)
        state = states[head]
        for span, here in enumerate(spans):
            before[head, span] = state
            if span + 1 < len(spans):
                update = dot_tn(key[here, lanes], value[here, lanes])
                state = update if state is None else state + update
    for head, span in units:
        lanes, here = head_lanes(head), spans[span]
        if before[head, span] is None:
            out = dot(local[head, span], value[here, lanes])
        else:
            out = dot(
                jnp.concatenate([query[here, lanes], local[head, span]], axis=1),
                jnp.concatenate(
                    [before[head, span].astype(jnp.bfloat16), value[here, lanes]], axis=0
                ),
            )
        mixed.append((head, here, out))
    return mixed


def mixer_kernel(has_state, *refs):
    if has_state:
        state_ref, *refs = refs
    tokens_hbm, w_hbm, gain_ref, *refs = refs
    tiles, (tokens_ref, out_ref, *weights, tokens_in, weights_in, sent) = refs[:SB], refs[SB:]
    rows, width = tokens_ref.shape
    size = rows // SB
    place = lax.rem(lax.axis_index("tm"), SB)

    first = [pltpu.make_async_copy(tokens_hbm, tokens_ref, tokens_in)]
    copies = []
    for index, (low, high) in enumerate(GROUPS):
        here = []
        for part in range(3):
            columns = slice(part * width + low * HD, part * width + high * HD)
            here.append(
                pltpu.make_async_copy(
                    w_hbm.at[:, columns], weights[index].at[part], weights_in.at[index, part]
                )
            )
        copies.append(here)
    for copy in first + sum(copies, []):
        copy.start()
    gains = gain_ref[...].astype(jnp.float32).reshape(1, width)

    leaving = []

    def project(index):
        for copy in copies[index]:
            copy.wait()
        tokens = tokens_ref[...]
        return [dot(tokens, weights[index][part]).astype(jnp.bfloat16) for part in range(3)]

    def mix(index, parts):
        low, high = GROUPS[index]
        states = [state_ref[head] if has_state else None for head in range(low, high)]
        for head, here, out in mix_heads(*parts, states):
            lanes = head_lanes(low + head)
            mean_square = jnp.mean(out * out, axis=-1, keepdims=True)
            normed = out * lax.rsqrt(mean_square + epsilon) * gains[:, lanes]
            residual = tokens_ref[here, lanes].astype(jnp.float32)
            out_ref[here, lanes] = (residual + normed).astype(jnp.bfloat16)
        lanes = slice(low * HD, high * HD)
        for slot, (apart, tile) in enumerate(zip(APART, tiles)):
            here = pl.ds(pl.multiple_of((place ^ apart) * size, size), size)
            copy = pltpu.make_async_copy(
                out_ref.at[here, lanes], tile.at[:, lanes], sent.at[index, slot]
            )
            copy.start()
            leaving.append(copy)

    first[0].wait()
    parts = project(0)
    for index in range(len(GROUPS)):
        upcoming = project(index + 1) if index + 1 < len(GROUPS) else None
        mix(index, parts)
        parts = upcoming
    for copy in leaving:
        copy.wait()


def mixer(tokens, w_lin, gain_lin, state):
    rows, width = tokens.shape
    hbm = pl.BlockSpec(memory_space=pl.ANY)
    vmem = pl.BlockSpec(memory_space=pltpu.VMEM)
    in_specs = [hbm, hbm, vmem]
    operands = [tokens, w_lin, gain_lin]
    if state is not None:
        operands.insert(0, state)
        in_specs.insert(0, vmem)
    return pl.pallas_call(
        functools.partial(mixer_kernel, state is not None),
        in_specs=in_specs,
        out_specs=[hbm] * SB,
        out_shape=[jax.ShapeDtypeStruct((rows // SB, width), jnp.bfloat16)] * SB,
        scratch_shapes=[pltpu.VMEM((rows, width), jnp.bfloat16)] * 2
        + [pltpu.VMEM((3, width, (high - low) * HD), jnp.bfloat16) for low, high in GROUPS]
        + [
            pltpu.SemaphoreType.DMA,
            pltpu.SemaphoreType.DMA((len(GROUPS), 3)),
            pltpu.SemaphoreType.DMA((len(GROUPS), SB)),
        ],
        compiler_params=pltpu.CompilerParams(vmem_limit_bytes=60 * MIB),
        cost_estimate=pl.CostEstimate(
            flops=2 * rows * width * 3 * width + 8 * rows * SPAN * width,
            bytes_accessed=2 * (3 * width * width + 2 * rows * width),
            transcendentals=rows * HEADS,
        ),
        name="mixer",
    )(*operands)


def incoming_state(tokens, w_lin, time_ranges):
    rows, width = tokens.shape
    packed = dot(tokens, w_lin[:, width:]).astype(jnp.bfloat16).reshape(rows, 2, HEADS, HD)
    block_total = jnp.einsum(
        "nhd,nhe->hde", packed[:, 0], packed[:, 1], preferred_element_type=jnp.float32
    )
    within = lax.axis_index("tm") // SB

    def advance_hop(turn_index, running_total):
        moved = shifted(running_total + block_total, "tm", SB)
        return jnp.where(within > 0, moved, 0.0)

    return lax.fori_loop(0, time_ranges - 1, advance_hop, jnp.zeros_like(block_total))


def norm_rows(gain_ref, tiles):
    gain = gain_ref[...].astype(jnp.float32).reshape(1, -1)
    widened = jnp.concatenate([tile[...] for tile in tiles], axis=0).astype(jnp.float32)
    mean_square = jnp.mean(widened * widened, axis=-1, keepdims=True)
    return (widened * lax.rsqrt(mean_square + epsilon) * gain).astype(jnp.bfloat16)


def write_pairs(normed, w_ref, offset, outs):
    pairs = dot(normed, w_ref[...]).astype(jnp.bfloat16)
    rows = pairs.shape[0]
    for head, out_ref in enumerate(outs):
        for start in range(0, rows, HD):
            there = slice(offset + start, offset + start + HD)
            out_ref[there, :HD] = pairs[start : start + HD, head_lanes(head)].T
        out_ref[offset : offset + rows, HD:] = pairs[:, head_lanes(KVH + head)]


def early_kernel(gain_ref, w_kv_ref, w_query_ref, *refs):
    tiles, query_ref, outs = refs[:EARLY], refs[EARLY], refs[EARLY + 1 :]
    normed = norm_rows(gain_ref, tiles)
    write_pairs(normed, w_kv_ref, 0, outs)
    query_ref[...] = dot(normed, w_query_ref[...]).astype(jnp.bfloat16)


def pairs_kernel(gain_ref, w_kv_ref, *refs):
    late = SB - EARLY
    tiles, done, normed_ref, outs = refs[:late], refs[late:-KVH - 1], refs[-KVH - 1], refs[-KVH:]
    normed = norm_rows(gain_ref, tiles)
    normed_ref[...] = normed
    rows = done[0].shape[0]
    for done_ref, out_ref in zip(done, outs):
        out_ref[:rows] = done_ref[...]
    write_pairs(normed, w_kv_ref, rows, outs)


def make_early(tiles, gain, w_kv, w_query):
    width, wide = w_kv.shape
    rows = sum(tile.shape[0] for tile in tiles)
    return pl.pallas_call(
        early_kernel,
        out_shape=[jax.ShapeDtypeStruct((rows, w_query.shape[1]), jnp.bfloat16)]
        + [jax.ShapeDtypeStruct((rows, wide // KVH), jnp.bfloat16)] * KVH,
        compiler_params=pltpu.CompilerParams(vmem_limit_bytes=16 * MIB),
        cost_estimate=pl.CostEstimate(
            flops=2 * rows * width * (wide + width),
            bytes_accessed=2 * (2 * rows * width + width * wide + width * width),
            transcendentals=rows,
        ),
        name="early_rows",
    )(gain, w_kv, w_query, *tiles)


def make_pairs(tiles, gain, w_kv, done):
    width, wide = w_kv.shape
    rows = sum(tile.shape[0] for tile in tiles)
    total = rows + done[0].shape[0]
    return pl.pallas_call(
        pairs_kernel,
        out_shape=[jax.ShapeDtypeStruct((rows, width), jnp.bfloat16)]
        + [jax.ShapeDtypeStruct((total, wide // KVH), jnp.bfloat16)] * KVH,
        compiler_params=pltpu.CompilerParams(vmem_limit_bytes=16 * MIB),
        cost_estimate=pl.CostEstimate(
            flops=2 * rows * width * wide,
            bytes_accessed=2 * (2 * rows * width + width * wide + rows * wide),
            transcendentals=rows,
        ),
        name="pairs",
    )(gain, w_kv, *tiles, *done)


SCORE_SCALE = math.log2(math.e) / math.sqrt(HD)
GROUP = HEADS // KVH


def key_and_value(ref):
    key = jnp.concatenate(
        [ref[start : start + HD, :HD] for start in range(0, ref.shape[0], HD)], axis=1
    )
    value = ref[:, HD:]
    return key, jnp.concatenate([value, jnp.ones_like(value)], axis=1)


def own_kernel(normed_ref, w_ref, early_ref, *refs):
    both = [key_and_value(ref) for ref in refs[:KVH]]
    query_ref, sum_ref, total_ref, top_ref = refs[KVH:]
    columns = GROUP * HD

    def project(group):
        lanes = slice(group * columns, (group + 1) * columns)
        late = dot(normed_ref[...], w_ref[:, lanes]).astype(jnp.bfloat16)
        query = jnp.concatenate([early_ref[:, lanes], late], axis=0)
        query_ref[:, lanes] = query
        return query

    queries = {0: project(0)}

    def scores_of(head):
        group = head // GROUP
        return dot(queries[group][:, head_lanes(head % GROUP)], both[group][0])

    scores = scores_of(0)
    for head in range(HEADS):
        if head % GROUP == 0 and head + GROUP < HEADS:
            queries[head // GROUP + 1] = project(head // GROUP + 1)
        upcoming = scores_of(head + 1) if head + 1 < HEADS else None
        lanes = head_lanes(head)
        largest = jnp.max(scores, axis=-1, keepdims=True)
        raised = jnp.exp2((scores - largest) * SCORE_SCALE).astype(jnp.bfloat16)
        summed = dot(raised, both[head // GROUP][1])
        sum_ref[:, lanes] = summed[:, :HD]
        total_ref[:, lanes] = summed[:, HD:]
        top_ref[:, lanes] = jnp.broadcast_to(largest * SCORE_SCALE, (scores.shape[0], HD))
        scores = upcoming


def own_frame(normed, w_query, early, pairs):
    rows, width = pairs[0].shape[0], normed.shape[1]
    return pl.pallas_call(
        own_kernel,
        out_shape=[jax.ShapeDtypeStruct((rows, width), jnp.bfloat16)]
        + [jax.ShapeDtypeStruct((rows, width), jnp.float32)] * 3,
        compiler_params=pltpu.CompilerParams(vmem_limit_bytes=32 * MIB),
        cost_estimate=pl.CostEstimate(
            flops=2 * rows * width * width + 4 * rows * rows * width,
            bytes_accessed=2 * width * width + 8 * rows * width,
            transcendentals=rows * rows * HEADS,
        ),
        name="own_frame",
    )(normed, w_query, early, *pairs)


def earlier_kernel(group, query_ref, pairs_ref, sum_ref, total_ref, top_ref, *refs):
    key, value = key_and_value(pairs_ref)
    index = lax.axis_index("tm")
    barred = jnp.where(index > 0, 0.0, -jnp.inf)
    place = lax.rem(index, SB)
    size = query_ref.shape[0] // SB
    columns = GROUP * HD
    last = group == KVH - 1
    copies = []
    if last:
        *done_refs, out_hbm, out_ref, sent = refs

        def leave(source, start):
            there = out_hbm.at[:, start : start + source.shape[1]]
            copies.append(pltpu.make_async_copy(source, there, sent.at[len(copies)]))
            copies[-1].start()

        for part, ref in enumerate(done_refs):
            leave(ref, part * columns)
    else:
        (out_ref,) = refs

    def scores_of(head):
        return dot(query_ref[:, head_lanes(group * GROUP + head)], key)

    scores = scores_of(0)
    for head in range(GROUP):
        lanes = head_lanes(group * GROUP + head)
        upcoming = scores_of(head + 1) if head + 1 < GROUP else None
        before = top_ref[:, lanes]
        here = jnp.max(scores, axis=-1, keepdims=True) * SCORE_SCALE + barred
        largest = jnp.maximum(jnp.broadcast_to(here, before.shape), before)
        below = jnp.concatenate([largest - barred] * (scores.shape[1] // HD), axis=1)
        raised = jnp.exp2(scores * SCORE_SCALE - below).astype(jnp.bfloat16)
        summed = dot(raised, value)
        share = jnp.exp2(before - largest)
        mixed = sum_ref[:, lanes] * share + summed[:, :HD]
        total = total_ref[:, lanes] * share + summed[:, HD:]
        mixed = (mixed / total).astype(jnp.bfloat16)
        for slot, apart in enumerate(APART):
            there = pl.ds(pl.multiple_of((place ^ apart) * size, size), size)
            out_ref[there, head_lanes(head)] = mixed[slot * size : (slot + 1) * size]
        if last and head % 2:
            start = (head - 1) * HD
            leave(out_ref.at[:, start : start + 2 * HD], group * columns + start)
        scores = upcoming
    for copy in copies:
        copy.wait()


def earlier_frame(group, query, pairs, so_far, done):
    rows, width = query.shape
    columns = GROUP * HD
    last = group == KVH - 1
    extra = dict(out_shape=jax.ShapeDtypeStruct((rows, columns), jnp.bfloat16))
    if last:
        extra = dict(
            out_shape=jax.ShapeDtypeStruct((rows, width), jnp.bfloat16),
            out_specs=pl.BlockSpec(memory_space=pl.ANY),
            scratch_shapes=[
                pltpu.VMEM((rows, columns), jnp.bfloat16),
                pltpu.SemaphoreType.DMA((KVH - 1 + GROUP // 2,)),
            ],
        )
    operands = [query, pairs, *so_far] + (done if last else [])
    return pl.pallas_call(
        functools.partial(earlier_kernel, group),
        compiler_params=pltpu.CompilerParams(vmem_limit_bytes=32 * MIB),
        cost_estimate=pl.CostEstimate(
            flops=4 * rows * rows * columns,
            bytes_accessed=20 * rows * columns,
            transcendentals=rows * rows * GROUP,
        ),
        name="earlier_frame",
        **extra,
    )(*operands)


def swap(tile, apart):
    devices = lax.axis_size("tm")
    route = [(i, i - i % SB + (i % SB ^ apart)) for i in range(devices)]
    return lax.ppermute(tile, "tm", route)


def body(space_time, w_lin, gain_lin, w_query, w_kv, frame_attention_gain):
    tokens = space_time[0]
    time_ranges = lax.axis_size("tm") // SB
    state = incoming_state(tokens, w_lin, time_ranges) if time_ranges > 1 else None
    tiles = mixer(tokens, w_lin, gain_lin, state)
    tiles = [swap(tile, apart) if apart else tile for apart, tile in zip(APART, tiles)]
    early, *done = make_early(tiles[:EARLY], frame_attention_gain, w_kv, w_query)
    normed, *pairs = make_pairs(tiles[EARLY:], frame_attention_gain, w_kv, done)
    earlier_pairs = [shifted(part, "tm", 1) for part in pairs]
    query, *so_far = own_frame(normed, w_query, early, pairs)
    done = []
    for group, part in enumerate(earlier_pairs):
        done.append(earlier_frame(group, query, part, so_far, done))
    return done[-1][None]


def solution(mesh):
    placed = (P(("groups", "tm"), None, None), P(), P(), P(), P(), P())
    return jax.shard_map(
        body, mesh=mesh, in_specs=placed, out_specs=P(("groups", "tm"), None, None), check_vma=False
    )
```

```python
import functools
import math

import jax
import jax.numpy as jnp
from jax import lax
from jax.experimental import pallas as pl
from jax.experimental.pallas import tpu as pltpu
from jax.sharding import PartitionSpec as P

HEADS = 8
HD = 128
KVH = 2
SB = 16
SPAN = 128
GROUPS = ((0, 4), (4, 8))
APART = (0, 5, 11, 9, 2, 12, 6, 4, 8, 14, 10, 15, 13, 3, 7, 1)
EARLY = SB - 4

epsilon = 1e-06
MIB = 1 << 20


def shifted(block, axis, distance):
    devices = range(lax.axis_size(axis))
    route = [(i - distance, i) for i in devices if i - distance in devices]
    return lax.ppermute(block, axis, route)


def dot(a, b):
    return jnp.dot(a, b, preferred_element_type=jnp.float32)


def dot_nt(a, b):
    return lax.dot_general(a, b, (((1,), (1,)), ((), ())), preferred_element_type=jnp.float32)


def dot_tn(a, b):
    return lax.dot_general(a, b, (((0,), (0,)), ((), ())), preferred_element_type=jnp.float32)


def head_lanes(head):
    return slice(head * HD, (head + 1) * HD)


def causal_mask():
    shape = (SPAN, SPAN)
    return lax.broadcasted_iota(jnp.int32, shape, 0) >= lax.broadcasted_iota(jnp.int32, shape, 1)


def mix_heads(query, key, value, states):
    rows = query.shape[0]
    causal = causal_mask()
    spans = [slice(start, start + SPAN) for start in range(0, rows, SPAN)]
    heads = range(query.shape[1] // HD)
    units = [(head, span) for head in heads for span in range(len(spans))]
    local, before, mixed = {}, {}, []
    for head, span in units:
        lanes, here = head_lanes(head), spans[span]
        scores = dot_nt(query[here, lanes], key[here, lanes])
        local[head, span] = jnp.where(causal, scores, 0.0).astype(jnp.bfloat16)
    for head in heads:
        lanes = head_lanes(head)
        state = states[head]
        for span, here in enumerate(spans):
            before[head, span] = state
            if span + 1 < len(spans):
                update = dot_tn(key[here, lanes], value[here, lanes])
                state = update if state is None else state + update
    for head, span in units:
        lanes, here = head_lanes(head), spans[span]
        if before[head, span] is None:
            out = dot(local[head, span], value[here, lanes])
        else:
            out = dot(
                jnp.concatenate([query[here, lanes], local[head, span]], axis=1),
                jnp.concatenate(
                    [before[head, span].astype(jnp.bfloat16), value[here, lanes]], axis=0
                ),
            )
        mixed.append((head, here, out))
    return mixed


def mixer_kernel(has_state, *refs):
    if has_state:
        state_ref, *refs = refs
    tokens_hbm, w_hbm, gain_ref, *refs = refs
    tiles, (tokens_ref, out_ref, *weights, tokens_in, weights_in, sent) = refs[:SB], refs[SB:]
    rows, width = tokens_ref.shape
    size = rows // SB
    place = lax.rem(lax.axis_index("tm"), SB)

    first = [pltpu.make_async_copy(tokens_hbm, tokens_ref, tokens_in)]
    copies = []
    for index, (low, high) in enumerate(GROUPS):
        here = []
        for part in range(3):
            columns = slice(part * width + low * HD, part * width + high * HD)
            here.append(
                pltpu.make_async_copy(
                    w_hbm.at[:, columns], weights[index].at[part], weights_in.at[index, part]
                )
            )
        copies.append(here)
    for copy in first + sum(copies, []):
        copy.start()
    gains = gain_ref[...].astype(jnp.float32).reshape(1, width)

    leaving = []

    def project(index):
        for copy in copies[index]:
            copy.wait()
        tokens = tokens_ref[...]
        return [dot(tokens, weights[index][part]).astype(jnp.bfloat16) for part in range(3)]

    def mix(index, parts):
        low, high = GROUPS[index]
        states = [state_ref[head] if has_state else None for head in range(low, high)]
        for head, here, out in mix_heads(*parts, states):
            lanes = head_lanes(low + head)
            mean_square = jnp.mean(out * out, axis=-1, keepdims=True)
            normed = out * lax.rsqrt(mean_square + epsilon) * gains[:, lanes]
            residual = tokens_ref[here, lanes].astype(jnp.float32)
            out_ref[here, lanes] = (residual + normed).astype(jnp.bfloat16)
        lanes = slice(low * HD, high * HD)
        for slot, (apart, tile) in enumerate(zip(APART, tiles)):
            here = pl.ds(pl.multiple_of((place ^ apart) * size, size), size)
            copy = pltpu.make_async_copy(
                out_ref.at[here, lanes], tile.at[:, lanes], sent.at[index, slot]
            )
            copy.start()
            leaving.append(copy)

    first[0].wait()
    parts = project(0)
    for index in range(len(GROUPS)):
        upcoming = project(index + 1) if index + 1 < len(GROUPS) else None
        mix(index, parts)
        parts = upcoming
    for copy in leaving:
        copy.wait()


def mixer(tokens, w_lin, gain_lin, state):
    rows, width = tokens.shape
    hbm = pl.BlockSpec(memory_space=pl.ANY)
    vmem = pl.BlockSpec(memory_space=pltpu.VMEM)
    in_specs = [hbm, hbm, vmem]
    operands = [tokens, w_lin, gain_lin]
    if state is not None:
        operands.insert(0, state)
        in_specs.insert(0, vmem)
    return pl.pallas_call(
        functools.partial(mixer_kernel, state is not None),
        in_specs=in_specs,
        out_specs=[hbm] * SB,
        out_shape=[jax.ShapeDtypeStruct((rows // SB, width), jnp.bfloat16)] * SB,
        scratch_shapes=[pltpu.VMEM((rows, width), jnp.bfloat16)] * 2
        + [pltpu.VMEM((3, width, (high - low) * HD), jnp.bfloat16) for low, high in GROUPS]
        + [
            pltpu.SemaphoreType.DMA,
            pltpu.SemaphoreType.DMA((len(GROUPS), 3)),
            pltpu.SemaphoreType.DMA((len(GROUPS), SB)),
        ],
        compiler_params=pltpu.CompilerParams(vmem_limit_bytes=60 * MIB),
        cost_estimate=pl.CostEstimate(
            flops=2 * rows * width * 3 * width + 8 * rows * SPAN * width,
            bytes_accessed=2 * (3 * width * width + 2 * rows * width),
            transcendentals=rows * HEADS,
        ),
        name="mixer",
    )(*operands)


def incoming_state(tokens, w_lin, time_ranges):
    rows, width = tokens.shape
    packed = dot(tokens, w_lin[:, width:]).astype(jnp.bfloat16).reshape(rows, 2, HEADS, HD)
    block_total = jnp.einsum(
        "nhd,nhe->hde", packed[:, 0], packed[:, 1], preferred_element_type=jnp.float32
    )
    within = lax.axis_index("tm") // SB

    def advance_hop(turn_index, running_total):
        moved = shifted(running_total + block_total, "tm", SB)
        return jnp.where(within > 0, moved, 0.0)

    return lax.fori_loop(0, time_ranges - 1, advance_hop, jnp.zeros_like(block_total))


def norm_rows(gain_ref, tiles):
    gain = gain_ref[...].astype(jnp.float32).reshape(1, -1)
    widened = jnp.concatenate([tile[...] for tile in tiles], axis=0).astype(jnp.float32)
    mean_square = jnp.mean(widened * widened, axis=-1, keepdims=True)
    return (widened * lax.rsqrt(mean_square + epsilon) * gain).astype(jnp.bfloat16)


def write_pairs(normed, w_ref, offset, outs):
    pairs = dot(normed, w_ref[...]).astype(jnp.bfloat16)
    rows = pairs.shape[0]
    for head, out_ref in enumerate(outs):
        for start in range(0, rows, HD):
            there = slice(offset + start, offset + start + HD)
            out_ref[there, :HD] = pairs[start : start + HD, head_lanes(head)].T
        out_ref[offset : offset + rows, HD:] = pairs[:, head_lanes(KVH + head)]


def early_kernel(gain_ref, w_kv_ref, w_query_ref, *refs):
    tiles, query_ref, outs = refs[:EARLY], refs[EARLY], refs[EARLY + 1 :]
    normed = norm_rows(gain_ref, tiles)
    write_pairs(normed, w_kv_ref, 0, outs)
    query_ref[...] = dot(normed, w_query_ref[...]).astype(jnp.bfloat16)


def pairs_kernel(gain_ref, w_kv_ref, *refs):
    late = SB - EARLY
    tiles, done, normed_ref, outs = refs[:late], refs[late:-KVH - 1], refs[-KVH - 1], refs[-KVH:]
    normed = norm_rows(gain_ref, tiles)
    normed_ref[...] = normed
    rows = done[0].shape[0]
    for done_ref, out_ref in zip(done, outs):
        out_ref[:rows] = done_ref[...]
    write_pairs(normed, w_kv_ref, rows, outs)


def make_early(tiles, gain, w_kv, w_query):
    width, wide = w_kv.shape
    rows = sum(tile.shape[0] for tile in tiles)
    return pl.pallas_call(
        early_kernel,
        out_shape=[jax.ShapeDtypeStruct((rows, w_query.shape[1]), jnp.bfloat16)]
        + [jax.ShapeDtypeStruct((rows, wide // KVH), jnp.bfloat16)] * KVH,
        compiler_params=pltpu.CompilerParams(vmem_limit_bytes=16 * MIB),
        cost_estimate=pl.CostEstimate(
            flops=2 * rows * width * (wide + width),
            bytes_accessed=2 * (2 * rows * width + width * wide + width * width),
            transcendentals=rows,
        ),
        name="early_rows",
    )(gain, w_kv, w_query, *tiles)


def make_pairs(tiles, gain, w_kv, done):
    width, wide = w_kv.shape
    rows = sum(tile.shape[0] for tile in tiles)
    total = rows + done[0].shape[0]
    return pl.pallas_call(
        pairs_kernel,
        out_shape=[jax.ShapeDtypeStruct((rows, width), jnp.bfloat16)]
        + [jax.ShapeDtypeStruct((total, wide // KVH), jnp.bfloat16)] * KVH,
        compiler_params=pltpu.CompilerParams(vmem_limit_bytes=16 * MIB),
        cost_estimate=pl.CostEstimate(
            flops=2 * rows * width * wide,
            bytes_accessed=2 * (2 * rows * width + width * wide + rows * wide),
            transcendentals=rows,
        ),
        name="pairs",
    )(gain, w_kv, *tiles, *done)


SCORE_SCALE = math.log2(math.e) / math.sqrt(HD)
GROUP = HEADS // KVH


def key_and_value(ref):
    key = jnp.concatenate(
        [ref[start : start + HD, :HD] for start in range(0, ref.shape[0], HD)], axis=1
    )
    value = ref[:, HD:]
    return key, jnp.concatenate([value, jnp.ones_like(value)], axis=1)


def own_kernel(normed_ref, w_ref, early_ref, *refs):
    both = [key_and_value(ref) for ref in refs[:KVH]]
    query_ref, sum_ref, total_ref, top_ref = refs[KVH:]
    columns = GROUP * HD

    def project(group):
        lanes = slice(group * columns, (group + 1) * columns)
        late = dot(normed_ref[...], w_ref[:, lanes]).astype(jnp.bfloat16)
        query = jnp.concatenate([early_ref[:, lanes], late], axis=0)
        query_ref[:, lanes] = query
        return query

    queries = {0: project(0)}

    def scores_of(head):
        group = head // GROUP
        return dot(queries[group][:, head_lanes(head % GROUP)], both[group][0])

    scores = scores_of(0)
    for head in range(HEADS):
        if head % GROUP == 0 and head + GROUP < HEADS:
            queries[head // GROUP + 1] = project(head // GROUP + 1)
        upcoming = scores_of(head + 1) if head + 1 < HEADS else None
        lanes = head_lanes(head)
        largest = jnp.max(scores, axis=-1, keepdims=True)
        raised = jnp.exp2((scores - largest) * SCORE_SCALE).astype(jnp.bfloat16)
        summed = dot(raised, both[head // GROUP][1])
        sum_ref[:, lanes] = summed[:, :HD]
        total_ref[:, lanes] = summed[:, HD:]
        top_ref[:, lanes] = jnp.broadcast_to(largest * SCORE_SCALE, (scores.shape[0], HD))
        scores = upcoming


def own_frame(normed, w_query, early, pairs):
    rows, width = pairs[0].shape[0], normed.shape[1]
    return pl.pallas_call(
        own_kernel,
        out_shape=[jax.ShapeDtypeStruct((rows, width), jnp.bfloat16)]
        + [jax.ShapeDtypeStruct((rows, width), jnp.float32)] * 3,
        compiler_params=pltpu.CompilerParams(vmem_limit_bytes=32 * MIB),
        cost_estimate=pl.CostEstimate(
            flops=2 * rows * width * width + 4 * rows * rows * width,
            bytes_accessed=2 * width * width + 8 * rows * width,
            transcendentals=rows * rows * HEADS,
        ),
        name="own_frame",
    )(normed, w_query, early, *pairs)


def earlier_kernel(group, query_ref, pairs_ref, sum_ref, total_ref, top_ref, *refs):
    key, value = key_and_value(pairs_ref)
    index = lax.axis_index("tm")
    barred = jnp.where(index > 0, 0.0, -jnp.inf)
    place = lax.rem(index, SB)
    size = query_ref.shape[0] // SB
    columns = GROUP * HD
    last = group == KVH - 1
    copies = []
    if last:
        *done_refs, out_hbm, out_ref, sent = refs

        def leave(source, start):
            there = out_hbm.at[:, start : start + source.shape[1]]
            copies.append(pltpu.make_async_copy(source, there, sent.at[len(copies)]))
            copies[-1].start()

        for part, ref in enumerate(done_refs):
            leave(ref, part * columns)
    else:
        (out_ref,) = refs

    def scores_of(head):
        return dot(query_ref[:, head_lanes(group * GROUP + head)], key)

    scores = scores_of(0)
    for head in range(GROUP):
        lanes = head_lanes(group * GROUP + head)
        upcoming = scores_of(head + 1) if head + 1 < GROUP else None
        before = top_ref[:, lanes]
        here = jnp.max(scores, axis=-1, keepdims=True) * SCORE_SCALE + barred
        largest = jnp.maximum(jnp.broadcast_to(here, before.shape), before)
        below = jnp.concatenate([largest - barred] * (scores.shape[1] // HD), axis=1)
        raised = jnp.exp2(scores * SCORE_SCALE - below).astype(jnp.bfloat16)
        summed = dot(raised, value)
        share = jnp.exp2(before - largest)
        mixed = sum_ref[:, lanes] * share + summed[:, :HD]
        total = total_ref[:, lanes] * share + summed[:, HD:]
        mixed = (mixed / total).astype(jnp.bfloat16)
        for slot, apart in enumerate(APART):
            there = pl.ds(pl.multiple_of((place ^ apart) * size, size), size)
            out_ref[there, head_lanes(head)] = mixed[slot * size : (slot + 1) * size]
        if last and head % 2:
            start = (head - 1) * HD
            leave(out_ref.at[:, start : start + 2 * HD], group * columns + start)
        scores = upcoming
    for copy in copies:
        copy.wait()


def earlier_frame(group, query, pairs, so_far, done):
    rows, width = query.shape
    columns = GROUP * HD
    last = group == KVH - 1
    extra = dict(out_shape=jax.ShapeDtypeStruct((rows, columns), jnp.bfloat16))
    if last:
        extra = dict(
            out_shape=jax.ShapeDtypeStruct((rows, width), jnp.bfloat16),
            out_specs=pl.BlockSpec(memory_space=pl.ANY),
            scratch_shapes=[
                pltpu.VMEM((rows, columns), jnp.bfloat16),
                pltpu.SemaphoreType.DMA((KVH - 1 + GROUP // 2,)),
            ],
        )
    operands = [query, pairs, *so_far] + (done if last else [])
    return pl.pallas_call(
        functools.partial(earlier_kernel, group),
        compiler_params=pltpu.CompilerParams(vmem_limit_bytes=32 * MIB),
        cost_estimate=pl.CostEstimate(
            flops=4 * rows * rows * columns,
            bytes_accessed=20 * rows * columns,
            transcendentals=rows * rows * GROUP,
        ),
        name="earlier_frame",
        **extra,
    )(*operands)


def swap(tile, apart):
    devices = lax.axis_size("tm")
    route = [(i, i - i % SB + (i % SB ^ apart)) for i in range(devices)]
    return lax.ppermute(tile, "tm", route)


def body(space_time, w_lin, gain_lin, w_query, w_kv, frame_attention_gain):
    tokens = space_time[0]
    time_ranges = lax.axis_size("tm") // SB
    state = incoming_state(tokens, w_lin, time_ranges) if time_ranges > 1 else None
    tiles = mixer(tokens, w_lin, gain_lin, state)
    tiles = [swap(tile, apart) if apart else tile for apart, tile in zip(APART, tiles)]
    early, *done = make_early(tiles[:EARLY], frame_attention_gain, w_kv, w_query)
    normed, *pairs = make_pairs(tiles[EARLY:], frame_attention_gain, w_kv, done)
    earlier_pairs = [shifted(part, "tm", 1) for part in pairs]
    query, *so_far = own_frame(normed, w_query, early, pairs)
    done = []
    for group, part in enumerate(earlier_pairs):
        done.append(earlier_frame(group, query, part, so_far, done))
    return done[-1][None]


def solution(mesh):
    placed = (P(("groups", "tm"), None, None), P(), P(), P(), P(), P())
    return jax.shard_map(
        body, mesh=mesh, in_specs=placed, out_specs=P(("groups", "tm"), None, None), check_vma=False
    )
```

```python
import functools
import math

import jax
import jax.numpy as jnp
from jax import lax
from jax.experimental import pallas as pl
from jax.experimental.pallas import tpu as pltpu
from jax.sharding import PartitionSpec as P

HEADS = 8
HD = 128
KVH = 2
SB = 16
SPAN = 128
GROUPS = ((0, 4), (4, 8))
APART = (0, 5, 11, 9, 2, 12, 6, 8, 14, 4, 10, 15, 13, 3, 7, 1)
EARLY = SB - 4

epsilon = 1e-06
MIB = 1 << 20


def shifted(block, axis, distance):
    devices = range(lax.axis_size(axis))
    route = [(i - distance, i) for i in devices if i - distance in devices]
    return lax.ppermute(block, axis, route)


def dot(a, b):
    return jnp.dot(a, b, preferred_element_type=jnp.float32)


def dot_nt(a, b):
    return lax.dot_general(a, b, (((1,), (1,)), ((), ())), preferred_element_type=jnp.float32)


def dot_tn(a, b):
    return lax.dot_general(a, b, (((0,), (0,)), ((), ())), preferred_element_type=jnp.float32)


def head_lanes(head):
    return slice(head * HD, (head + 1) * HD)


def causal_mask():
    shape = (SPAN, SPAN)
    return lax.broadcasted_iota(jnp.int32, shape, 0) >= lax.broadcasted_iota(jnp.int32, shape, 1)


def mix_heads(query, key, value, states):
    rows = query.shape[0]
    causal = causal_mask()
    spans = [slice(start, start + SPAN) for start in range(0, rows, SPAN)]
    heads = range(query.shape[1] // HD)
    units = [(head, span) for head in heads for span in range(len(spans))]
    local, before, mixed = {}, {}, []
    for head, span in units:
        lanes, here = head_lanes(head), spans[span]
        scores = dot_nt(query[here, lanes], key[here, lanes])
        local[head, span] = jnp.where(causal, scores, 0.0).astype(jnp.bfloat16)
    for head in heads:
        lanes = head_lanes(head)
        state = states[head]
        for span, here in enumerate(spans):
            before[head, span] = state
            if span + 1 < len(spans):
                update = dot_tn(key[here, lanes], value[here, lanes])
                state = update if state is None else state + update
    for head, span in units:
        lanes, here = head_lanes(head), spans[span]
        if before[head, span] is None:
            out = dot(local[head, span], value[here, lanes])
        else:
            out = dot(
                jnp.concatenate([query[here, lanes], local[head, span]], axis=1),
                jnp.concatenate(
                    [before[head, span].astype(jnp.bfloat16), value[here, lanes]], axis=0
                ),
            )
        mixed.append((head, here, out))
    return mixed


def mixer_kernel(has_state, *refs):
    if has_state:
        state_ref, *refs = refs
    tokens_hbm, w_hbm, gain_ref, *refs = refs
    tiles, (tokens_ref, out_ref, *weights, tokens_in, weights_in, sent) = refs[:SB], refs[SB:]
    rows, width = tokens_ref.shape
    size = rows // SB
    place = lax.rem(lax.axis_index("tm"), SB)

    first = [pltpu.make_async_copy(tokens_hbm, tokens_ref, tokens_in)]
    copies = []
    for index, (low, high) in enumerate(GROUPS):
        here = []
        for part in range(3):
            columns = slice(part * width + low * HD, part * width + high * HD)
            here.append(
                pltpu.make_async_copy(
                    w_hbm.at[:, columns], weights[index].at[part], weights_in.at[index, part]
                )
            )
        copies.append(here)
    for copy in first + sum(copies, []):
        copy.start()
    gains = gain_ref[...].astype(jnp.float32).reshape(1, width)

    leaving = []

    def project(index):
        for copy in copies[index]:
            copy.wait()
        tokens = tokens_ref[...]
        return [dot(tokens, weights[index][part]).astype(jnp.bfloat16) for part in range(3)]

    def mix(index, parts):
        low, high = GROUPS[index]
        states = [state_ref[head] if has_state else None for head in range(low, high)]
        for head, here, out in mix_heads(*parts, states):
            lanes = head_lanes(low + head)
            mean_square = jnp.mean(out * out, axis=-1, keepdims=True)
            normed = out * lax.rsqrt(mean_square + epsilon) * gains[:, lanes]
            residual = tokens_ref[here, lanes].astype(jnp.float32)
            out_ref[here, lanes] = (residual + normed).astype(jnp.bfloat16)
        lanes = slice(low * HD, high * HD)
        for slot, (apart, tile) in enumerate(zip(APART, tiles)):
            here = pl.ds(pl.multiple_of((place ^ apart) * size, size), size)
            copy = pltpu.make_async_copy(
                out_ref.at[here, lanes], tile.at[:, lanes], sent.at[index, slot]
            )
            copy.start()
            leaving.append(copy)

    first[0].wait()
    parts = project(0)
    for index in range(len(GROUPS)):
        upcoming = project(index + 1) if index + 1 < len(GROUPS) else None
        mix(index, parts)
        parts = upcoming
    for copy in leaving:
        copy.wait()


def mixer(tokens, w_lin, gain_lin, state):
    rows, width = tokens.shape
    hbm = pl.BlockSpec(memory_space=pl.ANY)
    vmem = pl.BlockSpec(memory_space=pltpu.VMEM)
    in_specs = [hbm, hbm, vmem]
    operands = [tokens, w_lin, gain_lin]
    if state is not None:
        operands.insert(0, state)
        in_specs.insert(0, vmem)
    return pl.pallas_call(
        functools.partial(mixer_kernel, state is not None),
        in_specs=in_specs,
        out_specs=[hbm] * SB,
        out_shape=[jax.ShapeDtypeStruct((rows // SB, width), jnp.bfloat16)] * SB,
        scratch_shapes=[pltpu.VMEM((rows, width), jnp.bfloat16)] * 2
        + [pltpu.VMEM((3, width, (high - low) * HD), jnp.bfloat16) for low, high in GROUPS]
        + [
            pltpu.SemaphoreType.DMA,
            pltpu.SemaphoreType.DMA((len(GROUPS), 3)),
            pltpu.SemaphoreType.DMA((len(GROUPS), SB)),
        ],
        compiler_params=pltpu.CompilerParams(vmem_limit_bytes=60 * MIB),
        cost_estimate=pl.CostEstimate(
            flops=2 * rows * width * 3 * width + 8 * rows * SPAN * width,
            bytes_accessed=2 * (3 * width * width + 2 * rows * width),
            transcendentals=rows * HEADS,
        ),
        name="mixer",
    )(*operands)


def incoming_state(tokens, w_lin, time_ranges):
    rows, width = tokens.shape
    packed = dot(tokens, w_lin[:, width:]).astype(jnp.bfloat16).reshape(rows, 2, HEADS, HD)
    block_total = jnp.einsum(
        "nhd,nhe->hde", packed[:, 0], packed[:, 1], preferred_element_type=jnp.float32
    )
    within = lax.axis_index("tm") // SB

    def advance_hop(turn_index, running_total):
        moved = shifted(running_total + block_total, "tm", SB)
        return jnp.where(within > 0, moved, 0.0)

    return lax.fori_loop(0, time_ranges - 1, advance_hop, jnp.zeros_like(block_total))


def norm_rows(gain_ref, tiles):
    gain = gain_ref[...].astype(jnp.float32).reshape(1, -1)
    widened = jnp.concatenate([tile[...] for tile in tiles], axis=0).astype(jnp.float32)
    mean_square = jnp.mean(widened * widened, axis=-1, keepdims=True)
    return (widened * lax.rsqrt(mean_square + epsilon) * gain).astype(jnp.bfloat16)


def write_pairs(normed, w_ref, offset, outs):
    pairs = dot(normed, w_ref[...]).astype(jnp.bfloat16)
    rows = pairs.shape[0]
    for head, out_ref in enumerate(outs):
        for start in range(0, rows, HD):
            there = slice(offset + start, offset + start + HD)
            out_ref[there, :HD] = pairs[start : start + HD, head_lanes(head)].T
        out_ref[offset : offset + rows, HD:] = pairs[:, head_lanes(KVH + head)]


def early_kernel(gain_ref, w_kv_ref, w_query_ref, *refs):
    tiles, query_ref, outs = refs[:EARLY], refs[EARLY], refs[EARLY + 1 :]
    normed = norm_rows(gain_ref, tiles)
    write_pairs(normed, w_kv_ref, 0, outs)
    query_ref[...] = dot(normed, w_query_ref[...]).astype(jnp.bfloat16)


def pairs_kernel(gain_ref, w_kv_ref, *refs):
    late = SB - EARLY
    tiles, done, normed_ref, outs = refs[:late], refs[late:-KVH - 1], refs[-KVH - 1], refs[-KVH:]
    normed = norm_rows(gain_ref, tiles)
    normed_ref[...] = normed
    rows = done[0].shape[0]
    for done_ref, out_ref in zip(done, outs):
        out_ref[:rows] = done_ref[...]
    write_pairs(normed, w_kv_ref, rows, outs)


def make_early(tiles, gain, w_kv, w_query):
    width, wide = w_kv.shape
    rows = sum(tile.shape[0] for tile in tiles)
    return pl.pallas_call(
        early_kernel,
        out_shape=[jax.ShapeDtypeStruct((rows, w_query.shape[1]), jnp.bfloat16)]
        + [jax.ShapeDtypeStruct((rows, wide // KVH), jnp.bfloat16)] * KVH,
        compiler_params=pltpu.CompilerParams(vmem_limit_bytes=16 * MIB),
        cost_estimate=pl.CostEstimate(
            flops=2 * rows * width * (wide + width),
            bytes_accessed=2 * (2 * rows * width + width * wide + width * width),
            transcendentals=rows,
        ),
        name="early_rows",
    )(gain, w_kv, w_query, *tiles)


def make_pairs(tiles, gain, w_kv, done):
    width, wide = w_kv.shape
    rows = sum(tile.shape[0] for tile in tiles)
    total = rows + done[0].shape[0]
    return pl.pallas_call(
        pairs_kernel,
        out_shape=[jax.ShapeDtypeStruct((rows, width), jnp.bfloat16)]
        + [jax.ShapeDtypeStruct((total, wide // KVH), jnp.bfloat16)] * KVH,
        compiler_params=pltpu.CompilerParams(vmem_limit_bytes=16 * MIB),
        cost_estimate=pl.CostEstimate(
            flops=2 * rows * width * wide,
            bytes_accessed=2 * (2 * rows * width + width * wide + rows * wide),
            transcendentals=rows,
        ),
        name="pairs",
    )(gain, w_kv, *tiles, *done)


SCORE_SCALE = math.log2(math.e) / math.sqrt(HD)
GROUP = HEADS // KVH


def key_and_value(ref):
    key = jnp.concatenate(
        [ref[start : start + HD, :HD] for start in range(0, ref.shape[0], HD)], axis=1
    )
    value = ref[:, HD:]
    return key, jnp.concatenate([value, jnp.ones_like(value)], axis=1)


def own_kernel(normed_ref, w_ref, early_ref, *refs):
    both = [key_and_value(ref) for ref in refs[:KVH]]
    query_ref, sum_ref, total_ref, top_ref = refs[KVH:]
    columns = GROUP * HD

    def project(group):
        lanes = slice(group * columns, (group + 1) * columns)
        late = dot(normed_ref[...], w_ref[:, lanes]).astype(jnp.bfloat16)
        query = jnp.concatenate([early_ref[:, lanes], late], axis=0)
        query_ref[:, lanes] = query
        return query

    queries = {0: project(0)}

    def scores_of(head):
        group = head // GROUP
        return dot(queries[group][:, head_lanes(head % GROUP)], both[group][0])

    scores = scores_of(0)
    for head in range(HEADS):
        if head % GROUP == 0 and head + GROUP < HEADS:
            queries[head // GROUP + 1] = project(head // GROUP + 1)
        upcoming = scores_of(head + 1) if head + 1 < HEADS else None
        lanes = head_lanes(head)
        largest = jnp.max(scores, axis=-1, keepdims=True)
        raised = jnp.exp2((scores - largest) * SCORE_SCALE).astype(jnp.bfloat16)
        summed = dot(raised, both[head // GROUP][1])
        sum_ref[:, lanes] = summed[:, :HD]
        total_ref[:, lanes] = summed[:, HD:]
        top_ref[:, lanes] = jnp.broadcast_to(largest * SCORE_SCALE, (scores.shape[0], HD))
        scores = upcoming


def own_frame(normed, w_query, early, pairs):
    rows, width = pairs[0].shape[0], normed.shape[1]
    return pl.pallas_call(
        own_kernel,
        out_shape=[jax.ShapeDtypeStruct((rows, width), jnp.bfloat16)]
        + [jax.ShapeDtypeStruct((rows, width), jnp.float32)] * 3,
        compiler_params=pltpu.CompilerParams(vmem_limit_bytes=32 * MIB),
        cost_estimate=pl.CostEstimate(
            flops=2 * rows * width * width + 4 * rows * rows * width,
            bytes_accessed=2 * width * width + 8 * rows * width,
            transcendentals=rows * rows * HEADS,
        ),
        name="own_frame",
    )(normed, w_query, early, *pairs)


def earlier_kernel(group, query_ref, pairs_ref, sum_ref, total_ref, top_ref, *refs):
    key, value = key_and_value(pairs_ref)
    index = lax.axis_index("tm")
    barred = jnp.where(index > 0, 0.0, -jnp.inf)
    place = lax.rem(index, SB)
    size = query_ref.shape[0] // SB
    columns = GROUP * HD
    last = group == KVH - 1
    copies = []
    if last:
        *done_refs, out_hbm, out_ref, sent = refs

        def leave(source, start):
            there = out_hbm.at[:, start : start + source.shape[1]]
            copies.append(pltpu.make_async_copy(source, there, sent.at[len(copies)]))
            copies[-1].start()

        for part, ref in enumerate(done_refs):
            leave(ref, part * columns)
    else:
        (out_ref,) = refs

    def scores_of(head):
        return dot(query_ref[:, head_lanes(group * GROUP + head)], key)

    scores = scores_of(0)
    for head in range(GROUP):
        lanes = head_lanes(group * GROUP + head)
        upcoming = scores_of(head + 1) if head + 1 < GROUP else None
        before = top_ref[:, lanes]
        here = jnp.max(scores, axis=-1, keepdims=True) * SCORE_SCALE + barred
        largest = jnp.maximum(jnp.broadcast_to(here, before.shape), before)
        below = jnp.concatenate([largest - barred] * (scores.shape[1] // HD), axis=1)
        raised = jnp.exp2(scores * SCORE_SCALE - below).astype(jnp.bfloat16)
        summed = dot(raised, value)
        share = jnp.exp2(before - largest)
        mixed = sum_ref[:, lanes] * share + summed[:, :HD]
        total = total_ref[:, lanes] * share + summed[:, HD:]
        mixed = (mixed / total).astype(jnp.bfloat16)
        for slot, apart in enumerate(APART):
            there = pl.ds(pl.multiple_of((place ^ apart) * size, size), size)
            out_ref[there, head_lanes(head)] = mixed[slot * size : (slot + 1) * size]
        if last and head % 2:
            start = (head - 1) * HD
            leave(out_ref.at[:, start : start + 2 * HD], group * columns + start)
        scores = upcoming
    for copy in copies:
        copy.wait()


def earlier_frame(group, query, pairs, so_far, done):
    rows, width = query.shape
    columns = GROUP * HD
    last = group == KVH - 1
    extra = dict(out_shape=jax.ShapeDtypeStruct((rows, columns), jnp.bfloat16))
    if last:
        extra = dict(
            out_shape=jax.ShapeDtypeStruct((rows, width), jnp.bfloat16),
            out_specs=pl.BlockSpec(memory_space=pl.ANY),
            scratch_shapes=[
                pltpu.VMEM((rows, columns), jnp.bfloat16),
                pltpu.SemaphoreType.DMA((KVH - 1 + GROUP // 2,)),
            ],
        )
    operands = [query, pairs, *so_far] + (done if last else [])
    return pl.pallas_call(
        functools.partial(earlier_kernel, group),
        compiler_params=pltpu.CompilerParams(vmem_limit_bytes=32 * MIB),
        cost_estimate=pl.CostEstimate(
            flops=4 * rows * rows * columns,
            bytes_accessed=20 * rows * columns,
            transcendentals=rows * rows * GROUP,
        ),
        name="earlier_frame",
        **extra,
    )(*operands)


def swap(tile, apart):
    devices = lax.axis_size("tm")
    route = [(i, i - i % SB + (i % SB ^ apart)) for i in range(devices)]
    return lax.ppermute(tile, "tm", route)


def body(space_time, w_lin, gain_lin, w_query, w_kv, frame_attention_gain):
    tokens = space_time[0]
    time_ranges = lax.axis_size("tm") // SB
    state = incoming_state(tokens, w_lin, time_ranges) if time_ranges > 1 else None
    tiles = mixer(tokens, w_lin, gain_lin, state)
    tiles = [swap(tile, apart) if apart else tile for apart, tile in zip(APART, tiles)]
    early, *done = make_early(tiles[:EARLY], frame_attention_gain, w_kv, w_query)
    normed, *pairs = make_pairs(tiles[EARLY:], frame_attention_gain, w_kv, done)
    earlier_pairs = [shifted(part, "tm", 1) for part in pairs]
    query, *so_far = own_frame(normed, w_query, early, pairs)
    done = []
    for group, part in enumerate(earlier_pairs):
        done.append(earlier_frame(group, query, part, so_far, done))
    return done[-1][None]


def solution(mesh):
    placed = (P(("groups", "tm"), None, None), P(), P(), P(), P(), P())
    return jax.shard_map(
        body, mesh=mesh, in_specs=placed, out_specs=P(("groups", "tm"), None, None), check_vma=False
    )
```
